32 devices in a mesh: rep: 8 (over z, x), fsdp: 4 (over y, core).
Axes of the slice: x: 2, y: 2, z: 4, core: 2. Of those that a mesh axis runs over, the one named last changes fastest.
Arguments:
- block_input: bfloat16 [4096, 2048], P(('rep', 'fsdp')), may hold values from -6 to 6
- positions: int32 [4096], P(('rep', 'fsdp')), may hold values from 0 to 511, as said below
- cotangent: bfloat16 [4096, 2048], P(('rep', 'fsdp')), may hold values from -6 to 6
- norm_attn: bfloat16 [2048], P(('rep', 'fsdp')), may hold values from 0.5 to 1.5
- w_qkv: bfloat16 [2048, 4096], P(('rep', 'fsdp')), may hold values from -0.125 to 0.125
- w_out: bfloat16 [2048, 2048], P(('rep', 'fsdp')), may hold values from -2 to 2
- norm_ffn: bfloat16 [2048], P(('rep', 'fsdp')), may hold values from 0.5 to 1.5
- w_gate: bfloat16 [2048, 8192], P(('rep', 'fsdp')), may hold values from -0.125 to 0.125
- w_up: bfloat16 [2048, 8192], P(('rep', 'fsdp')), may hold values from -0.125 to 0.125
- w_down: bfloat16 [2048, 8192], P(('rep', 'fsdp')), may hold values from -0.0625 to 0.0625
Outputs:
- layer_output: bfloat16 [4096, 2048], P(('rep', 'fsdp'))
- input_gradient: float32 [4096, 2048], P(('rep', 'fsdp'))
- grad_norm_attn: float32 [2048], P(('rep', 'fsdp'))
- grad_qkv: float32 [2048, 4096], P(('rep', 'fsdp'))
- grad_out: float32 [2048, 2048], P(('rep', 'fsdp'))
- grad_norm_ffn: float32 [2048], P(('rep', 'fsdp'))
- grad_gate: float32 [2048, 8192], P(('rep', 'fsdp'))
- grad_up: float32 [2048, 8192], P(('rep', 'fsdp'))
- grad_down: float32 [2048, 8192], P(('rep', 'fsdp'))
The draws below stay inside these ranges and needn't reach their ends.
Inputs may be any that keep to these rules, and one draw needn't show every extreme that they name: Each aligned group of 512 tokens holds up to three documents; positions start at 0 at each document's first token and rise by one; the group's first token starts a document; the middle document starts within the group's first 64 tokens and ends within its last 64.
All inputs are finite; a program needn't handle non-finite values.
Results may differ from the reference program's by a relative error of at most 0.02.
Values may be sent and summed in bfloat16 or wider, within the bound.
A program may use at most 576 MiB of HBM per device.

```python
import math
import jax
import jax.numpy as jnp
from jax import lax

D = 2048
HEADS = 16
KV_HEADS = 8
HEAD_DIM = 128
FF = 8192
TOK_DEV = 128
BLOCK = 256
QKV = 4096
SEQ_LEN = 512
TOKENS = 4096


def draw_positions(key, part):
    key = jax.random.fold_in(key, 11)
    group_count = TOKENS // SEQ_LEN
    key_head, key_tail = jax.random.split(key)
    head_cut = jax.random.randint(key_head, (group_count, 1), 0, TOK_DEV // 2)
    tail_cut = jax.random.randint(key_tail, (group_count, 1), 0, TOK_DEV // 2)
    first_group = (jnp.arange(group_count) == 0)[:, None]
    head_cut = jnp.where(first_group, 0, head_cut)
    tail_cut = jnp.where(first_group, 0, tail_cut)
    index_row = jnp.arange(SEQ_LEN)[None, :]
    starts = jnp.where(index_row < head_cut, 0, jnp.where(index_row < SEQ_LEN - tail_cut, head_cut, SEQ_LEN - tail_cut))
    return (index_row - starts).reshape(-1).astype(jnp.int32)


def raised(array, own_key, source, target, shards_of, factor):
    owner, partner = [(jnp.arange(array.shape[position]) // (array.shape[position] // shards_of)).reshape([-1 if axis == position else 1 for axis in range(array.ndim)]) for position in (source, target)]
    chosen = jax.random.permutation(own_key, shards_of)[partner]
    strong = (owner == chosen) | (owner == (partner + shards_of // 2) % shards_of)
    return jnp.where(strong, factor * array, array)


def steps_of(rng, dims, cuts, low, top_value):
    def one(position, blocks):
        steps = jax.random.uniform(jax.random.fold_in(jax.random.fold_in(rng, 6), position), (blocks,), jnp.float32, low / len(cuts), top_value / len(cuts))
        return jnp.repeat(jnp.exp(steps), dims[position] // blocks).reshape((-1,) + (1,) * (len(dims) - position - 1))

    gain = one(*cuts[0])
    for cut in cuts[1:]:
        gain = gain * one(*cut)
    return gain


def centred(stream_key, extent, spread, most, shards=(), held_as=jnp.bfloat16):
    drawn = jax.random.normal(stream_key, extent, jnp.float32) * spread
    if len(shards) > 0:
        drawn = steps_of(stream_key, extent, shards, -0.22, 0.18) * drawn
    return jnp.clip(drawn, min=-most, max=most).astype(held_as)


def heavy_noise(own_key, shape, spread, most, cuts, heavy, kind=jnp.bfloat16):
    drawn = spread * jax.random.normal(own_key, shape, jnp.float32)
    if cuts:
        drawn = drawn * steps_of(own_key, shape, cuts, -0.22, 0.18)
    return jnp.clip(raised(drawn, jax.random.fold_in(own_key, 3), *heavy), -most, most).astype(kind)


def setup_inputs(seed: int = 0) -> dict:
    keys = jax.random.split(jax.random.key(seed), 11)
    return {
        "block_input": centred(keys[0], (TOKENS, D), 1.0, 6.0, ((0, 32),)),
        "positions": draw_positions(jax.random.fold_in(keys[10], 71), 0),
        "cotangent": heavy_noise(keys[2], (TOKENS, D), 1.0, 6.0, ((0, 32),), (0, 1, 32, 2.75)),
        "norm_attn": jnp.clip(1.0 + 0.1 * jax.random.normal(keys[3], (D,), jnp.float32), 0.5, 1.5).astype(jnp.bfloat16),
        "w_qkv": centred(keys[4], (D, QKV), D ** -0.5, 0.125, ((0, 32),)),
        "w_out": centred(keys[5], (D, D), (max(D // 256, 1)) ** -0.5, 2.0, ((0, 32),)),
        "norm_ffn": jnp.clip(1.0 + 0.1 * jax.random.normal(keys[6], (D,), jnp.float32), 0.5, 1.5).astype(jnp.bfloat16),
        "w_gate": centred(keys[7], (D, FF), D ** -0.5, 0.125, ((0, 32),)),
        "w_up": centred(keys[8], (D, FF), D ** -0.5, 0.125, ((0, 32),)),
        "w_down": centred(keys[9], (D, FF), FF ** -0.5, 0.0625, ((0, 32),)),
    }


EPS = 1e-05
THETA = 1000000.0

@jax.custom_vjp
def low(v):
    return lax.optimization_barrier(v.astype(jnp.bfloat16)).astype(jnp.float32)

@jax.custom_vjp
def low_back(v):
    return v

def low_keep(v):
    return (low(v), None)

def low_pass(kept, grad):
    return (grad,)

def back_keep(v):
    return (v, None)

def back_low(kept, grad):
    return (low(grad),)
low.defvjp(low_keep, low_pass)
low_back.defvjp(back_keep, back_low)

def rope_tables(places, head_width):
    frequency = THETA ** (-(jnp.arange(0, head_width, 2, dtype=jnp.float32) / head_width))
    angles = places.astype(jnp.float32)[:, None] * frequency[None, :]
    angles = jnp.concatenate([angles, angles], axis=-1)
    return (jnp.cos(angles)[:, None, :], jnp.sin(angles)[:, None, :])

def rotate(vectors, cosine, sine_table):
    half_dim = vectors.shape[-1] // 2
    turned = jnp.concatenate([-vectors[..., half_dim:], vectors[..., :half_dim]], axis=-1)
    return vectors * cosine + turned * sine_table

def product(left_side, right_side):
    return jnp.dot(left_side, right_side, precision=lax.Precision.HIGHEST)

def attend(queries, key_heads, value_heads, places):
    length = places.shape[0]
    index_row = jnp.arange(length, dtype=jnp.int32)
    starts = index_row - places
    blocks = places // BLOCK
    allowed = (starts[:, None] == starts[None, :]) & (blocks[None, :] <= blocks[:, None])
    grouped = queries.reshape(length, KV_HEADS, HEADS // KV_HEADS, HEAD_DIM)
    scores = jnp.einsum('tkgd,skd->kgts', grouped, key_heads, precision=lax.Precision.HIGHEST) * HEAD_DIM ** (-0.5)
    scores = low_back(jnp.where(allowed, scores, -1e+30))
    weights = low(jax.nn.softmax(scores, axis=-1))
    mixed_heads = jnp.einsum('kgts,skd->tkgd', weights, value_heads, precision=lax.Precision.HIGHEST)
    return mixed_heads.reshape(length, HEADS * HEAD_DIM)

def attend_bundle(bundle):
    return attend(bundle[0], bundle[1], bundle[2], bundle[3])

def layer_slab(residual_flow, places, gain_a, qkv_weight, out_weight, gain_f, gate_weight, up_weight, down_weight):
    q_cols = HEADS * HEAD_DIM
    kv_cols = KV_HEADS * HEAD_DIM
    attention_inverse_norm = lax.rsqrt(lax.optimization_barrier(jnp.mean(residual_flow * residual_flow, axis=-1, keepdims=True)) + EPS)
    attention_normalized = low(residual_flow * attention_inverse_norm * gain_a)
    qkv = low_back(product(attention_normalized, qkv_weight))
    cosine, sine_table = rope_tables(places, HEAD_DIM)
    queries = low(rotate(qkv[:, :q_cols].reshape(-1, HEADS, HEAD_DIM), cosine, sine_table))
    key_heads = low(rotate(qkv[:, q_cols:q_cols + kv_cols].reshape(-1, KV_HEADS, HEAD_DIM), cosine, sine_table))
    value_heads = low(qkv[:, q_cols + kv_cols:].reshape(-1, KV_HEADS, HEAD_DIM))
    seq_count = residual_flow.shape[0] // SEQ_LEN
    attended = lax.map(jax.checkpoint(attend_bundle), (queries.reshape(seq_count, SEQ_LEN, HEADS, HEAD_DIM), key_heads.reshape(seq_count, SEQ_LEN, KV_HEADS, HEAD_DIM), value_heads.reshape(seq_count, SEQ_LEN, KV_HEADS, HEAD_DIM), places.reshape(seq_count, SEQ_LEN)))
    attended = low(low_back(attended.reshape(-1, q_cols)))
    branch = low_back(product(attended, out_weight))
    middle_residual = residual_flow + branch
    feedforward_inverse_norm = lax.rsqrt(lax.optimization_barrier(jnp.mean(middle_residual * middle_residual, axis=-1, keepdims=True)) + EPS)
    feedforward_normalized = low(middle_residual * feedforward_inverse_norm * gain_f)
    gate_pre = low_back(product(feedforward_normalized, gate_weight))
    up_pre = low_back(product(feedforward_normalized, up_weight))
    hidden = low(jax.nn.silu(gate_pre) * up_pre)
    down = low_back(product(hidden, down_weight.T))
    return middle_residual + down

def reference(block_input, positions, cotangent, norm_attn, w_qkv, w_out, norm_ffn, w_gate, w_up, w_down):
    slab_seqs = math.gcd(TOKENS // SEQ_LEN, max(1, 4096 // SEQ_LEN))
    slab_rows = slab_seqs * SEQ_LEN
    slab_count = TOKENS // slab_rows
    checked = jax.checkpoint(layer_slab)

    def forward(residual_flow, gain_a, qkv_weight, out_weight, gain_f, gate_weight, up_weight, down_weight):

        def one_slab(carried, bundle):
            return (carried, checked(bundle[0], bundle[1], gain_a, qkv_weight, out_weight, gain_f, gate_weight, up_weight, down_weight))
        unused, slabs = lax.scan(one_slab, None, (residual_flow.reshape(slab_count, slab_rows, D), positions.reshape(slab_count, slab_rows)))
        return slabs.reshape(TOKENS, D)
    result, pullback = jax.vjp(forward, block_input.astype(jnp.float32), norm_attn.astype(jnp.float32), w_qkv.astype(jnp.float32), w_out.astype(jnp.float32), norm_ffn.astype(jnp.float32), w_gate.astype(jnp.float32), w_up.astype(jnp.float32), w_down.astype(jnp.float32))
    grads = pullback(cotangent.astype(jnp.float32))
    return (result.astype(jnp.bfloat16), grads[0], grads[1], grads[2], grads[3], grads[4], grads[5], grads[6], grads[7])
```

```python
import functools

import jax
import jax.numpy as jnp
from jax import lax
from jax.experimental import pallas as pl
from jax.experimental.pallas import tpu as pltpu
from jax.sharding import PartitionSpec as P

HEADS = 16
KV_HEADS = 8
HEAD_DIM = 128
BLOCK = 256
MOST_BLOCKS = 2
GROUP = HEADS // KV_HEADS
EPS = 1e-05
THETA = 1000000.0
MESH = pl.DeviceIdType.MESH
F32 = jnp.float32
BF16 = jnp.bfloat16

PLANE = 8
DEPTH = 4
FLIPS = [(1, 0), (0, 1), (1, 1)]


def rope_tables(places, head_width):
    frequency = THETA ** (-(jnp.arange(0, head_width, 2, dtype=F32) / head_width))
    angles = places.astype(F32)[:, None] * frequency[None, :]
    cosine, sine = jnp.cos(angles), jnp.sin(angles)
    return jnp.concatenate([cosine, cosine], axis=1), jnp.concatenate([-sine, sine], axis=1)


def dot(a, b, dims=((1,), (0,))):
    return lax.dot_general(a, b, (dims, ((), ())), preferred_element_type=F32)


NT = ((1,), (1,))
TN = ((0,), (0,))


def flip(bit, by):
    return lax.rem(bit + by, 2)


class Place:
    def __init__(self):
        rep, self.f = lax.axis_index("rep"), lax.axis_index("fsdp")
        self.r = lax.rem(rep, PLANE)
        self.base = rep - self.r
        self.z, self.x = lax.div(self.r, 2), lax.rem(self.r, 2)
        self.y, self.c = lax.div(self.f, 2), lax.rem(self.f, 2)
        self.p = self.x * 4 + self.f
        self.q = self.z * 2 + self.c
        self.d = self.r * 4 + self.f

    def at(self, z, x, y, c):
        return (self.base + z * 2 + x, y * 2 + c)

    def plane(self, dx, dy, dc):
        x, y, c = flip(self.x, dx), flip(self.y, dy), flip(self.c, dc)
        return self.at(self.z, x, y, c), x * 4 + y * 2 + c

    def column(self, dz, dc):
        z, c = lax.rem(self.z + dz, DEPTH), flip(self.c, dc)
        return self.at(z, self.x, self.y, c), z, c

    def behind(self, dz):
        return lax.rem(self.z + (DEPTH - dz), DEPTH)


class Net:
    def __init__(self, send, recv, local):
        self.send, self.recv, self.local_sem = send, recv, local
        self.used = 0
        self.sent, self.kept = [], []

    def take(self, count):
        self.used += count
        return self.used - count

    def copy(self, src, dst, send, recv, device):
        return pltpu.make_async_remote_copy(
            src_ref=src,
            dst_ref=dst,
            send_sem=self.send.at[send],
            recv_sem=self.recv.at[recv],
            device_id=device,
            device_id_type=MESH,
        )

    def put(self, src, dst, device):
        k = self.take(1)
        copy = self.copy(src, dst, k, k, device)
        copy.start()
        self.sent.append((None, copy))
        return copy

    def put_if(self, when, copy):
        pl.when(when)(copy.start)
        self.sent.append((when, copy))
        return copy

    def keep(self, src, dst):
        copy = pltpu.make_async_copy(src, dst, self.local_sem.at[len(self.kept)])
        copy.start()
        self.kept.append(copy)
        return copy

    def finish(self):
        for when, copy in self.sent:
            if when is None:
                copy.wait_send()
            else:
                pl.when(when)(copy.wait_send)


class Chain:
    def __init__(self, me, net, slot, twins=None):
        self.me, self.net, self.slot, self.twins = me, net, slot, twins
        self.base = net.take(8)
        last = DEPTH - 1
        self.first, self.last = me.z == 0, me.z == last
        self.inner = jnp.logical_and(me.z > 0, me.z < last)
        self.order = [
            me.z,
            1 + lax.rem(me.z, 2),
            jnp.where(self.inner, last * (me.z - 1), 2 - lax.div(me.z, last)),
            last * (1 - lax.div(me.z, 2)),
        ]

    def link(self, z, k, target):
        me = self.me
        ref = self.slot(z, me.c)
        return self.net.copy(ref, ref, self.base + k, self.base + z, me.at(target, me.x, me.y, me.c))

    def start(self):
        me, net = self.me, self.net
        net.put_if(jnp.logical_not(self.last), self.link(me.z, 0, me.z + 1))
        net.put_if(jnp.logical_not(self.first), self.link(me.z, 1, me.z - 1))
        if self.twins is not None:
            self.twin(me.z, 0)

    def twin(self, z, k):
        ref, net = self.slot(z, self.me.c), self.net
        copy = net.copy(ref, ref, self.base + 4 + k, self.base + 4 + z, self.twins)
        copy.start()
        net.sent.append((None, copy))

    def arrival(self, i):
        me, net = self.me, self.net
        z = self.order[i]
        onward = self.link(z, 1 + i, me.z + jnp.where(z < me.z, 1, -1))
        across = None
        net.sent.append((self.inner, onward))
        if self.twins is not None:
            ref = self.slot(z, me.c)
            across = net.copy(ref, ref, self.base + 4 + i, self.base + 4 + z, self.twins)
            net.sent.append((None, across))

        def take(passes):
            onward.wait_recv()
            if passes:
                onward.start()
            if across is not None:
                across.start()

        return (
            lambda: pl.when(self.inner)(lambda: take(True)),
            lambda: pl.when(jnp.logical_not(self.inner))(lambda: take(False)),
        )

    def arrive(self, i):
        for step in self.arrival(i):
            step()

    def twin_has(self, z):
        ref = self.slot(z, 1 - self.me.c)
        self.net.copy(ref, ref, self.base + 4, self.base + 4 + z, self.twins).wait_recv()

    def twin_all(self):
        for z in range(DEPTH):
            self.twin_has(z)


def greet(devices):
    barrier = pltpu.get_barrier_semaphore()
    for device in devices:
        pl.semaphore_signal(barrier, inc=1, device_id=device, device_id_type=MESH)
    return barrier


def plane_ids(me):
    return [
        me.plane(dx, dy, dc)[0] for dx in (0, 1) for dy in (0, 1) for dc in (0, 1) if dx + dy + dc
    ]


def column_ids(me):
    return [me.column(dz, dc)[0] for dz in range(1, DEPTH) for dc in (0, 1)]


def sems(sends, locals_):
    return [
        pltpu.SemaphoreType.DMA((sends,)),
        pltpu.SemaphoreType.DMA((sends,)),
        pltpu.SemaphoreType.DMA((locals_,)),
    ]


ANY = pl.BlockSpec(memory_space=pl.ANY)


def call(kernel, ident, outs, args, sends, locals_, scratch=()):
    return pl.pallas_call(
        kernel,
        out_shape=outs,
        in_specs=[ANY] * len(args),
        out_specs=[ANY] * len(outs),
        scratch_shapes=list(scratch) + sems(sends, locals_),
        compiler_params=pltpu.CompilerParams(
            collective_id=ident, has_side_effects=True, vmem_limit_bytes=60 * 1024 * 1024
        ),
    )(*args)


def swap_owner(me):
    there = me.at(me.f, lax.div(me.r, 4), lax.div(lax.rem(me.r, 4), 2), lax.rem(me.r, 2))
    back = (me.base + me.p, me.z)
    away = jnp.logical_or(me.r != me.p, me.f != me.z)
    return there, back, away


def turn(v):
    return pltpu.roll(v, HEAD_DIM // 2, 1)


def attend(R, T, codes, P, A, seq, length):
    half = length // 2
    keys_at = pl.ds(pl.multiple_of(seq * length, length), length)
    keys = R[keys_at, GROUP * HEAD_DIM : (GROUP + 1) * HEAD_DIM]
    values = R[keys_at, (GROUP + 1) * HEAD_DIM :]
    code = codes[seq, 0:1, :]
    for h in range(GROUP):
        cols = slice(h * HEAD_DIM, (h + 1) * HEAD_DIM)
        for part in range(2):
            rows = pl.ds(pl.multiple_of(seq * length + part * half, half), half)
            scores = dot(R[rows, cols], keys, NT) * HEAD_DIM ** (-0.5)
            most, least = T[2, rows, 0:1], T[2, rows, HEAD_DIM // 2 : HEAD_DIM // 2 + 1]
            scores = jnp.where((code <= most) & (code >= least), scores, -1e30)
            exponent = jnp.exp(scores - jnp.max(scores, axis=-1, keepdims=True))
            weights = (exponent / jnp.sum(exponent, axis=-1, keepdims=True)).astype(BF16)
            P[h, rows, :] = weights
            A[rows, cols] = dot(weights, values).astype(BF16)


def front_kernel(
    x, tab, code, cot, wq, wo, wg, wu, wd,
    sums, Uo, Ro, Po, Ao, To, Wqo, Woo, cg, Wg, Wu, Wd,
    U, T, codes, Wq, Wo, R, P, A, E, left, right, send, recv, local,
):
    me = Place()
    net = Net(send, recv, local)
    tokens = x.shape[0]
    there, back, away = swap_owner(me)
    barrier = greet(plane_ids(me) + column_ids(me))

    @pl.when(away)
    def _():
        pl.semaphore_signal(barrier, inc=1, device_id=there, device_id_type=MESH)
        pl.semaphore_signal(barrier, inc=1, device_id=back, device_id_type=MESH)

    pl.semaphore_wait(barrier, jnp.where(away, 15, 13))
    twin = me.plane(0, 0, 1)[0]
    x_next, y_next = me.plane(1, 0, 0)[0], me.plane(0, 1, 0)[0]

    def to_column(w, W):
        got = []
        for dz in (2, 1, 3, 0):
            for dc in (0, 1):
                device, z, c = me.column(dz, dc)
                cols = pl.ds(pl.multiple_of((z * 2 + c) * 1024, 1024), 1024)
                if dz + dc:
                    got.append(net.put(w.at[:, cols], W.at[me.d], device))
                else:
                    own = net.keep(w.at[:, cols], W.at[me.d])
        return got, own

    def spread(W, arrived):
        got, own = arrived
        for copy in got:
            copy.wait_recv()
        own.wait()
        sent = []
        for z in range(DEPTH):
            rows = pl.ds(z * 8 + me.p - me.c, 2)
            sent.append((net.put(W.at[rows], W.at[rows], x_next), net.put(W.at[rows], W.at[rows], y_next)))
        return sent

    def relay(W, sent):
        last = []
        for z in range(DEPTH):
            by_x, by_y = sent[z]
            if z % 2:
                by_x.wait_recv()
                rows = pl.ds(z * 8 + me.plane(1, 0, 0)[1] - me.c, 2)
                last += [net.put(W.at[rows], W.at[rows], y_next), by_y]
            else:
                by_y.wait_recv()
                rows = pl.ds(z * 8 + me.plane(0, 1, 0)[1] - me.c, 2)
                last += [net.put(W.at[rows], W.at[rows], x_next), by_x]
        return last

    def slab(p):
        return pl.ds(pl.multiple_of(p * tokens, tokens), tokens)

    q_in = []
    for dx in (0, 1):
        for dy in (0, 1):
            for dc in (0, 1):
                if dx + dy + dc:
                    device, p = me.plane(dx, dy, dc)
                    q_in.append(net.put(wq.at[p], Wq.at[me.d], device))
    q_own = net.keep(wq.at[me.p], Wq.at[me.d])
    k = net.take(1)
    swap = net.copy(wo, Wo.at[me.f], k, k, there)
    stay = pltpu.make_async_copy(wo, Wo.at[me.f], local.at[local.shape[0] - 1])
    stays = jnp.logical_not(away)
    pl.when(away)(swap.start)
    pl.when(stays)(stay.start)
    x_in = []
    for dx, dy in FLIPS:
        device, p = me.plane(dx, dy, 0)
        x_in.append((net.put(x, U.at[slab(me.p)], device), p))
    x_late = [net.put(x, U.at[slab(me.p)], twin)]
    x_own = [net.keep(x, U.at[slab(me.p)])]
    seq = lax.div(me.p, 4)
    lanes = pl.ds(pl.multiple_of(lax.rem(me.p, 4) * tokens, tokens), tokens)
    for src, dst in ((tab, T.at[:, slab(me.p)]), (code, codes.at[seq, :, lanes])):
        for device in plane_ids(me):
            x_late.append(net.put(src, dst, device))
        x_own.append(net.keep(src, dst))
    gate_in = to_column(wg, Wg)
    for copy in q_in:
        copy.wait_recv()
    q_own.wait()
    q_chain = Chain(me, net, lambda z, c: Wq.at[pl.ds(z * PLANE, PLANE)])
    o_chain = Chain(me, net, lambda z, c: Wo.at[z])
    c_chain = Chain(me, net, lambda z, c: cg.at[z * 2 + c], twin)
    c_own = net.keep(cot, cg.at[me.q])
    q_chain.start()
    for copy, p in x_in:
        copy.wait_recv()
        x_late.append(net.put(U.at[slab(p)], U.at[slab(p)], twin))
    pl.when(away)(swap.wait)
    pl.when(stays)(stay.wait)
    o_chain.start()
    q_chain.arrive(1)
    gate_sent = spread(Wg, gate_in)
    up_in = to_column(wu, Wu)
    q_chain.arrive(2)
    o_chain.arrive(1)
    last = relay(Wg, gate_sent)
    o_chain.arrive(2)
    q_chain.arrive(3)
    o_chain.arrive(3)
    for copy in x_late:
        copy.wait_recv()
    for copy in x_own:
        copy.wait()

    block = 2 * tokens
    lead = GROUP * HEAD_DIM

    def project(i, carry):
        rows = pl.ds(pl.multiple_of(i * block, block), block)
        q = dot(U[rows, :], Wq[...].reshape(Wq.shape[0] * Wq.shape[1], Wq.shape[2]))
        cosine, sine = T[0, rows, :], T[1, rows, :]
        for h in range(GROUP + 1):
            v = q[:, h * HEAD_DIM : (h + 1) * HEAD_DIM]
            R[rows, h * HEAD_DIM : (h + 1) * HEAD_DIM] = (v * cosine + turn(v) * sine).astype(BF16)
        R[rows, lead + HEAD_DIM :] = q[:, lead + HEAD_DIM :].astype(BF16)
        return carry

    lax.fori_loop(0, 8 * tokens // block, project, 0)

    def one(seq, carry):
        attend(R, T, codes, P, A, seq, 4 * tokens)
        return carry

    lax.fori_loop(0, 2, one, 0)

    def out_block(i, carry):
        rows = pl.ds(pl.multiple_of(i * block, block), block)
        E[rows, :] = dot(A[rows, :], Wo[...].reshape(Wo.shape[0] * Wo.shape[1], Wo.shape[2])).astype(BF16)
        return carry

    lax.fori_loop(0, 8 * tokens // block, out_block, 0)
    peers = plane_peers(me)
    waits = reduce_start(me, net, E, peers, left, right, 0, slab)
    for src, dst in ((U, Uo), (R, Ro), (P, Po), (A, Ao), (T, To), (Wq, Wqo), (Wo, Woo)):
        net.keep(src, dst)
    stores = net.kept[-7:]
    up_sent = spread(Wu, up_in)
    down_in = to_column(wd, Wd)
    more, own = reduce_finish(net, sums, peers, left, right, 0, waits)
    c_own.wait()
    c_chain.start()
    last += relay(Wu, up_sent)
    c_chain.arrive(1)
    c_chain.arrive(2)
    down_sent = spread(Wd, down_in)
    c_chain.arrive(3)
    last += relay(Wd, down_sent)
    for copy in last + more:
        copy.wait_recv()
    c_chain.twin_all()
    for copy in own + stores:
        copy.wait()
    net.finish()


def add_into(left, right, k):
    rows = left.shape[1]

    def body(i, carry):
        at = pl.ds(pl.multiple_of(i * 16, 16), 16)
        left[k, at] = (left[k, at].astype(F32) + right[k, at].astype(F32)).astype(BF16)
        return carry

    lax.fori_loop(0, rows // 16, body, 0)


def reduce_start(me, net, part, peers, left, right, first, at=lambda p: p):
    twin = me.plane(0, 0, 1)[0]
    waits = []
    for k, (own, other, _) in enumerate(peers):
        got = net.put(part.at[at(other)], right.at[first + k], twin)
        mine = net.keep(part.at[at(own)], left.at[first + k])
        waits.append((got, mine))
    return waits


def reduce_finish(net, out, peers, left, right, first, waits):
    late, own = [], []
    for k, ((_, _, device), (got, mine)) in enumerate(zip(peers, waits)):
        got.wait_recv()
        mine.wait()
        add_into(left, right, first + k)
        if device is None:
            own.append(net.keep(left.at[first + k], out.at[k]))
        else:
            late.append(net.put(left.at[first + k], out.at[k], device))
    return late, own


def plane_peers(me):
    peers = []
    for dx, dy in FLIPS + [(0, 0)]:
        device, p = me.plane(dx, dy, 0)
        peers.append((p, me.plane(dx, dy, 1)[1], device if dx + dy else None))
    return peers


def column_peers(me):
    peers = []
    for dz in (2, 1, 3, 0):
        device, z, c = me.column(dz, 0)
        peers.append((z * 2 + c, z * 2 + flip(c, 1), device if dz else None))
    return peers


def ffn_kernel(x, cot, wg, wu, wd, e_out, o_out, gg, gu, gd, gain, N, C, Wg, Wu, Wd, H, DG, DU, O, E, R, G, S, n_send, n_recv, x_send, x_recv, e_send, e_recv, local):
    me = Place()
    tokens = x.shape[0]
    chip = 2 * tokens
    twin = me.plane(0, 0, 1)[0]
    ids = [me.column(dz, 0)[0] for dz in range(1, DEPTH)] + [twin]
    barrier = greet(ids)
    loads = [
        pltpu.make_async_copy(src, dst, local.at[i])
        for i, (src, dst) in enumerate(((wg, Wg), (wu, Wu), (wd, Wd), (cot, C)))
    ]
    for load in loads:
        load.start()
    own_rows = pl.ds(pl.multiple_of(me.q * tokens, tokens), tokens)
    mine = pltpu.make_async_copy(x, N.at[own_rows], local.at[4])
    mine.start()
    pl.semaphore_wait(barrier, 4)

    def rows_of(z, c):
        return pl.ds(pl.multiple_of((z * 2 + c) * tokens, tokens), tokens)

    def remote(src, dst, send, recv, device):
        return pltpu.make_async_remote_copy(
            src_ref=src,
            dst_ref=dst,
            send_sem=send,
            recv_sem=recv,
            device_id=device,
            device_id_type=MESH,
        )

    def column_id(z):
        return me.at(z, me.x, me.y, me.c)

    odd = lax.rem(me.z, 2)
    order = [me.z, 1 + odd, lax.rem(me.z + 2, DEPTH), 3 * (1 - odd)]
    net = Net(n_send, n_recv, local)
    chain = Chain(me, net, lambda z, c: N.at[rows_of(z, c)], twin)

    def twin_has(i):
        chain.twin_has(order[i])

    tile = 512

    def block(i):
        base = order[i] * chip
        rows = pl.ds(pl.multiple_of(base, chip), chip)

        def hidden_tile(t, carry):
            cols = pl.ds(pl.multiple_of(t * tile, tile), tile)
            gate = dot(N[rows, :], Wg[:, cols])
            raised = dot(N[rows, :], Wu[:, cols])
            d_hidden = dot(C[rows, :], Wd[:, cols])
            sig = jax.nn.sigmoid(gate)
            act = gate * sig
            H[rows, cols] = (act * raised).astype(BF16)
            DU[rows, cols] = (d_hidden * act).astype(BF16)
            DG[rows, cols] = (d_hidden * raised * sig * (1.0 + gate * (1.0 - sig))).astype(BF16)
            return carry

        lax.fori_loop(0, H.shape[1] // tile, hidden_tile, 0)

        def out_tile(t, carry):
            cols = pl.ds(pl.multiple_of(t * tile, tile), tile)
            e = dot(DG[rows, :], Wg[cols, :], NT) + dot(DU[rows, :], Wu[cols, :], NT)
            E[rows, cols] = e.astype(BF16)
            piece = jnp.sum((e * N[rows, cols].astype(F32)).reshape(chip // 8, 8, tile), axis=0)
            if i == 0:
                S[:, cols] = piece
            else:
                S[:, cols] += piece
            O[rows, cols] = dot(H[rows, :], Wd[cols, :], NT).astype(BF16)
            return carry

        lax.fori_loop(0, E.shape[1] // tile, out_tile, 0)

    swaps, sums = [], []

    def swap(i):
        o = order[i]
        copy = remote(E.at[rows_of(o, 1 - me.c)], R.at[i], x_send.at[i], x_recv.at[i], twin)
        copy.start()
        swaps.append(copy)

    def total(i):
        o = order[i]
        swaps[i].wait_recv()
        first = (o * 2 + me.c) * tokens

        def body(k, carry):
            at = pl.ds(pl.multiple_of(k * 16, 16), 16)
            to = pl.ds(pl.multiple_of(first + k * 16, 16), 16)
            E[to, :] = (E[to, :].astype(F32) + R[i, at, :].astype(F32)).astype(BF16)
            return carry

        lax.fori_loop(0, tokens // 16, body, 0)
        rows = rows_of(o, me.c)
        if i == 0:
            copy = pltpu.make_async_copy(E.at[rows], e_out.at[me.z], local.at[5])
        else:
            copy = remote(E.at[rows], e_out.at[me.z], e_send.at[i], e_recv.at[me.z], column_id(o))
        copy.start()
        sums.append(copy)

    mine.wait()
    chain.start()
    for load in loads:
        load.wait()
    twin_has(0)
    block(0)
    swap(0)
    chain.arrive(1)
    early, later = chain.arrival(2)
    early()
    twin_has(1)
    block(1)
    swap(1)
    total(0)
    later()
    chain.arrive(3)
    twin_has(2)
    block(2)
    swap(2)
    total(1)
    twin_has(3)
    block(3)
    swap(3)
    total(2)
    stores = [
        pltpu.make_async_copy(O, o_out, local.at[6]),
        pltpu.make_async_copy(S, gain, local.at[7]),
    ]
    for store in stores:
        store.start()
    total(3)

    span = 256

    def grad_tile(t, carry):
        rows = pl.ds(pl.multiple_of(t * span, span), span)
        n, c = N[:, rows], C[:, rows]
        G[0, rows, :] = dot(n, DG[...], TN).astype(BF16)
        G[1, rows, :] = dot(n, DU[...], TN).astype(BF16)
        G[2, rows, :] = dot(c, H[...], TN).astype(BF16)
        return carry

    lax.fori_loop(0, G.shape[1] // span, grad_tile, 0)
    for i, dst in enumerate((gg, gu, gd)):
        store = pltpu.make_async_copy(G.at[i], dst, local.at[8 + i])
        store.start()
        stores.append(store)
    for i in range(1, DEPTH):
        o = order[i]
        remote(E.at[own_rows], e_out.at[o], e_send.at[i], e_recv.at[o], twin).wait_recv()
    sums[0].wait()
    for copy in sums[1:] + swaps:
        copy.wait_send()
    net.finish()
    for store in stores:
        store.wait()


def add_rows(into, i, more, j):
    slots, rows = into.shape[-3], into.shape[-2]
    steps = rows // 16

    def body(k, carry):
        s, at = lax.div(k, steps), pl.ds(pl.multiple_of(lax.rem(k, steps) * 16, 16), 16)
        into[i, s, at] = (into[i, s, at].astype(F32) + more[j, s, at].astype(F32)).astype(BF16)
        return carry

    lax.fori_loop(0, slots * steps, body, 0)


def back_kernel(
    x, part_o, gg, gu, gd, gain_f, u, r, pw, att, t, wq, wo,
    out_o, out_e, og, ou, od, oq, oo, ov,
    D, U, R, P, A, T, Wq, Wo, dA, dR, E, GQ, GO, gains, left, right, own, side, came, rq, ro, rv,
    send, recv, local,
):
    me = Place()
    net = Net(send, recv, local)
    tokens = x.shape[0]
    back, there, away = swap_owner(me)
    barrier = greet(plane_ids(me) + column_ids(me))

    @pl.when(away)
    def _():
        pl.semaphore_signal(barrier, inc=1, device_id=there, device_id_type=MESH)
        pl.semaphore_signal(barrier, inc=1, device_id=back, device_id_type=MESH)

    pl.semaphore_wait(barrier, jnp.where(away, 15, 13))
    twin = me.plane(0, 0, 1)[0]
    x_next, px = me.plane(1, 0, 0)
    y_next, py = me.plane(0, 1, 0)
    pd = me.plane(1, 1, 0)[1]

    def slab(p):
        return pl.ds(pl.multiple_of(p * tokens, tokens), tokens)

    def quarter(grad, p, z):
        return grad.at[pl.ds(z * 8 + p - me.c, 2)]

    def first(g, grad):
        sent = []
        for z in range(DEPTH):
            device, near = (x_next, px) if z < 2 else (y_next, py)
            side_p = py if z < 2 else px
            at = pl.ds(z % 2 * 2, 2)
            half = z // 2
            sent.append(net.put(quarter(grad, near, z), came.at[g * 6 + half * 3, at], device))
            sent.append(net.put(quarter(grad, pd, z), came.at[g * 6 + half * 3 + 1, at], device))
            net.keep(quarter(grad, me.p, z), own.at[g * 2 + half, at])
            net.keep(quarter(grad, side_p, z), side.at[g * 2 + half, at])
        return sent, net.kept[-8:]

    def second(g, begun):
        sent, kept = begun
        for copy in sent:
            copy.wait_recv()
        for copy in kept:
            copy.wait()
        passed = []
        for half in (0, 1):
            add_rows(side, g * 2 + half, came, g * 6 + half * 3 + 1)
            device = x_next if half else y_next
            passed.append(net.put(side.at[g * 2 + half], came.at[g * 6 + half * 3 + 2], device))
        for half in (0, 1):
            add_rows(own, g * 2 + half, came, g * 6 + half * 3)
        return passed

    cols = pl.ds(pl.multiple_of(me.q * 1024, 1024), 1024)
    thirds = []

    def third(g, passed, out):
        for half in (0, 1):
            passed[half].wait_recv()
            add_rows(own, g * 2 + half, came, g * 6 + half * 3 + 2)
        for dz in (2, 1, 3, 0):
            for dc in (0, 1):
                device, z, c = me.column(dz, dc)
                src = own.at[g * 2 + lax.div(z, 2), lax.rem(z, 2) * 2 + c]
                if dz + dc:
                    late.append(net.put(src, out.at[:, cols], device))
                else:
                    thirds.append(net.keep(src, out.at[:, cols]))

    got = []
    for dx, dy in FLIPS:
        device, p = me.plane(dx, dy, 0)
        got.append((net.put(x, D.at[slab(me.p)], device), p))
    d_late = [net.put(x, D.at[slab(me.p)], twin)]
    loads = [net.keep(x, D.at[slab(me.p)])]
    for src, dst in ((wo, Wo), (att, A), (r, R), (pw, P), (t, T), (u, U), (wq, Wq), (gain_f, gains.at[1])):
        loads.append(net.keep(src, dst))
    late = []
    begun = [first(0, gd)]
    peers = column_peers(me)
    waits = reduce_start(me, net, part_o, peers, left, right, 0, slab)
    for copy, p in got:
        copy.wait_recv()
        d_late.append(net.put(D.at[slab(p)], D.at[slab(p)], twin))
    begun.append(first(1, gg))
    more, kept = reduce_finish(net, out_o, peers, left, right, 0, waits)
    for copy in d_late:
        copy.wait_recv()
    for copy in loads:
        copy.wait()

    block = 2 * tokens
    length = 4 * tokens
    lead = GROUP * HEAD_DIM
    scale = HEAD_DIM ** (-0.5)

    def d_attended(i, carry):
        rows = pl.ds(pl.multiple_of(i * block, block), block)
        dA[rows, :] = dot(D[rows, :], Wo[...].reshape(Wo.shape[0] * Wo.shape[1], Wo.shape[2]), NT).astype(BF16)
        return carry

    lax.fori_loop(0, 8 * tokens // block, d_attended, 0)

    def turn_back(v, rows):
        return (v * T[0, rows, :] - turn(v) * T[1, rows, :]).astype(BF16)

    def one(seq, carry):
        keys_at = pl.ds(pl.multiple_of(seq * length, length), length)
        keys = R[keys_at, lead : lead + HEAD_DIM]
        values = R[keys_at, lead + HEAD_DIM :]
        d_keys = jnp.zeros((length, HEAD_DIM), F32)
        d_values = jnp.zeros((length, HEAD_DIM), F32)
        for h in range(GROUP):
            cols = slice(h * HEAD_DIM, (h + 1) * HEAD_DIM)
            for part in range(2):
                rows = pl.ds(pl.multiple_of(seq * length + part * (length // 2), length // 2), length // 2)
                low = P[h, rows, :]
                weights = low.astype(F32)
                d_out = dA[rows, cols]
                d_weights = dot(d_out, values, NT)
                d_scores = (
                    weights * (d_weights - jnp.sum(weights * d_weights, axis=-1, keepdims=True))
                ).astype(BF16)
                dR[rows, cols] = turn_back(dot(d_scores, keys) * scale, rows)
                d_keys += dot(d_scores, R[rows, cols], TN)
                d_values += dot(low, d_out, TN)
        dR[keys_at, lead : lead + HEAD_DIM] = turn_back(d_keys * scale, keys_at)
        dR[keys_at, lead + HEAD_DIM :] = d_values.astype(BF16)
        return carry

    lax.fori_loop(0, 2, one, 0)
    tile = 512

    def e_tile(k, carry):
        i, j = lax.div(k, E.shape[1] // tile), lax.rem(k, E.shape[1] // tile)
        rows = pl.ds(pl.multiple_of(i * block, block), block)
        cols = pl.ds(pl.multiple_of(j * tile, tile), tile)
        slots = pl.ds(j * (tile // Wq.shape[1]), tile // Wq.shape[1])
        e = dot(dR[rows, :], Wq[slots].reshape(tile, Wq.shape[2]), NT)
        E[rows, cols] = e.astype(BF16)
        piece = jnp.sum((e * U[rows, cols].astype(F32)).reshape(block // 8, 8, tile), axis=0)
        gains[0, :, cols] = jnp.where(i == 0, 0.0, gains[0, :, cols]) + piece
        return carry

    lax.fori_loop(0, 8 * tokens // block * (E.shape[1] // tile), e_tile, 0)
    peers_e = plane_peers(me)
    waits_e = reduce_start(me, net, E, peers_e, left, right, 4, slab)
    passed = [second(0, begun[0])]
    begun.append(first(2, gu))
    span = 256

    def q_tile(k, carry):
        cols = pl.ds(pl.multiple_of(k * span, span), span)
        slots = pl.ds(k * (span // GQ.shape[1]), span // GQ.shape[1])
        g = dot(U[:, cols], dR[...], TN).astype(BF16)
        GQ[slots] = g.reshape(span // GQ.shape[1], GQ.shape[1], GQ.shape[2])
        return carry

    lax.fori_loop(0, U.shape[1] // span, q_tile, 0)

    def o_tile(k, carry):
        cols = pl.ds(pl.multiple_of(k * tile, tile), tile)
        g = dot(A[...], D[:, cols], TN).astype(BF16)
        GO[:, :, cols] = g.reshape(GO.shape[0], GO.shape[1], tile)
        return carry

    lax.fori_loop(0, D.shape[1] // tile, o_tile, 0)
    a_late, a_own = [], []
    for dz in (2, 1, 3, 0):
        device, z, _ = me.column(dz, 0)
        rows = pl.ds(z * PLANE, PLANE)
        lanes = pl.ds(pl.multiple_of(z * 512, 512), 512)
        for src, dst in (
            (GQ.at[rows], rq.at[dz]),
            (GO.at[z], ro.at[dz]),
            (gains.at[:, :, lanes], rv.at[dz]),
        ):
            if dz:
                a_late.append(net.put(src, dst, device))
            else:
                a_own.append(net.keep(src, dst))
    e_late, e_own = reduce_finish(net, out_e, peers_e, left, right, 4, waits_e)
    passed.append(second(1, begun[1]))
    third(0, passed[0], od)
    for copy in a_late:
        copy.wait_recv()
    for copy in a_own:
        copy.wait()

    def sum_q(k, carry):
        s, at = lax.div(k, 4), pl.ds(pl.multiple_of(lax.rem(k, 4) * 16, 16), 16)
        rq[0, s, at] = sum(rq[i, s, at].astype(F32) for i in range(DEPTH)).astype(BF16)
        return carry

    lax.fori_loop(0, PLANE * 4, sum_q, 0)

    def sum_o(k, carry):
        at = pl.ds(pl.multiple_of(k * 16, 16), 16)
        ro[0, at] = sum(ro[i, at].astype(F32) for i in range(DEPTH)).astype(BF16)
        return carry

    lax.fori_loop(0, ro.shape[1] // 16, sum_o, 0)
    rv[0] = rv[0] + rv[1] + rv[2] + rv[3]
    k = net.take(1)
    swap = net.copy(ro.at[0], oo, k, k, there)
    stay = pltpu.make_async_copy(ro.at[0], oo, local.at[local.shape[0] - 1])
    stays = jnp.logical_not(away)
    pl.when(away)(swap.start)
    pl.when(stays)(stay.start)
    for dx in (0, 1):
        for dy in (0, 1):
            for dc in (0, 1):
                device, p = me.plane(dx, dy, dc)
                lanes = pl.ds(pl.multiple_of(lax.div(p, 2) * 128, 128), 128)
                for src, dst in ((rq.at[0, p], oq.at[me.p]), (rv.at[0, :, :, lanes], ov.at[me.p])):
                    if dx + dy + dc:
                        late.append(net.put(src, dst, device))
                    else:
                        kept.append(net.keep(src, dst))
    passed.append(second(2, begun[2]))
    third(1, passed[1], og)
    third(2, passed[2], ou)
    for copy in late + more + e_late:
        copy.wait_recv()
    for copy in kept + e_own + thirds:
        copy.wait()
    net.finish()
    pl.when(away)(swap.wait)
    pl.when(stays)(stay.wait)


def shape(*dims, dtype=BF16):
    return jax.ShapeDtypeStruct(dims, dtype)


def shards(copies, block_input, positions, cotangent, norm_attn, w_qkv, w_out, norm_ffn, w_gate, w_up, w_down):
    tokens, width = block_input.shape
    ff = w_gate.shape[1]
    q_cols, kv_cols = HEADS * HEAD_DIM, KV_HEADS * HEAD_DIM
    spread = ("rep", "fsdp")
    place = lax.rem(lax.axis_index("rep"), PLANE) * 4 + lax.axis_index("fsdp")

    def take(w):
        if copies == 1:
            return w
        rows = w.shape[0] * copies
        whole = lax.all_gather(w, spread, axis=0, tiled=True)
        return lax.dynamic_slice_in_dim(whole, place * rows, rows, axis=0)

    def give(grad):
        if copies == 1:
            return grad
        rows = grad.shape[0]
        whole = jnp.zeros((rows * 32,) + grad.shape[1:], grad.dtype)
        whole = lax.dynamic_update_slice_in_dim(whole, grad, place * rows, axis=0)
        return lax.psum_scatter(whole, spread, scatter_dimension=0, tiled=True)

    gain_a = take(norm_attn).astype(F32)
    gain_f = take(norm_ffn).astype(F32)
    own_qkv = (take(w_qkv).astype(F32) * gain_a[:, None]).astype(BF16)
    rows = own_qkv.shape[0]
    own_qkv = jnp.concatenate(
        [
            own_qkv[:, :q_cols].reshape(rows, KV_HEADS, GROUP * HEAD_DIM),
            own_qkv[:, q_cols : q_cols + kv_cols].reshape(rows, KV_HEADS, HEAD_DIM),
            own_qkv[:, q_cols + kv_cols :].reshape(rows, KV_HEADS, HEAD_DIM),
        ],
        axis=2,
    ).transpose(1, 0, 2)
    own_gate = (take(w_gate).astype(F32) * gain_f[:, None]).astype(BF16)
    own_up = (take(w_up).astype(F32) * gain_f[:, None]).astype(BF16)
    own_down = take(w_down)
    own_out = take(w_out)
    head_cols = (GROUP + 2) * HEAD_DIM
    ff_cols = ff // 8
    full = 8 * tokens
    residual = block_input.astype(F32)
    inv_a = lax.rsqrt(jnp.mean(residual * residual, axis=-1, keepdims=True) + EPS)
    xhat_a = residual * inv_a
    cosine, sine = rope_tables(positions, HEAD_DIM)
    starts = lax.axis_index("fsdp") * tokens + jnp.arange(tokens, dtype=jnp.int32) - positions
    least = (starts * MOST_BLOCKS).astype(F32)
    code = least + (positions // BLOCK).astype(F32)
    half = HEAD_DIM // 2
    sees = jnp.concatenate(
        [jnp.broadcast_to(v[:, None], (tokens, half)) for v in (code, least)], axis=1
    )
    tables = jnp.stack([cosine, sine, sees])
    sums, U, R, Pw, A, T, Wq, Wo, cg, Wg, Wu, Wd = call(
        front_kernel,
        0,
        [
            shape(4, tokens, width),
            shape(full, width),
            shape(full, head_cols),
            shape(GROUP, full, full // 2),
            shape(full, GROUP * HEAD_DIM),
            shape(3, full, HEAD_DIM, dtype=F32),
            shape(32, rows, head_cols),
            shape(4, rows, width),
            shape(8, tokens, width),
            shape(32, rows, ff_cols),
            shape(32, rows, ff_cols),
            shape(32, rows, ff_cols),
        ],
        (
            xhat_a.astype(BF16),
            tables,
            jnp.broadcast_to(code[None, :], (8, tokens)),
            cotangent,
            own_qkv,
            own_out,
            own_gate,
            own_up,
            own_down,
        ),
        150,
        30,
        [
            pltpu.VMEM((full, width), BF16),
            pltpu.VMEM((3, full, HEAD_DIM), F32),
            pltpu.VMEM((2, 8, full // 2), F32),
            pltpu.VMEM((32, rows, head_cols), BF16),
            pltpu.VMEM((4, rows, width), BF16),
            pltpu.VMEM((full, head_cols), BF16),
            pltpu.VMEM((GROUP, full, full // 2), BF16),
            pltpu.VMEM((full, GROUP * HEAD_DIM), BF16),
            pltpu.VMEM((full, width), BF16),
            pltpu.VMEM((4, tokens, width), BF16),
            pltpu.VMEM((4, tokens, width), BF16),
        ],
    )
    cg = cg.reshape(full, width)
    Wg, Wu, Wd = [w.reshape(width, ff_cols) for w in (Wg, Wu, Wd)]

    middle = residual + jnp.sum(sums.astype(F32), axis=0)
    inv_f = lax.rsqrt(jnp.mean(middle * middle, axis=-1, keepdims=True) + EPS)
    unit_f = middle * inv_f
    e_sums, out_part, g_gate, g_up, g_down, gain_f_part = pl.pallas_call(
        ffn_kernel,
        out_shape=[
            shape(4, tokens, width),
            shape(full, width),
            shape(width, ff_cols),
            shape(width, ff_cols),
            shape(width, ff_cols),
            shape(8, width, dtype=F32),
        ],
        in_specs=[ANY] * 5,
        out_specs=[ANY] * 6,
        scratch_shapes=[pltpu.VMEM((full, width), BF16)] * 2
        + [pltpu.VMEM((width, ff_cols), BF16)] * 3
        + [pltpu.VMEM((full, ff_cols), BF16)] * 3
        + [pltpu.VMEM((full, width), BF16)] * 2
        + [
            pltpu.VMEM((4, tokens, width), BF16),
            pltpu.VMEM((3, width, ff_cols), BF16),
            pltpu.VMEM((8, width), F32),
        ]
        + [pltpu.SemaphoreType.DMA((8,))] * 6
        + [pltpu.SemaphoreType.DMA((12,))],
        compiler_params=pltpu.CompilerParams(
            collective_id=2, has_side_effects=True, vmem_limit_bytes=60 * 1024 * 1024
        ),
    )(unit_f.astype(BF16), cg, Wg, Wu, Wd)
    g_gate, g_up, g_down = [g.reshape(32, rows, ff_cols) for g in (g_gate, g_up, g_down)]
    e_own = jnp.sum(e_sums.astype(F32), axis=0)
    d_middle = cotangent.astype(F32) + inv_f * (
        e_own - unit_f * jnp.mean(e_own * unit_f, axis=-1, keepdims=True)
    )

    quad = pltpu.VMEM((8, tokens, width), BF16)
    out_sums, ea_sums, og, ou, od, oq, oo, ov = call(
        back_kernel,
        3,
        [shape(4, tokens, width)] * 2
        + [shape(rows, ff)] * 3
        + [
            shape(8, rows, head_cols),
            shape(rows, width),
            shape(8, 2, 8, 128, dtype=F32),
        ],
        (d_middle.astype(BF16), out_part, g_gate, g_up, g_down, gain_f_part, U, R, Pw, A, T, Wq, Wo),
        140,
        80,
        [
            pltpu.VMEM((full, width), BF16),
            pltpu.VMEM((full, width), BF16),
            pltpu.VMEM((full, head_cols), BF16),
            pltpu.VMEM((GROUP, full, full // 2), BF16),
            pltpu.VMEM((full, GROUP * HEAD_DIM), BF16),
            pltpu.VMEM((3, full, HEAD_DIM), F32),
            pltpu.VMEM((32, rows, head_cols), BF16),
            pltpu.VMEM((4, rows, width), BF16),
            pltpu.VMEM((full, GROUP * HEAD_DIM), BF16),
            pltpu.VMEM((full, head_cols), BF16),
            pltpu.VMEM((full, width), BF16),
            pltpu.VMEM((32, rows, head_cols), BF16),
            pltpu.VMEM((4, rows, width), BF16),
            pltpu.VMEM((2, 8, width), F32),
            quad,
            quad,
            pltpu.VMEM((6, 4, rows, ff_cols), BF16),
            pltpu.VMEM((6, 4, rows, ff_cols), BF16),
            pltpu.VMEM((18, 4, rows, ff_cols), BF16),
            pltpu.VMEM((4, 8, rows, head_cols), BF16),
            pltpu.VMEM((4, rows, width), BF16),
            pltpu.VMEM((4, 2, 8, 512), F32),
        ],
    )
    layer_output = (middle + jnp.sum(out_sums.astype(F32), axis=0)).astype(BF16)
    e_own_a = jnp.sum(ea_sums.astype(F32), axis=0)
    input_gradient = d_middle + inv_a * (
        e_own_a - xhat_a * jnp.mean(e_own_a * xhat_a, axis=-1, keepdims=True)
    )
    gain_sums = jnp.sum(ov, axis=(0, 2))
    gain_sums = lax.dynamic_slice_in_dim(gain_sums, place % 2 * rows, rows, axis=1)
    oq = oq.astype(F32) * gain_a[None, :, None]
    q_part = oq[:, :, : GROUP * HEAD_DIM].transpose(1, 0, 2).reshape(rows, q_cols)
    k_part = oq[:, :, GROUP * HEAD_DIM : (GROUP + 1) * HEAD_DIM].transpose(1, 0, 2)
    v_part = oq[:, :, (GROUP + 1) * HEAD_DIM :].transpose(1, 0, 2)
    grad_qkv = jnp.concatenate(
        [q_part, k_part.reshape(rows, kv_cols), v_part.reshape(rows, kv_cols)], axis=1
    )
    return (
        layer_output,
        input_gradient,
        give(gain_sums[0] / gain_a),
        give(grad_qkv),
        give(oo.astype(F32)),
        give(gain_sums[1] / gain_f),
        give(og.astype(F32) * gain_f[:, None]),
        give(ou.astype(F32) * gain_f[:, None]),
        give(od.astype(F32)),
    )


def solution(mesh):
    copies = mesh.shape["rep"] * mesh.shape["fsdp"] // 32
    rows, flat = P(("rep", "fsdp"), None), P(("rep", "fsdp"))
    return jax.shard_map(
        functools.partial(shards, copies),
        mesh=mesh,
        in_specs=(rows, flat, rows, flat, rows, rows, flat, rows, rows, rows),
        out_specs=(rows, rows, flat, rows, rows, flat, rows, rows, rows),
        check_vma=False,
    )
```

```python
import functools
import math

import jax
import jax.numpy as jnp
from jax import lax
from jax.experimental import pallas as pl
from jax.experimental.pallas import tpu as pltpu
from jax.sharding import PartitionSpec as P

HEADS = 16
KV_HEADS = 8
HEAD_DIM = 128
BLOCK = 256
MOST_BLOCKS = 2
GROUP = HEADS // KV_HEADS
EPS = 1e-05
THETA = 1000000.0
MESH = pl.DeviceIdType.MESH
F32 = jnp.float32
BF16 = jnp.bfloat16

PLANE = 8
DEPTH = 4
FLIPS = [(1, 0), (0, 1), (1, 1)]


def dot(a, b, dims=((1,), (0,))):
    return lax.dot_general(a, b, (dims, ((), ())), preferred_element_type=F32)


NT = ((1,), (1,))
TN = ((0,), (0,))


def flip(bit, by):
    return lax.rem(bit + by, 2)


class Place:
    def __init__(self):
        rep, self.f = lax.axis_index("rep"), lax.axis_index("fsdp")
        self.r = lax.rem(rep, PLANE)
        self.base = rep - self.r
        self.z, self.x = lax.div(self.r, 2), lax.rem(self.r, 2)
        self.y, self.c = lax.div(self.f, 2), lax.rem(self.f, 2)
        self.p = self.x * 4 + self.f
        self.q = self.z * 2 + self.c
        self.d = self.r * 4 + self.f

    def at(self, z, x, y, c):
        return (self.base + z * 2 + x, y * 2 + c)

    def plane(self, dx, dy, dc):
        x, y, c = flip(self.x, dx), flip(self.y, dy), flip(self.c, dc)
        return self.at(self.z, x, y, c), x * 4 + y * 2 + c

    def column(self, dz, dc):
        z, c = lax.rem(self.z + dz, DEPTH), flip(self.c, dc)
        return self.at(z, self.x, self.y, c), z, c

    def behind(self, dz):
        return lax.rem(self.z + (DEPTH - dz), DEPTH)


class Net:
    def __init__(self, send, recv, local):
        self.send, self.recv, self.local_sem = send, recv, local
        self.used = 0
        self.sent, self.kept = [], []

    def take(self, count):
        self.used += count
        return self.used - count

    def copy(self, src, dst, send, recv, device):
        return pltpu.make_async_remote_copy(
            src_ref=src,
            dst_ref=dst,
            send_sem=self.send.at[send],
            recv_sem=self.recv.at[recv],
            device_id=device,
            device_id_type=MESH,
        )

    def put(self, src, dst, device):
        k = self.take(1)
        copy = self.copy(src, dst, k, k, device)
        copy.start()
        self.sent.append((None, copy))
        return copy

    def put_if(self, when, copy):
        pl.when(when)(copy.start)
        self.sent.append((when, copy))
        return copy

    def keep(self, src, dst):
        copy = pltpu.make_async_copy(src, dst, self.local_sem.at[len(self.kept)])
        copy.start()
        self.kept.append(copy)
        return copy

    def finish(self):
        for when, copy in self.sent:
            if when is None:
                copy.wait_send()
            else:
                pl.when(when)(copy.wait_send)


class Chain:
    def __init__(self, me, net, slot, twins=None):
        self.me, self.net, self.slot, self.twins = me, net, slot, twins
        self.base = net.take(12)
        last = DEPTH - 1
        self.first, self.last = me.z == 0, me.z == last
        self.inner = jnp.logical_and(me.z > 0, me.z < last)
        self.order = [
            me.z,
            1 + lax.rem(me.z, 2),
            jnp.where(self.inner, last * (me.z - 1), 2 - lax.div(me.z, last)),
            last * (1 - lax.div(me.z, 2)),
        ]
        self.steps = [None] + [self.arrival(i) for i in range(1, DEPTH)]

    def pass_on(self, i):
        self.steps[i][0]()

    def take_in(self, i):
        self.steps[i][1]()

    def link(self, z, k, target):
        me = self.me
        ref = self.slot(z, me.c)
        return self.net.copy(ref, ref, self.base + k, self.base + z, me.at(target, me.x, me.y, me.c))

    def start(self):
        me, net = self.me, self.net
        net.put_if(jnp.logical_not(self.last), self.link(me.z, 0, me.z + 1))
        net.put_if(jnp.logical_not(self.first), self.link(me.z, 1, me.z - 1))
        if self.twins is not None:
            self.twin(me.z, 0)

    def twin(self, z, k):
        ref, net = self.slot(z, self.me.c), self.net
        copy = net.copy(ref, ref, self.base + 8 + k, self.base + 4 + z, self.twins)
        copy.start()
        net.sent.append((None, copy))

    def arrival(self, i):
        me, net = self.me, self.net
        z = self.order[i]
        onward = self.link(z, 1 + i, me.z + jnp.where(z < me.z, 1, -1))
        across = None
        net.sent.append((self.inner, onward))
        if self.twins is not None:
            ref = self.slot(z, me.c)
            across = net.copy(ref, ref, self.base + 8 + i, self.base + 4 + z, self.twins)
            net.sent.append((None, across))

        def take(passes):
            onward.wait_recv()
            if passes:
                onward.start()
            if across is not None:
                across.start()

        return (
            lambda: pl.when(self.inner)(lambda: take(True)),
            lambda: pl.when(jnp.logical_not(self.inner))(lambda: take(False)),
        )

    def twin_has(self, z):
        ref = self.slot(z, 1 - self.me.c)
        self.net.copy(ref, ref, self.base + 4, self.base + 4 + z, self.twins).wait_recv()

    def twin_all(self):
        for z in range(DEPTH):
            self.twin_has(z)


def greet(devices):
    barrier = pltpu.get_barrier_semaphore()
    for device in devices:
        pl.semaphore_signal(barrier, inc=1, device_id=device, device_id_type=MESH)
    return barrier


def plane_ids(me):
    return [
        me.plane(dx, dy, dc)[0] for dx in (0, 1) for dy in (0, 1) for dc in (0, 1) if dx + dy + dc
    ]


def column_ids(me):
    return [me.column(dz, dc)[0] for dz in range(1, DEPTH) for dc in (0, 1)]


def sems(sends, locals_):
    return [
        pltpu.SemaphoreType.DMA((sends,)),
        pltpu.SemaphoreType.DMA((sends,)),
        pltpu.SemaphoreType.DMA((locals_,)),
    ]


ANY = pl.BlockSpec(memory_space=pl.ANY)


def call(kernel, ident, outs, args, sends, locals_, scratch=()):
    return pl.pallas_call(
        kernel,
        out_shape=outs,
        in_specs=[ANY] * len(args),
        out_specs=[ANY] * len(outs),
        scratch_shapes=list(scratch) + sems(sends, locals_),
        compiler_params=pltpu.CompilerParams(
            collective_id=ident, has_side_effects=True, vmem_limit_bytes=60 * 1024 * 1024
        ),
    )(*args)


def swap_owner(me):
    there = me.at(me.f, lax.div(me.r, 4), lax.div(lax.rem(me.r, 4), 2), lax.rem(me.r, 2))
    back = (me.base + me.p, me.z)
    away = jnp.logical_or(me.r != me.p, me.f != me.z)
    return there, back, away


def turn(v):
    return pltpu.roll(v, HEAD_DIM // 2, 1)


def rotations(table):
    swapped = turn(table)
    low = lax.broadcasted_iota(jnp.int32, table.shape, 1) < HEAD_DIM // 2
    return jnp.where(low, table, swapped), jnp.where(low, -swapped, table)


def attend(R, codes, P, A, seq, length):
    half = length // 2
    keys_at = pl.ds(seq * length, length)
    keys = R[keys_at, GROUP * HEAD_DIM : (GROUP + 1) * HEAD_DIM]
    values = R[keys_at, (GROUP + 1) * HEAD_DIM :]
    code = codes[seq, 0:1, :]
    for part in range(2):
        rows = pl.ds(seq * length + part * half, half)
        most = jnp.transpose(codes[seq, :, part * half : (part + 1) * half])[:, 0:1]
        least = jnp.floor(most * (1.0 / MOST_BLOCKS)) * MOST_BLOCKS
        allowed = (code <= most) & (code >= least)
        for h in range(GROUP):
            cols = slice(h * HEAD_DIM, (h + 1) * HEAD_DIM)
            scores = dot(R[rows, cols], keys, NT) * HEAD_DIM ** (-0.5)
            scores = jnp.where(allowed, scores, -1e30)
            exponent = jnp.exp(scores - jnp.max(scores, axis=-1, keepdims=True))
            weights = (exponent / jnp.sum(exponent, axis=-1, keepdims=True)).astype(BF16)
            P[h, rows, :] = weights
            A[rows, cols] = dot(weights, values).astype(BF16)


def front_kernel(
    x, pos, gain, cot, wq, wo, wg, wu, wd,
    sums, Uo, Ro, Po, Ao, To, Wqo, Woo, cg, Wg, Wu, Wd,
    X, places, gains, code, q_raw, q_own, g_own, u_own, U, T, codes, Wq, Wo, R, P, A, E, swapped, came, send, recv, local,
):
    me = Place()
    net = Net(send, recv, local)
    tokens = x.shape[0]
    there, back, away = swap_owner(me)
    barrier = greet(plane_ids(me) + column_ids(me))

    raw = [net.keep(src, dst) for src, dst in ((pos, places), (gain, gains), (x, X), (wq, q_raw), (wg, g_own), (wu, u_own))]

    @pl.when(away)
    def _():
        pl.semaphore_signal(barrier, inc=1, device_id=there, device_id_type=MESH)
        pl.semaphore_signal(barrier, inc=1, device_id=back, device_id_type=MESH)

    pl.semaphore_wait(barrier, jnp.where(away, 15, 13))
    twin = me.plane(0, 0, 1)[0]
    x_next, y_next = me.plane(1, 0, 0)[0], me.plane(0, 1, 0)[0]

    def slab(p):
        return pl.ds(pl.multiple_of(p * tokens, tokens), tokens)

    own_rows = slab(me.p)
    raw[1].wait()

    def normalize():
        raw[2].wait()

        def body(i, carry):
            at = pl.ds(pl.multiple_of(i * 16, 16), 16)
            v = X[at, :].astype(F32)
            v = v * lax.rsqrt(jnp.mean(v * v, axis=-1, keepdims=True) + EPS)
            U[pl.ds(pl.multiple_of(me.p * tokens + i * 16, 16), 16), :] = v.astype(BF16)
            return carry

        lax.fori_loop(0, tokens // 16, body, 0)

    def rotation_table():
        raw[0].wait()
        half = HEAD_DIM // 2
        place = places[...]
        column = jnp.transpose(place.astype(F32))[:, 0:1]
        index = lax.broadcasted_iota(jnp.int32, (1, half), 1).astype(F32)
        angles = column * jnp.exp(index * (-math.log(THETA) / half))
        T[own_rows, :] = jnp.concatenate([jnp.cos(angles), jnp.sin(angles)], axis=1)
        lane = lax.broadcasted_iota(jnp.int32, place.shape, 1)
        start = me.f * tokens + lane - place
        code[...] = (start * MOST_BLOCKS + lax.div(place, jnp.full_like(place, BLOCK))).astype(F32)

    def scale_q():
        raw[3].wait()
        by = gains[0, :, 0:1]
        lead = GROUP * HEAD_DIM
        for p in range(KV_HEADS):
            parts = (p * lead, lead), (HEADS * HEAD_DIM + p * HEAD_DIM, HEAD_DIM), ((HEADS + KV_HEADS + p) * HEAD_DIM, HEAD_DIM)
            to = 0
            for first, size in parts:
                q_own[p, :, to : to + size] = (q_raw[:, first : first + size].astype(F32) * by).astype(BF16)
                to += size

    def scale_f(k):
        raw[4 + k].wait()
        w = (g_own, u_own)[k]
        by = gains[1, :, 0:1]

        def body(i, carry):
            cols = pl.ds(pl.multiple_of(i * 1024, 1024), 1024)
            w[:, cols] = (w[:, cols].astype(F32) * by).astype(BF16)
            return carry

        lax.fori_loop(0, w.shape[1] // 1024, body, 0)

    weights = {"g": (g_own, Wg), "u": (u_own, Wu), "d": (wd, Wd)}
    taken, sent, last = {}, {}, []

    def column(n):
        if n != "d":
            scale_f("gu".index(n))
        w, W = weights[n]
        got = []
        for dz in (2, 1, 3, 0):
            for dc in (0, 1):
                device, z, c = me.column(dz, dc)
                cols = pl.ds(pl.multiple_of((z * 2 + c) * 1024, 1024), 1024)
                if dz + dc:
                    got.append(net.put(w.at[:, cols], W.at[me.d], device))
                else:
                    own = net.keep(w.at[:, cols], W.at[me.d])
        taken[n] = got, own

    def spread(n):
        W = weights[n][1]
        got, own = taken[n]
        for copy in got:
            copy.wait_recv()
        own.wait()
        for z in range(DEPTH):
            rows = pl.ds(z * 8 + me.p - me.c, 2)
            sent[n, z] = [net.put(W.at[rows], W.at[rows], device) for device in (x_next, y_next)]

    def relay(n, z):
        W = weights[n][1]
        by_x, by_y = sent[n, z]
        if z % 2:
            by_x.wait_recv()
            rows = pl.ds(z * 8 + me.plane(1, 0, 0)[1] - me.c, 2)
            last.extend((net.put(W.at[rows], W.at[rows], y_next), by_y))
        else:
            by_y.wait_recv()
            rows = pl.ds(z * 8 + me.plane(0, 1, 0)[1] - me.c, 2)
            last.extend((net.put(W.at[rows], W.at[rows], x_next), by_x))

    q_in = []

    def q_go():
        scale_q()
        for dx in (0, 1):
            for dy in (0, 1):
                for dc in (0, 1):
                    device, p = me.plane(dx, dy, dc)
                    if dx + dy + dc:
                        q_in.append(net.put(q_own.at[p], Wq.at[me.d], device))
                    else:
                        own = net.keep(q_own.at[p], Wq.at[me.d])
        q_in.append(own)

    q_chain = Chain(me, net, lambda z, c: Wq.at[pl.ds(z * PLANE, PLANE)])
    o_chain = Chain(me, net, lambda z, c: Wo.at[z])
    c_chain = Chain(me, net, lambda z, c: cg.at[z * 2 + c], twin)
    c_own = net.keep(cot, cg.at[me.q])

    def q_start():
        for copy in q_in[:-1]:
            copy.wait_recv()
        q_in[-1].wait()
        q_chain.start()

    k = net.take(1)
    swap = net.copy(wo, Wo.at[me.f], k, k, there)
    stay = pltpu.make_async_copy(wo, Wo.at[me.f], local.at[local.shape[0] - 1])
    stays = jnp.logical_not(away)

    def swap_go():
        pl.when(away)(swap.start)
        pl.when(stays)(stay.start)

    def o_start():
        pl.when(away)(swap.wait)
        pl.when(stays)(stay.wait)
        o_chain.start()

    def c_start():
        c_own.wait()
        c_chain.start()

    t_gather = PlaneGather(me, net, lambda p: T.at[slab(p)])
    x_gather = PlaneGather(me, net, lambda p: U.at[slab(p)])
    code_in = []

    def x_go():
        normalize()
        x_gather.start()

    def t_go():
        rotation_table()
        t_gather.start()

    def code_go():
        lanes = pl.ds(pl.multiple_of(lax.rem(me.p, 4) * tokens, tokens), tokens)
        at = codes.at[lax.div(me.p, 4), :, lanes]
        code_in.extend(net.put(code, at, device) for device in plane_ids(me))
        code_in.append(net.keep(code, at))

    block = 2 * tokens
    lead = GROUP * HEAD_DIM

    def project():
        def body(i, carry):
            rows = pl.ds(pl.multiple_of(i * block, block), block)
            q = dot(U[rows, :], Wq[...].reshape(Wq.shape[0] * Wq.shape[1], Wq.shape[2]))
            cosine, sine = rotations(T[rows, :])
            for h in range(GROUP + 1):
                v = q[:, h * HEAD_DIM : (h + 1) * HEAD_DIM]
                R[rows, h * HEAD_DIM : (h + 1) * HEAD_DIM] = (v * cosine + turn(v) * sine).astype(BF16)
            R[rows, lead + HEAD_DIM :] = q[:, lead + HEAD_DIM :].astype(BF16)
            return carry

        lax.fori_loop(0, 8 * tokens // block, body, 0)

    def attention(seq):
        if seq == 0:
            for copy in code_in[:-1]:
                copy.wait_recv()
            code_in[-1].wait()
        attend(R, codes, P, A, seq, 4 * tokens)

    total = PlaneSum(me, net, lambda p: E.at[slab(p)], swapped, came)
    stores = []

    def out_product():
        def body(i, carry):
            rows = pl.ds(pl.multiple_of(i * block, block), block)
            E[rows, :] = dot(A[rows, :], Wo[...].reshape(Wo.shape[0] * Wo.shape[1], Wo.shape[2])).astype(BF16)
            return carry

        lax.fori_loop(0, 8 * tokens // block, body, 0)
        total.start()
        for src, dst in ((U, Uo), (R, Ro), (P, Po), (A, Ao), (T, To), (Wq, Wqo), (Wo, Woo)):
            stores.append(net.keep(src, dst))

    column("d")
    column("u")
    t_go()
    code_go()
    column("g")
    q_go()
    x_go()
    x_gather.relay()
    x_gather.finish()
    spread("d")
    q_start()
    spread("u")
    swap_go()
    spread("g")
    relay("u", 0)
    q_chain.take_in(1)
    q_chain.pass_on(1)
    q_chain.pass_on(2)
    t_gather.relay()
    relay("u", 1)
    o_start()
    relay("u", 2)
    q_chain.pass_on(3)
    o_chain.pass_on(1)
    o_chain.pass_on(2)
    relay("g", 0)
    relay("g", 1)
    o_chain.pass_on(3)
    c_start()
    relay("g", 2)
    t_gather.finish()
    relay("d", 0)
    q_chain.take_in(2)
    relay("d", 1)
    o_chain.take_in(1)
    relay("d", 2)
    relay("g", 3)
    relay("u", 3)
    q_chain.take_in(3)
    project()
    attention(0)
    c_chain.pass_on(1)
    attention(1)
    c_chain.pass_on(2)
    o_chain.take_in(2)
    relay("d", 3)
    o_chain.take_in(3)
    out_product()
    total.cores()
    c_chain.take_in(1)
    c_chain.pass_on(3)
    total.chips()
    c_chain.take_in(2)
    c_chain.take_in(3)
    stores.append(total.finish(sums))
    for copy in last:
        copy.wait_recv()
    c_chain.twin_all()
    for copy in stores:
        copy.wait()
    net.finish()


def add_to(into, more):
    step = 16
    rows = into.shape[-2]
    steps = rows // step

    def body(k, carry):
        if len(into.shape) == 2:
            at = (pl.ds(pl.multiple_of(k * step, step), step),)
        else:
            at = (lax.div(k, steps), pl.ds(pl.multiple_of(lax.rem(k, steps) * step, step), step))
        into[at] = (into[at].astype(F32) + more[at].astype(F32)).astype(BF16)
        return carry

    lax.fori_loop(0, steps * (1 if len(into.shape) == 2 else into.shape[0]), body, 0)


class PlaneGather:
    def __init__(self, me, net, slab):
        self.me, self.net, self.slab = me, net, slab
        self.twin = me.plane(0, 0, 1)[0]
        self.x_next, self.px = me.plane(1, 0, 0)
        self.y_next, self.py = me.plane(0, 1, 0)
        self.pd = me.plane(1, 1, 0)[1]

    def start(self):
        net, own = self.net, self.slab(self.me.p)
        self.by_x = net.put(own, own, self.x_next)
        self.by_y = net.put(own, own, self.y_next)
        self.late = [net.put(own, own, self.twin)]

    def half(self, p, k):
        ref = self.slab(p)
        rows = ref.shape[0] // 2
        return ref.at[pl.ds(k * rows, rows)]

    def across(self, p):
        ref = self.slab(p)
        self.late.append(self.net.put(ref, ref, self.twin))

    def relay(self):
        net = self.net
        self.by_x.wait_recv()
        ref = self.half(self.px, 0)
        self.first = net.put(ref, ref, self.y_next)
        self.by_y.wait_recv()
        ref = self.half(self.py, 1)
        self.second = net.put(ref, ref, self.x_next)
        self.across(self.px)
        self.across(self.py)

    def finish(self):
        self.first.wait_recv()
        self.second.wait_recv()
        self.across(self.pd)
        for copy in self.late:
            copy.wait_recv()


class PlaneSum:
    def __init__(self, me, net, slab, swapped, came):
        self.me, self.net, self.slab, self.swapped, self.came = me, net, slab, swapped, came
        self.x_next, self.y_next = me.plane(1, 0, 0)[0], me.plane(0, 1, 0)[0]
        self.places = [me.plane(dx, dy, 0)[1] for dx, dy in FLIPS + [(0, 0)]]

    def start(self):
        me = self.me
        self.swaps = []
        for k, (dx, dy) in enumerate(FLIPS + [(0, 0)]):
            other = me.plane(dx, dy, 1)[1]
            self.swaps.append(
                self.net.put(self.slab(other), self.swapped.at[k], me.plane(0, 0, 1)[0])
            )

    def half(self, k, h):
        ref = self.slab(self.places[k])
        rows = ref.shape[0] // 2
        return ref.at[pl.ds(h * rows, rows)]

    def cores(self):
        for k in range(4):
            self.swaps[k].wait_recv()
            add_to(self.slab(self.places[k]), self.swapped.at[k])
            if k == 2:
                net, came = self.net, self.came
                self.first = [
                    net.put(self.half(2, 0), came.at[1], self.x_next),
                    net.put(self.half(2, 1), came.at[3], self.y_next),
                    net.put(self.half(0, 0), came.at[0], self.x_next),
                    net.put(self.half(1, 1), came.at[2], self.y_next),
                ]

    def chips(self):
        net, came = self.net, self.came
        for copy in self.first:
            copy.wait_recv()
        add_to(self.half(1, 0), came.at[1])
        second = [net.put(self.half(1, 0), came.at[4], self.y_next)]
        add_to(self.half(0, 1), came.at[3])
        second.append(net.put(self.half(0, 1), came.at[5], self.x_next))
        add_to(self.half(3, 0), came.at[0])
        add_to(self.half(3, 1), came.at[2])
        self.second = second

    def finish(self, out):
        for h in (0, 1):
            self.second[h].wait_recv()
            add_to(self.half(3, h), self.came.at[4 + h])
        return self.net.keep(self.slab(self.places[3]), out)


class ChainSum:
    def __init__(self, me, net, slots, up, down, add=add_to):
        self.me, self.net, self.slots, self.up, self.down, self.add = me, net, slots, up, down, add
        self.base = net.take(8)

    def copy(self, z, upward, target):
        me = self.me
        landing = self.up.at[z - 1] if upward else self.down.at[z]
        k = self.base + z + (0 if upward else 4)
        return self.net.copy(self.slots.at[z], landing, k, k, me.at(target, me.x, me.y, me.c))

    def step(self, at, z, upward):
        copy = self.copy(z, upward, at + 1 if upward else at - 1)
        here = self.me.z == at

        def go():
            if at != (0 if upward else DEPTH - 1):
                copy.wait_recv()
                self.add(self.slots.at[z], self.up.at[z - 1] if upward else self.down.at[z])
            copy.start()

        pl.when(here)(go)
        self.net.sent.append((here, copy))

    def begin(self, hops):
        self.step(0, hops, True)
        self.step(DEPTH - 1, DEPTH - 1 - hops, False)

    def near(self, hops):
        self.step(1, 1 + hops, True)
        self.step(2, 2 - hops, False)

    def far(self):
        self.step(2, 3, True)
        self.step(1, 0, False)

    def finish(self):
        me = self.me

        @pl.when(me.z > 0)
        def _():
            self.copy(me.z, True, me.z).wait_recv()
            self.add(self.slots.at[me.z], self.up.at[me.z - 1])

        @pl.when(me.z < DEPTH - 1)
        def _():
            self.copy(me.z, False, me.z).wait_recv()
            self.add(self.slots.at[me.z], self.down.at[me.z])


class ColumnSum:
    def __init__(self, me, net, slots, came):
        self.me, self.net, self.slots, self.came = me, net, slots, came

    def start(self):
        me = self.me
        self.sent = []
        for k, dz in enumerate((2, 1, 3)):
            device, z, _ = me.column(dz, 0)
            self.sent.append(self.net.put(self.slots.at[z], self.came.at[k], device))

    def finish(self):
        for k, copy in enumerate(self.sent):
            copy.wait_recv()
            add_to(self.slots.at[self.me.z], self.came.at[k])


def ffn_kernel(
    x, branch, cot, wg, wu, wd, e_out, o_out, gg, gu, gd, gain, X, N, C, Wg, Wu, Wd, H, DG, DU, O, E, R, G, S, n_send, n_recv, x_send, x_recv, e_send, e_recv, local,
):
    me = Place()
    tokens = x.shape[0]
    chip = 2 * tokens
    twin = me.plane(0, 0, 1)[0]
    ids = [me.column(dz, 0)[0] for dz in range(1, DEPTH)] + [twin]
    barrier = greet(ids)
    loads = [
        pltpu.make_async_copy(src, dst, local.at[i])
        for i, (src, dst) in enumerate(((wg, Wg), (wu, Wu), (wd, Wd), (cot, C)))
    ]
    own_rows = pl.ds(pl.multiple_of(me.q * tokens, tokens), tokens)
    mine = [pltpu.make_async_copy(src, X.at[i], local.at[(4, 11)[i]]) for i, src in enumerate((x, branch))]
    for load in mine:
        load.start()

    def rows_of(z, c):
        return pl.ds(pl.multiple_of((z * 2 + c) * tokens, tokens), tokens)

    def remote(src, dst, send, recv, device):
        return pltpu.make_async_remote_copy(
            src_ref=src,
            dst_ref=dst,
            send_sem=send,
            recv_sem=recv,
            device_id=device,
            device_id_type=MESH,
        )

    def column_id(z):
        return me.at(z, me.x, me.y, me.c)

    odd = lax.rem(me.z, 2)
    order = [me.z, 1 + odd, lax.rem(me.z + 2, DEPTH), 3 * (1 - odd)]
    net = Net(n_send, n_recv, local)
    chain = Chain(me, net, lambda z, c: N.at[rows_of(z, c)], twin)

    def twin_has(i):
        chain.twin_has(order[i])

    tile = 512

    def rows_at(i):
        return pl.ds(pl.multiple_of(order[i] * chip, chip), chip)

    def hidden(i):
        twin_has(i)
        rows = rows_at(i)

        def body(t, carry):
            cols = pl.ds(pl.multiple_of(t * tile, tile), tile)
            gate = dot(N[rows, :], Wg[:, cols])
            raised = dot(N[rows, :], Wu[:, cols])
            d_hidden = dot(C[rows, :], Wd[:, cols])
            sig = jax.nn.sigmoid(gate)
            act = gate * sig
            H[rows, cols] = (act * raised).astype(BF16)
            DU[rows, cols] = (d_hidden * act).astype(BF16)
            DG[rows, cols] = (d_hidden * raised * sig * (1.0 + gate * (1.0 - sig))).astype(BF16)
            return carry

        lax.fori_loop(0, H.shape[1] // tile, body, 0)

    def products(i):
        rows = rows_at(i)

        def body(t, carry):
            cols = pl.ds(pl.multiple_of(t * tile, tile), tile)
            e = dot(DG[rows, :], Wg[cols, :], NT) + dot(DU[rows, :], Wu[cols, :], NT)
            E[rows, cols] = e.astype(BF16)
            piece = jnp.sum((e * N[rows, cols].astype(F32)).reshape(chip // 8, 8, tile), axis=0)
            if i == 0:
                S[:, cols] = piece
            else:
                S[:, cols] += piece
            O[rows, cols] = dot(H[rows, :], Wd[cols, :], NT).astype(BF16)
            return carry

        lax.fori_loop(0, E.shape[1] // tile, body, 0)
        swap(i)

    swaps, sums = [], []

    def swap(i):
        o = order[i]
        copy = remote(E.at[rows_of(o, 1 - me.c)], R.at[i], x_send.at[i], x_recv.at[i], twin)
        copy.start()
        swaps.append(copy)

    def total(i):
        o = order[i]
        swaps[i].wait_recv()
        first = (o * 2 + me.c) * tokens

        def body(k, carry):
            at = pl.ds(pl.multiple_of(k * 16, 16), 16)
            to = pl.ds(pl.multiple_of(first + k * 16, 16), 16)
            E[to, :] = (E[to, :].astype(F32) + R[i, at, :].astype(F32)).astype(BF16)
            return carry

        lax.fori_loop(0, tokens // 16, body, 0)
        rows = rows_of(o, me.c)
        if i == 0:
            copy = pltpu.make_async_copy(E.at[rows], e_out.at[me.z], local.at[5])
        else:
            copy = remote(E.at[rows], e_out.at[me.z], e_send.at[i], e_recv.at[me.z], column_id(o))
        copy.start()
        sums.append(copy)

    for load in mine:
        load.wait()

    def normalize(i, carry):
        at = pl.ds(pl.multiple_of(i * 16, 16), 16)
        v = X[0, at, :].astype(F32) + X[1, at, :].astype(F32)
        v = v * lax.rsqrt(jnp.mean(v * v, axis=-1, keepdims=True) + EPS)
        N[pl.ds(pl.multiple_of(me.q * tokens + i * 16, 16), 16), :] = v.astype(BF16)
        return carry

    lax.fori_loop(0, tokens // 16, normalize, 0)
    for load in loads:
        load.start()
    pl.semaphore_wait(barrier, 4)
    chain.start()
    for load in loads:
        load.wait()
    chain.take_in(1)
    hidden(0)
    products(0)
    chain.pass_on(1)
    chain.pass_on(2)
    hidden(1)
    chain.take_in(2)
    products(1)
    total(0)
    chain.pass_on(3)
    total(1)
    hidden(2)
    chain.take_in(3)
    products(2)
    total(2)
    hidden(3)
    products(3)
    total(3)
    stores = [
        pltpu.make_async_copy(O, o_out, local.at[6]),
        pltpu.make_async_copy(S, gain, local.at[7]),
    ]
    for store in stores:
        store.start()

    span = 256

    def grad_tile(t, carry):
        rows = pl.ds(pl.multiple_of(t * span, span), span)
        n, c = N[:, rows], C[:, rows]
        G[0, rows, :] = dot(n, DG[...], TN).astype(BF16)
        G[1, rows, :] = dot(n, DU[...], TN).astype(BF16)
        G[2, rows, :] = dot(c, H[...], TN).astype(BF16)
        return carry

    lax.fori_loop(0, G.shape[1] // span, grad_tile, 0)
    for i, dst in enumerate((gg, gu, gd)):
        store = pltpu.make_async_copy(G.at[i], dst, local.at[8 + i])
        store.start()
        stores.append(store)
    for i in range(1, DEPTH):
        o = order[i]
        remote(E.at[own_rows], e_out.at[o], e_send.at[i], e_recv.at[o], twin).wait_recv()
    sums[0].wait()
    for copy in sums[1:] + swaps:
        copy.wait_send()
    net.finish()
    for store in stores:
        store.wait()


def back_kernel(
    x, branch, cot, e_parts, part_o, gg, gu, gd, gain_f, u, r, pw, att, t, wq, wo,
    d_mid, out_o, out_e, og, ou, od, oq, oo, ov,
    DM, D, U, R, P, A, T, Wq, Wo, dA, dR, E, GQ, GO, gains, out, out_swap, out_came, e_swap, e_came,
    own, side, came, q_up, q_down, o_up, o_down, v_up, v_down, send, recv, local,
):
    me = Place()
    net = Net(send, recv, local)
    tokens = x.shape[0]
    raw = [net.keep(src, E.at[pl.ds(k * tokens, tokens)]) for k, src in enumerate((x, branch, cot))]
    raw += [net.keep(e_parts.at[k], E.at[pl.ds((3 + k) * tokens, tokens)]) for k in range(DEPTH)]
    back, there, away = swap_owner(me)
    barrier = greet(plane_ids(me) + column_ids(me))

    @pl.when(away)
    def _():
        pl.semaphore_signal(barrier, inc=1, device_id=there, device_id_type=MESH)
        pl.semaphore_signal(barrier, inc=1, device_id=back, device_id_type=MESH)

    pl.semaphore_wait(barrier, jnp.where(away, 15, 13))
    twin = me.plane(0, 0, 1)[0]
    x_next, px = me.plane(1, 0, 0)
    y_next, py = me.plane(0, 1, 0)
    pd = me.plane(1, 1, 0)[1]

    def slab(p):
        return pl.ds(pl.multiple_of(p * tokens, tokens), tokens)

    def quarter(grad, p, z):
        return grad.at[pl.ds(z * 8 + p - me.c, 2)]

    grads = {"d": (0, gd, od), "g": (1, gg, og), "u": (2, gu, ou)}
    begun, passed, late, kept = {}, {}, [], []
    hand_send = hand_recv = net.take(24)

    def first(n):
        g, grad, _ = grads[n]
        for z in range(DEPTH):
            half = z // 2
            device, near, far = (y_next, py, px) if half else (x_next, px, py)
            at = pl.ds(z % 2 * 2, 2)
            begun[n, z] = [
                net.put(quarter(grad, near, z), came.at[g * 6 + half * 3, at], device),
                net.put(quarter(grad, pd, z), came.at[g * 6 + half * 3 + 1, at], device),
            ], [
                net.keep(quarter(grad, me.p, z), own.at[g * 2 + half, at]),
                net.keep(quarter(grad, far, z), side.at[g * 2 + half, at]),
            ]

    def second(n, half):
        g = grads[n][0]
        for z in (half * 2, half * 2 + 1):
            got, mine = begun[n, z]
            for copy in got:
                copy.wait_recv()
            for copy in mine:
                copy.wait()
        add_to(side.at[g * 2 + half], came.at[g * 6 + half * 3 + 1])
        device = x_next if half else y_next
        passed[n, half] = net.put(side.at[g * 2 + half], came.at[g * 6 + half * 3 + 2], device)
        add_to(own.at[g * 2 + half], came.at[g * 6 + half * 3])

    def third(n, half):
        g, _, result = grads[n]
        cols = pl.ds(pl.multiple_of(me.q * 1024, 1024), 1024)
        passed[n, half].wait_recv()
        add_to(own.at[g * 2 + half], came.at[g * 6 + half * 3 + 2])
        for z in (half * 2, half * 2 + 1):
            for c in (0, 1):
                src, dst = own.at[g * 2 + half, z % 2 * 2 + c], result.at[:, cols]
                mine = jnp.logical_and(me.z == z, me.c == c)
                k = hand_send + g * 8 + z * 2 + c
                copy = net.copy(src, dst, k, hand_recv + g * 8 + me.q, me.at(z, me.x, me.y, c))
                net.put_if(jnp.logical_not(mine), copy)
                here = pltpu.make_async_copy(src, dst, local.at[local.shape[0] - 2 - g])
                pl.when(mine)(here.start)
                late.append((mine, here))

    for copy in raw:
        copy.wait()

    def normed_back(i, carry):
        def part(k):
            return E[pl.ds(pl.multiple_of(k * tokens + i * 16, 16), 16), :].astype(F32)

        v = part(0) + part(1)
        inverse = lax.rsqrt(jnp.mean(v * v, axis=-1, keepdims=True) + EPS)
        unit = v * inverse
        e = part(3) + part(4) + part(5) + part(6)
        d = part(2) + inverse * (e - unit * jnp.mean(e * unit, axis=-1, keepdims=True))
        DM[pl.ds(pl.multiple_of(i * 16, 16), 16), :] = d
        D[pl.ds(pl.multiple_of(me.p * tokens + i * 16, 16), 16), :] = d.astype(BF16)
        return carry

    lax.fori_loop(0, tokens // 16, normed_back, 0)
    kept.append(net.keep(DM, d_mid))
    d_gather = PlaneGather(me, net, lambda p: D.at[slab(p)])
    loads = {}
    for name, src, dst in (
        ("att", att, A), ("wo", wo, Wo), ("r", r, R), ("pw", pw, P), ("t", t, T), ("u", u, U), ("wq", wq, Wq),
    ):
        loads[name] = [net.keep(src, dst)]
    loads["gain"] = [
        net.keep(gain_f.at[:, pl.ds(z * 512, 512)], gains.at[z, 1]) for z in range(DEPTH)
    ]

    def need(*names):
        for name in names:
            for copy in loads.pop(name, ()):
                copy.wait()

    out_in = []

    def out_swaps():
        for z in range(DEPTH):
            other, mine = slab(z * 2 + 1 - me.c), slab(z * 2 + me.c)
            out_in.append((net.put(part_o.at[other], out_swap.at[z], twin), net.keep(part_o.at[mine], out.at[z])))

    def out_add():
        for z in range(DEPTH):
            got, mine = out_in[z]
            got.wait_recv()
            mine.wait()
            add_to(out.at[z], out_swap.at[z])

    out_sum = ColumnSum(me, net, out, out_came)

    def out_finish():
        out_sum.finish()
        kept.append(net.keep(out.at[me.z], out_o))

    block = 2 * tokens
    length = 4 * tokens
    lead = GROUP * HEAD_DIM
    scale = HEAD_DIM ** (-0.5)

    def d_attended():
        need("wo")

        def body(i, carry):
            rows = pl.ds(pl.multiple_of(i * block, block), block)
            dA[rows, :] = dot(D[rows, :], Wo[...].reshape(Wo.shape[0] * Wo.shape[1], Wo.shape[2]), NT).astype(BF16)
            return carry

        lax.fori_loop(0, 8 * tokens // block, body, 0)

    def turn_back(v, rows):
        cosine, sine = rotations(T[rows, :])
        return (v * cosine - turn(v) * sine).astype(BF16)

    def attend_back(seq):
        need("r", "pw", "t")
        keys_at = pl.ds(seq * length, length)
        keys = R[keys_at, lead : lead + HEAD_DIM]
        values = R[keys_at, lead + HEAD_DIM :]
        d_keys = jnp.zeros((length, HEAD_DIM), F32)
        d_values = jnp.zeros((length, HEAD_DIM), F32)
        for h in range(GROUP):
            cols = slice(h * HEAD_DIM, (h + 1) * HEAD_DIM)
            for part in range(2):
                rows = pl.ds(seq * length + part * (length // 2), length // 2)
                low = P[h, rows, :]
                weights = low.astype(F32)
                d_out = dA[rows, cols]
                d_weights = dot(d_out, values, NT)
                d_scores = (
                    weights * (d_weights - jnp.sum(weights * d_weights, axis=-1, keepdims=True))
                ).astype(BF16)
                dR[rows, cols] = turn_back(dot(d_scores, keys) * scale, rows)
                d_keys += dot(d_scores, R[rows, cols], TN)
                d_values += dot(low, d_out, TN)
        dR[keys_at, lead : lead + HEAD_DIM] = turn_back(d_keys * scale, keys_at)
        dR[keys_at, lead + HEAD_DIM :] = d_values.astype(BF16)

    tile = 512

    def e_product():
        need("u", "wq", "gain")

        def body(k, carry):
            i, j = lax.div(k, E.shape[1] // tile), lax.rem(k, E.shape[1] // tile)
            rows = pl.ds(pl.multiple_of(i * block, block), block)
            cols = pl.ds(pl.multiple_of(j * tile, tile), tile)
            slots = pl.ds(j * (tile // Wq.shape[1]), tile // Wq.shape[1])
            e = dot(dR[rows, :], Wq[slots].reshape(tile, Wq.shape[2]), NT)
            E[rows, cols] = e.astype(BF16)
            piece = jnp.sum((e * U[rows, cols].astype(F32)).reshape(block // 8, 8, tile), axis=0)
            gains[j, 0] = jnp.where(i == 0, 0.0, gains[j, 0]) + piece
            return carry

        lax.fori_loop(0, 8 * tokens // block * (E.shape[1] // tile), body, 0)

    e_sum = PlaneSum(me, net, lambda p: E.at[slab(p)], e_swap, e_came)
    span = 256

    def q_product():
        need("u")

        def body(k, carry):
            cols = pl.ds(pl.multiple_of(k * span, span), span)
            per = span // GQ.shape[2]
            g = dot(U[:, cols], dR[...], TN).astype(BF16)
            at = pl.ds(lax.rem(k, PLANE // per) * per, per)
            GQ[lax.div(k, PLANE // per), at] = g.reshape(per, GQ.shape[2], GQ.shape[3])
            return carry

        lax.fori_loop(0, U.shape[1] // span, body, 0)

    def o_product():
        need("att")

        def body(k, carry):
            cols = pl.ds(pl.multiple_of(k * tile, tile), tile)
            g = dot(A[...], D[:, cols], TN).astype(BF16)
            GO[:, 0, :, cols] = g.reshape(GO.shape[0], GO.shape[2], tile)
            return carry

        lax.fori_loop(0, D.shape[1] // tile, body, 0)

    def add_all(into, more):
        into[...] = into[...] + more[...]

    q_sum = ChainSum(me, net, GQ, q_up, q_down)
    o_sum = ChainSum(me, net, GO, o_up, o_down)
    v_sum = ChainSum(me, net, gains, v_up, v_down, add_all)

    def q_begin(hops):
        q_sum.begin(hops)
        v_sum.begin(hops)

    def q_near(hops):
        q_sum.near(hops)
        v_sum.near(hops)

    def q_far():
        q_sum.far()
        v_sum.far()

    def q_finish():
        q_sum.finish()
        v_sum.finish()

    k = net.take(1)
    swap = net.copy(GO.at[me.z, 0], oo, k, k, there)
    stay = pltpu.make_async_copy(GO.at[me.z, 0], oo, local.at[local.shape[0] - 1])
    stays = jnp.logical_not(away)
    owned = []

    def to_owners():
        pl.when(away)(swap.start)
        pl.when(stays)(stay.start)
        for dx in (0, 1):
            for dy in (0, 1):
                for dc in (0, 1):
                    device, p = me.plane(dx, dy, dc)
                    lanes = pl.ds(pl.multiple_of(lax.div(p, 2) * 128, 128), 128)
                    for src, dst in ((GQ.at[me.z, p], oq.at[me.p]), (gains.at[me.z, :, :, lanes], ov.at[me.p])):
                        if dx + dy + dc:
                            owned.append(net.put(src, dst, device))
                        else:
                            kept.append(net.keep(src, dst))

    def e_finish():
        kept.append(e_sum.finish(out_e))

    out_swaps()
    d_gather.start()
    out_add()
    out_sum.start()
    first("g")
    d_gather.relay()
    second("g", 0)
    d_gather.finish()
    second("g", 1)
    o_product()
    o_sum.begin(3)
    first("d")
    o_sum.near(2)
    third("g", 0)
    d_attended()
    o_sum.begin(2)
    attend_back(0)
    third("g", 1)
    o_sum.far()
    attend_back(1)
    o_sum.near(1)
    q_product()
    first("u")
    e_product()
    q_begin(3)
    second("d", 1)
    e_sum.start()
    q_near(2)
    second("d", 0)
    q_begin(2)
    out_finish()
    e_sum.cores()
    q_near(1)
    q_begin(1)
    q_far()
    third("d", 1)
    third("d", 0)
    o_sum.begin(1)
    second("u", 0)
    second("u", 1)
    q_finish()
    third("u", 1)
    third("u", 0)
    o_sum.finish()
    e_sum.chips()
    e_finish()
    to_owners()
    for n in "dgu":
        g, _, result = grads[n]
        for dz in range(DEPTH):
            for dc in (0, 1):
                if dz + dc:
                    _, z, c = me.column(dz, dc)
                    cols = pl.ds(pl.multiple_of((z * 2 + c) * 1024, 1024), 1024)
                    k = hand_recv + g * 8 + z * 2 + c
                    net.copy(own.at[g * 2, 0], result.at[:, cols], k, k, twin).wait_recv()
    for copy in owned:
        copy.wait_recv()
    for copy in kept:
        copy.wait()
    for mine, here in late:
        pl.when(mine)(here.wait)
    net.finish()
    pl.when(away)(swap.wait)
    pl.when(stays)(stay.wait)


def final_kernel(
    og, ou, od, oq, oo, o_sum, e_sum, d_mid, x, branch, gain,
    layer, input_grad, g_gate, g_up, g_down, g_qkv, g_out,
    v_og, v_ou, v_od, v_oq, v_oo, v_o, v_e, v_d, v_x, v_b, v_gain, f_gate, f_up, f_down, f_qkv, f_out, f_layer, f_input, sem,
):
    pairs = (
        (gain, v_gain), (og, v_og), (ou, v_ou), (od, v_od), (oq, v_oq), (oo, v_oo),
        (x, v_x), (branch, v_b), (o_sum, v_o), (e_sum, v_e), (d_mid, v_d),
    )
    loads = [pltpu.make_async_copy(src, dst, sem.at[i]) for i, (src, dst) in enumerate(pairs)]
    for load in loads:
        load.start()
    loads[0].wait()
    stores = []

    def store(src, dst):
        copy = pltpu.make_async_copy(src, dst, sem.at[len(pairs) + len(stores)])
        copy.start()
        stores.append(copy)

    def columns(src, dst, by):
        def body(i, carry):
            cols = pl.ds(pl.multiple_of(i * 1024, 1024), 1024)
            v = src[:, cols].astype(F32)
            dst[:, cols] = v if by is None else v * by
            return carry

        lax.fori_loop(0, src.shape[1] // 1024, body, 0)

    for i, (src, dst, out, by) in enumerate(
        ((v_og, f_gate, g_gate, gain), (v_ou, f_up, g_up, gain), (v_od, f_down, g_down, None))
    ):
        loads[1 + i].wait()
        columns(src, dst, None if by is None else v_gain[1, :, 0:1])
        store(dst, out)
    loads[4].wait()
    by = v_gain[0, :, 0:1]
    lead = GROUP * HEAD_DIM
    for p in range(KV_HEADS):
        parts = (p * lead, lead), (HEADS * HEAD_DIM + p * HEAD_DIM, HEAD_DIM), ((HEADS + KV_HEADS + p) * HEAD_DIM, HEAD_DIM)
        at = 0
        for first, size in parts:
            f_qkv[:, first : first + size] = v_oq[p, :, at : at + size].astype(F32) * by
            at += size
    store(f_qkv, g_qkv)
    loads[5].wait()
    columns(v_oo, f_out, None)
    store(f_out, g_out)
    for load in loads[6:]:
        load.wait()

    def tokens_back(i, carry):
        at = pl.ds(pl.multiple_of(i * 16, 16), 16)
        v = v_x[at, :].astype(F32)
        f_layer[at, :] = (v + v_b[at, :].astype(F32) + v_o[at, :].astype(F32)).astype(BF16)
        inverse = lax.rsqrt(jnp.mean(v * v, axis=-1, keepdims=True) + EPS)
        unit = v * inverse
        e = v_e[at, :].astype(F32)
        f_input[at, :] = v_d[at, :] + inverse * (e - unit * jnp.mean(e * unit, axis=-1, keepdims=True))
        return carry

    lax.fori_loop(0, f_layer.shape[0] // 16, tokens_back, 0)
    store(f_layer, layer)
    store(f_input, input_grad)
    for copy in stores:
        copy.wait()


def shape(*dims, dtype=BF16):
    return jax.ShapeDtypeStruct(dims, dtype)


def shards(copies, block_input, positions, cotangent, norm_attn, w_qkv, w_out, norm_ffn, w_gate, w_up, w_down):
    tokens, width = block_input.shape
    ff = w_gate.shape[1]
    q_cols, kv_cols = HEADS * HEAD_DIM, KV_HEADS * HEAD_DIM
    spread = ("rep", "fsdp")
    place = lax.rem(lax.axis_index("rep"), PLANE) * 4 + lax.axis_index("fsdp")

    def take(w):
        if copies == 1:
            return w
        rows = w.shape[0] * copies
        whole = lax.all_gather(w, spread, axis=0, tiled=True)
        return lax.dynamic_slice_in_dim(whole, place * rows, rows, axis=0)

    def give(grad):
        if copies == 1:
            return grad
        rows = grad.shape[0]
        whole = jnp.zeros((rows * 32,) + grad.shape[1:], grad.dtype)
        whole = lax.dynamic_update_slice_in_dim(whole, grad, place * rows, axis=0)
        return lax.psum_scatter(whole, spread, scatter_dimension=0, tiled=True)

    gain_a = take(norm_attn).astype(F32)
    gain_f = take(norm_ffn).astype(F32)
    rows = gain_a.shape[0]
    gains = jnp.broadcast_to(jnp.stack([gain_a, gain_f])[:, :, None], (2, rows, 128))
    own_qkv, own_gate, own_up = take(w_qkv), take(w_gate), take(w_up)
    own_down = take(w_down)
    own_out = take(w_out)
    head_cols = (GROUP + 2) * HEAD_DIM
    ff_cols = ff // 8
    full = 8 * tokens
    places = jnp.broadcast_to(positions[None, :], (8, tokens))
    sums, U, R, Pw, A, T, Wq, Wo, cg, Wg, Wu, Wd = call(
        front_kernel,
        0,
        [
            shape(tokens, width),
            shape(full, width),
            shape(full, head_cols),
            shape(GROUP, full, full // 2),
            shape(full, GROUP * HEAD_DIM),
            shape(full, HEAD_DIM, dtype=F32),
            shape(32, rows, head_cols),
            shape(4, rows, width),
            shape(8, tokens, width),
            shape(32, rows, ff_cols),
            shape(32, rows, ff_cols),
            shape(32, rows, ff_cols),
        ],
        (
            block_input,
            places,
            gains,
            cotangent,
            own_qkv,
            own_out,
            own_gate,
            own_up,
            own_down,
        ),
        150,
        36,
        [
            pltpu.VMEM((tokens, width), BF16),
            pltpu.VMEM((8, tokens), jnp.int32),
            pltpu.VMEM((2, rows, 128), F32),
            pltpu.VMEM((8, tokens), F32),
            pltpu.VMEM((rows, q_cols + 2 * kv_cols), BF16),
            pltpu.VMEM((8, rows, head_cols), BF16),
            pltpu.VMEM((rows, ff), BF16),
            pltpu.VMEM((rows, ff), BF16),
            pltpu.VMEM((full, width), BF16),
            pltpu.VMEM((full, HEAD_DIM), F32),
            pltpu.VMEM((2, 8, full // 2), F32),
            pltpu.VMEM((32, rows, head_cols), BF16),
            pltpu.VMEM((4, rows, width), BF16),
            pltpu.VMEM((full, head_cols), BF16),
            pltpu.VMEM((GROUP, full, full // 2), BF16),
            pltpu.VMEM((full, GROUP * HEAD_DIM), BF16),
            pltpu.VMEM((full, width), BF16),
            pltpu.VMEM((4, tokens, width), BF16),
            pltpu.VMEM((6, tokens // 2, width), BF16),
        ],
    )
    cg = cg.reshape(full, width)
    Wg, Wu, Wd = [w.reshape(width, ff_cols) for w in (Wg, Wu, Wd)]

    e_sums, out_part, g_gate, g_up, g_down, gain_f_part = pl.pallas_call(
        ffn_kernel,
        out_shape=[
            shape(4, tokens, width),
            shape(full, width),
            shape(width, ff_cols),
            shape(width, ff_cols),
            shape(width, ff_cols),
            shape(8, width, dtype=F32),
        ],
        in_specs=[ANY] * 6,
        out_specs=[ANY] * 6,
        scratch_shapes=[pltpu.VMEM((2, tokens, width), BF16)]
        + [pltpu.VMEM((full, width), BF16)] * 2
        + [pltpu.VMEM((width, ff_cols), BF16)] * 3
        + [pltpu.VMEM((full, ff_cols), BF16)] * 3
        + [pltpu.VMEM((full, width), BF16)] * 2
        + [
            pltpu.VMEM((4, tokens, width), BF16),
            pltpu.VMEM((3, width, ff_cols), BF16),
            pltpu.VMEM((8, width), F32),
        ]
        + [pltpu.SemaphoreType.DMA((12,))] * 6
        + [pltpu.SemaphoreType.DMA((12,))],
        compiler_params=pltpu.CompilerParams(
            collective_id=2, has_side_effects=True, vmem_limit_bytes=60 * 1024 * 1024
        ),
    )(block_input, sums, cg, Wg, Wu, Wd)
    g_gate, g_up, g_down = [g.reshape(32, rows, ff_cols) for g in (g_gate, g_up, g_down)]
    d_mid, out_sums, ea_sums, og, ou, od, oq, oo, ov = call(
        back_kernel,
        3,
        [shape(tokens, width, dtype=F32)]
        + [shape(tokens, width)] * 2
        + [shape(rows, ff)] * 3
        + [
            shape(8, rows, head_cols),
            shape(rows, width),
            shape(8, 2, 8, 128, dtype=F32),
        ],
        (block_input, sums, cotangent, e_sums, out_part, g_gate, g_up, g_down, gain_f_part, U, R, Pw, A, T, Wq, Wo),
        140,
        90,
        [
            pltpu.VMEM((tokens, width), F32),
            pltpu.VMEM((full, width), BF16),
            pltpu.VMEM((full, width), BF16),
            pltpu.VMEM((full, head_cols), BF16),
            pltpu.VMEM((GROUP, full, full // 2), BF16),
            pltpu.VMEM((full, GROUP * HEAD_DIM), BF16),
            pltpu.VMEM((full, HEAD_DIM), F32),
            pltpu.VMEM((32, rows, head_cols), BF16),
            pltpu.VMEM((4, rows, width), BF16),
            pltpu.VMEM((full, GROUP * HEAD_DIM), BF16),
            pltpu.VMEM((full, head_cols), BF16),
            pltpu.VMEM((full, width), BF16),
            pltpu.VMEM((4, PLANE, rows, head_cols), BF16),
            pltpu.VMEM((4, 1, rows, width), BF16),
            pltpu.VMEM((4, 2, 8, width // 4), F32),
            pltpu.VMEM((4, tokens, width), BF16),
            pltpu.VMEM((4, tokens, width), BF16),
            pltpu.VMEM((3, tokens, width), BF16),
            pltpu.VMEM((4, tokens, width), BF16),
            pltpu.VMEM((6, tokens // 2, width), BF16),
            pltpu.VMEM((6, 4, rows, ff_cols), BF16),
            pltpu.VMEM((6, 4, rows, ff_cols), BF16),
            pltpu.VMEM((18, 4, rows, ff_cols), BF16),
        ]
        + [pltpu.VMEM((3, PLANE, rows, head_cols), BF16)] * 2
        + [pltpu.VMEM((3, 1, rows, width), BF16)] * 2
        + [pltpu.VMEM((3, 2, 8, width // 4), F32)] * 2,
    )
    layer_output, input_gradient, g_gate, g_up, g_down, g_qkv, g_out = pl.pallas_call(
        final_kernel,
        out_shape=[
            shape(tokens, width),
            shape(tokens, width, dtype=F32),
            shape(rows, ff, dtype=F32),
            shape(rows, ff, dtype=F32),
            shape(rows, ff, dtype=F32),
            shape(rows, q_cols + 2 * kv_cols, dtype=F32),
            shape(rows, width, dtype=F32),
        ],
        in_specs=[ANY] * 11,
        out_specs=[ANY] * 7,
        scratch_shapes=[pltpu.VMEM((rows, ff), BF16)] * 3
        + [pltpu.VMEM((8, rows, head_cols), BF16), pltpu.VMEM((rows, width), BF16)]
        + [pltpu.VMEM((tokens, width), BF16)] * 2
        + [pltpu.VMEM((tokens, width), F32)]
        + [pltpu.VMEM((tokens, width), BF16)] * 2
        + [pltpu.VMEM((2, rows, 128), F32)]
        + [pltpu.VMEM((rows, ff), F32)] * 3
        + [
            pltpu.VMEM((rows, q_cols + 2 * kv_cols), F32),
            pltpu.VMEM((rows, width), F32),
            pltpu.VMEM((tokens, width), BF16),
            pltpu.VMEM((tokens, width), F32),
            pltpu.SemaphoreType.DMA((18,)),
        ],
        compiler_params=pltpu.CompilerParams(vmem_limit_bytes=60 * 1024 * 1024),
    )(og, ou, od, oq, oo, out_sums, ea_sums, d_mid, block_input, sums, gains)
    gain_sums = jnp.sum(ov, axis=(0, 2))
    gain_sums = lax.dynamic_slice_in_dim(gain_sums, place % 2 * rows, rows, axis=1)
    return (
        layer_output,
        input_gradient,
        give(gain_sums[0] / gain_a),
        give(g_qkv),
        give(g_out),
        give(gain_sums[1] / gain_f),
        give(g_gate),
        give(g_up),
        give(g_down),
    )


def solution(mesh):
    copies = mesh.shape["rep"] * mesh.shape["fsdp"] // 32
    rows, flat = P(("rep", "fsdp"), None), P(("rep", "fsdp"))
    return jax.shard_map(
        functools.partial(shards, copies),
        mesh=mesh,
        in_specs=(rows, flat, rows, flat, rows, rows, flat, rows, rows, rows),
        out_specs=(rows, rows, flat, rows, rows, flat, rows, rows, rows),
        check_vma=False,
    )
```

```python
import functools
import math

import jax
import jax.numpy as jnp
from jax import lax
from jax.experimental import pallas as pl
from jax.experimental.pallas import tpu as pltpu
from jax.sharding import PartitionSpec as P

HEADS = 16
KV_HEADS = 8
HEAD_DIM = 128
BLOCK = 256
MOST_BLOCKS = 2
GROUP = HEADS // KV_HEADS
EPS = 1e-05
THETA = 1000000.0
MESH = pl.DeviceIdType.MESH
F32 = jnp.float32
BF16 = jnp.bfloat16

PLANE = 8
DEPTH = 4
FLIPS = [(1, 0), (0, 1), (1, 1)]


def dot(a, b, dims=((1,), (0,))):
    return lax.dot_general(a, b, (dims, ((), ())), preferred_element_type=F32)


NT = ((1,), (1,))
TN = ((0,), (0,))


def flip(bit, by):
    return lax.rem(bit + by, 2)


class Place:
    def __init__(self):
        rep, self.f = lax.axis_index("rep"), lax.axis_index("fsdp")
        self.r = lax.rem(rep, PLANE)
        self.base = rep - self.r
        self.z, self.x = lax.div(self.r, 2), lax.rem(self.r, 2)
        self.y, self.c = lax.div(self.f, 2), lax.rem(self.f, 2)
        self.p = self.x * 4 + self.f
        self.q = self.z * 2 + self.c
        self.d = self.r * 4 + self.f

    def at(self, z, x, y, c):
        return (self.base + z * 2 + x, y * 2 + c)

    def plane(self, dx, dy, dc):
        x, y, c = flip(self.x, dx), flip(self.y, dy), flip(self.c, dc)
        return self.at(self.z, x, y, c), x * 4 + y * 2 + c

    def column(self, dz, dc):
        z, c = lax.rem(self.z + dz, DEPTH), flip(self.c, dc)
        return self.at(z, self.x, self.y, c), z, c

    def behind(self, dz):
        return lax.rem(self.z + (DEPTH - dz), DEPTH)


class Net:
    def __init__(self, send, recv, local):
        self.send, self.recv, self.local_sem = send, recv, local
        self.used = 0
        self.sent, self.kept = [], []

    def take(self, count):
        self.used += count
        return self.used - count

    def copy(self, src, dst, send, recv, device):
        return pltpu.make_async_remote_copy(
            src_ref=src,
            dst_ref=dst,
            send_sem=self.send.at[send],
            recv_sem=self.recv.at[recv],
            device_id=device,
            device_id_type=MESH,
        )

    def put(self, src, dst, device):
        k = self.take(1)
        copy = self.copy(src, dst, k, k, device)
        copy.start()
        self.sent.append((None, copy))
        return copy

    def put_if(self, when, copy):
        pl.when(when)(copy.start)
        self.sent.append((when, copy))
        return copy

    def keep(self, src, dst):
        copy = pltpu.make_async_copy(src, dst, self.local_sem.at[len(self.kept)])
        copy.start()
        self.kept.append(copy)
        return copy

    def finish(self):
        for when, copy in self.sent:
            if when is None:
                copy.wait_send()
            else:
                pl.when(when)(copy.wait_send)


class Chain:
    def __init__(self, me, net, slot, twins=None):
        self.me, self.net, self.slot, self.twins = me, net, slot, twins
        self.base = net.take(12)
        last = DEPTH - 1
        self.first, self.last = me.z == 0, me.z == last
        self.inner = jnp.logical_and(me.z > 0, me.z < last)
        self.order = [
            me.z,
            1 + lax.rem(me.z, 2),
            jnp.where(self.inner, last * (me.z - 1), 2 - lax.div(me.z, last)),
            last * (1 - lax.div(me.z, 2)),
        ]
        self.steps = [None] + [self.arrival(i) for i in range(1, DEPTH)]

    def pass_on(self, i):
        self.steps[i][0]()

    def take_in(self, i):
        self.steps[i][1]()

    def link(self, z, k, target):
        me = self.me
        ref = self.slot(z, me.c)
        return self.net.copy(ref, ref, self.base + k, self.base + z, me.at(target, me.x, me.y, me.c))

    def start(self):
        me, net = self.me, self.net
        net.put_if(jnp.logical_not(self.last), self.link(me.z, 0, me.z + 1))
        net.put_if(jnp.logical_not(self.first), self.link(me.z, 1, me.z - 1))
        if self.twins is not None:
            self.twin(me.z, 0)

    def twin(self, z, k):
        ref, net = self.slot(z, self.me.c), self.net
        copy = net.copy(ref, ref, self.base + 8 + k, self.base + 4 + z, self.twins)
        copy.start()
        net.sent.append((None, copy))

    def arrival(self, i):
        me, net = self.me, self.net
        z = self.order[i]
        onward = self.link(z, 1 + i, me.z + jnp.where(z < me.z, 1, -1))
        across = None
        net.sent.append((self.inner, onward))
        if self.twins is not None:
            ref = self.slot(z, me.c)
            across = net.copy(ref, ref, self.base + 8 + i, self.base + 4 + z, self.twins)
            net.sent.append((None, across))

        def take(passes):
            onward.wait_recv()
            if passes:
                onward.start()
            if across is not None:
                across.start()

        return (
            lambda: pl.when(self.inner)(lambda: take(True)),
            lambda: pl.when(jnp.logical_not(self.inner))(lambda: take(False)),
        )

    def twin_has(self, z):
        ref = self.slot(z, 1 - self.me.c)
        self.net.copy(ref, ref, self.base + 4, self.base + 4 + z, self.twins).wait_recv()

    def twin_all(self):
        for z in range(DEPTH):
            self.twin_has(z)


def greet(devices):
    barrier = pltpu.get_barrier_semaphore()
    for device in devices:
        pl.semaphore_signal(barrier, inc=1, device_id=device, device_id_type=MESH)
    return barrier


def plane_ids(me):
    return [
        me.plane(dx, dy, dc)[0] for dx in (0, 1) for dy in (0, 1) for dc in (0, 1) if dx + dy + dc
    ]


def column_ids(me):
    return [me.column(dz, dc)[0] for dz in range(1, DEPTH) for dc in (0, 1)]


def sems(sends, locals_):
    return [
        pltpu.SemaphoreType.DMA((sends,)),
        pltpu.SemaphoreType.DMA((sends,)),
        pltpu.SemaphoreType.DMA((locals_,)),
    ]


ANY = pl.BlockSpec(memory_space=pl.ANY)


def call(kernel, ident, outs, args, sends, locals_, scratch=()):
    return pl.pallas_call(
        kernel,
        out_shape=outs,
        in_specs=[ANY] * len(args),
        out_specs=[ANY] * len(outs),
        scratch_shapes=list(scratch) + sems(sends, locals_),
        compiler_params=pltpu.CompilerParams(
            collective_id=ident, has_side_effects=True, vmem_limit_bytes=60 * 1024 * 1024
        ),
    )(*args)


def head_of(p):
    return 2 * (p % 4) + p // 4


def head_columns(head):
    lead = GROUP * HEAD_DIM
    return (
        (head * lead, lead),
        (HEADS * HEAD_DIM + head * HEAD_DIM, HEAD_DIM),
        ((HEADS + KV_HEADS + head) * HEAD_DIM, HEAD_DIM),
    )


def column_of(row):
    return jnp.transpose(jnp.broadcast_to(row.astype(F32), (8, row.shape[1])))[:, 0:1]


def swap_owner(me):
    return me.at(me.f, me.x, lax.div(me.z, 2), lax.rem(me.z, 2)), me.f != me.z


def turn(v):
    return pltpu.roll(v, HEAD_DIM // 2, 1)


def rotations(table):
    swapped = turn(table)
    low = lax.broadcasted_iota(jnp.int32, table.shape, 1) < HEAD_DIM // 2
    return jnp.where(low, table, swapped), jnp.where(low, -swapped, table)


def attend(R, codes, P, A, seq, length):
    half = length // 2
    keys_at = pl.ds(seq * length, length)
    keys = R[keys_at, GROUP * HEAD_DIM : (GROUP + 1) * HEAD_DIM]
    values = R[keys_at, (GROUP + 1) * HEAD_DIM :]
    code = codes[seq, 0:1, :]
    for part in range(2):
        rows = pl.ds(seq * length + part * half, half)
        most = jnp.transpose(codes[seq, :, part * half : (part + 1) * half])[:, 0:1]
        least = jnp.floor(most * (1.0 / MOST_BLOCKS)) * MOST_BLOCKS
        allowed = (code <= most) & (code >= least)
        for h in range(GROUP):
            cols = slice(h * HEAD_DIM, (h + 1) * HEAD_DIM)
            scores = dot(R[rows, cols], keys, NT) * HEAD_DIM ** (-0.5)
            scores = jnp.where(allowed, scores, -1e30)
            exponent = jnp.exp(scores - jnp.max(scores, axis=-1, keepdims=True))
            weights = (exponent / jnp.sum(exponent, axis=-1, keepdims=True)).astype(BF16)
            P[h, rows, :] = weights
            A[rows, cols] = dot(weights, values).astype(BF16)


def front_kernel(
    x, pos, gain, cot, wq, wo, wg, wu, wd,
    sums, Uo, Ro, Po, Ao, To, Wqo, Woo, cg, Wg, Wu, Wd,
    X, places, gains, code, q_raw, q_own, g_own, u_own, U, T, codes, Wq, Wo, R, P, A, E, swapped, came, send, recv, local,
):
    me = Place()
    net = Net(send, recv, local)
    tokens = x.shape[0]
    there, away = swap_owner(me)
    barrier = greet(plane_ids(me) + column_ids(me))

    raw = [net.keep(src, dst) for src, dst in ((pos, places), (gain, gains), (x, X), (wq, q_raw), (wg, g_own), (wu, u_own))]

    @pl.when(away)
    def _():
        pl.semaphore_signal(barrier, inc=1, device_id=there, device_id_type=MESH)

    pl.semaphore_wait(barrier, jnp.where(away, 14, 13))
    twin = me.plane(0, 0, 1)[0]
    x_next, y_next = me.plane(1, 0, 0)[0], me.plane(0, 1, 0)[0]

    def slab(p):
        return pl.ds(pl.multiple_of(p * tokens, tokens), tokens)

    own_rows = slab(me.p)
    raw[1].wait()

    def normalize():
        raw[2].wait()

        def body(i, carry):
            at = pl.ds(pl.multiple_of(i * 16, 16), 16)
            v = X[at, :].astype(F32)
            v = v * lax.rsqrt(jnp.mean(v * v, axis=-1, keepdims=True) + EPS)
            U[pl.ds(pl.multiple_of(me.p * tokens + i * 16, 16), 16), :] = v.astype(BF16)
            return carry

        lax.fori_loop(0, tokens // 16, body, 0)

    def rotation_table():
        raw[0].wait()
        half = HEAD_DIM // 2
        place = jnp.broadcast_to(places[...], code.shape)
        column = jnp.transpose(place.astype(F32))[:, 0:1]
        index = lax.broadcasted_iota(jnp.int32, (1, half), 1).astype(F32)
        angles = column * jnp.exp(index * (-math.log(THETA) / half))
        T[own_rows, :] = jnp.concatenate([jnp.cos(angles), jnp.sin(angles)], axis=1)
        lane = lax.broadcasted_iota(jnp.int32, place.shape, 1)
        start = me.f * tokens + lane - place
        code[...] = (start * MOST_BLOCKS + lax.div(place, jnp.full_like(place, BLOCK))).astype(F32)

    def scale_q():
        raw[3].wait()
        by = column_of(gains[0:1, :])[: q_raw.shape[0]]
        for p in range(KV_HEADS):
            to = 0
            for first, size in head_columns(head_of(p)):
                q_own[p, :, to : to + size] = (q_raw[:, first : first + size].astype(F32) * by).astype(BF16)
                to += size

    def scale_f(k):
        raw[4 + k].wait()
        w = (g_own, u_own)[k]
        by = column_of(gains[1:2, :])[: w.shape[0]]

        def body(i, carry):
            cols = pl.ds(pl.multiple_of(i * 1024, 1024), 1024)
            w[:, cols] = (w[:, cols].astype(F32) * by).astype(BF16)
            return carry

        lax.fori_loop(0, w.shape[1] // 1024, body, 0)

    weights = {"g": (g_own, Wg), "u": (u_own, Wu), "d": (wd, Wd)}
    taken, sent, last = {}, {}, []

    def column(n, dz):
        w, W = weights[n]
        taken[n, dz] = []
        for dc in (0, 1):
            device, z, c = me.column(dz, dc)
            cols = pl.ds(pl.multiple_of((z * 2 + c) * 1024, 1024), 1024)
            if dz + dc:
                taken[n, dz].append(net.put(w.at[:, cols], W.at[me.d], device).wait_recv)
            else:
                taken[n, dz].append(net.keep(w.at[:, cols], W.at[me.d]).wait)

    def spread(n, dz):
        W = weights[n][1]
        for wait in taken[n, dz]:
            wait()
        rows = pl.ds(me.behind(dz) * 8 + me.p - me.c, 2)
        sent[n, dz] = [net.put(W.at[rows], W.at[rows], device) for device in (x_next, y_next)]

    def relay(n, dz):
        W = weights[n][1]
        by_x, by_y = sent[n, dz]
        first = me.behind(dz) * 8 - me.c
        if dz % 2:
            by_x.wait_recv()
            rows = pl.ds(first + me.plane(1, 0, 0)[1], 2)
            last.extend((net.put(W.at[rows], W.at[rows], y_next), by_y))
        else:
            by_y.wait_recv()
            rows = pl.ds(first + me.plane(0, 1, 0)[1], 2)
            last.extend((net.put(W.at[rows], W.at[rows], x_next), by_x))

    q_in = []

    def q_go():
        scale_q()
        for dx in (0, 1):
            for dy in (0, 1):
                for dc in (0, 1):
                    device, p = me.plane(dx, dy, dc)
                    if dx + dy + dc:
                        q_in.append(net.put(q_own.at[p], Wq.at[me.d], device))
                    else:
                        own = net.keep(q_own.at[p], Wq.at[me.d])
        q_in.append(own)

    q_chain = Chain(me, net, lambda z, c: Wq.at[pl.ds(z * PLANE, PLANE)])
    o_chain = Chain(me, net, lambda z, c: Wo.at[z])
    c_chain = Chain(me, net, lambda z, c: cg.at[z * 2 + c], twin)
    c_own = net.keep(cot, cg.at[me.q])

    def q_start():
        for copy in q_in[:-1]:
            copy.wait_recv()
        q_in[-1].wait()
        q_chain.start()

    k = net.take(1)
    swap = net.copy(wo, Wo.at[me.f], k, k, there)
    stay = pltpu.make_async_copy(wo, Wo.at[me.f], local.at[local.shape[0] - 1])
    stays = jnp.logical_not(away)

    def swap_go():
        pl.when(away)(swap.start)
        pl.when(stays)(stay.start)

    def o_start():
        pl.when(away)(swap.wait)
        pl.when(stays)(stay.wait)
        o_chain.start()

    def c_start():
        c_own.wait()
        c_chain.start()

    t_gather = PlaneGather(me, net, lambda p: T.at[slab(p)])
    x_gather = PlaneGather(me, net, lambda p: U.at[slab(p)])
    code_in = []

    def code_go():
        lanes = pl.ds(pl.multiple_of(lax.rem(me.p, 4) * tokens, tokens), tokens)
        at = codes.at[lax.div(me.p, 4), :, lanes]
        code_in.extend(net.put(code, at, device) for device in plane_ids(me))
        code_in.append(net.keep(code, at))

    block = 2 * tokens
    lead = GROUP * HEAD_DIM

    def project():
        def body(i, carry):
            rows = pl.ds(pl.multiple_of(i * block, block), block)
            q = dot(U[rows, :], Wq[...].reshape(Wq.shape[0] * Wq.shape[1], Wq.shape[2]))
            cosine, sine = rotations(T[rows, :])
            for h in range(GROUP + 1):
                v = q[:, h * HEAD_DIM : (h + 1) * HEAD_DIM]
                R[rows, h * HEAD_DIM : (h + 1) * HEAD_DIM] = (v * cosine + turn(v) * sine).astype(BF16)
            R[rows, lead + HEAD_DIM :] = q[:, lead + HEAD_DIM :].astype(BF16)
            return carry

        lax.fori_loop(0, 8 * tokens // block, body, 0)

    def attention(seq):
        if seq == 0:
            for copy in code_in[:-1]:
                copy.wait_recv()
            code_in[-1].wait()
        attend(R, codes, P, A, seq, 4 * tokens)

    total = PlaneSum(me, net, lambda p: E.at[slab(p)], swapped, came)
    stores = []

    def out_product():
        def body(i, carry):
            rows = pl.ds(pl.multiple_of(i * block, block), block)
            E[rows, :] = dot(A[rows, :], Wo[...].reshape(Wo.shape[0] * Wo.shape[1], Wo.shape[2])).astype(BF16)
            return carry

        lax.fori_loop(0, 8 * tokens // block, body, 0)
        for src, dst in ((U, Uo), (R, Ro), (P, Po), (A, Ao), (T, To), (Wq, Wqo), (Wo, Woo)):
            stores.append(net.keep(src, dst))

    column("d", 1)
    q_go()
    scale_f(1)
    column("d", 3)
    spread("d", 1)
    scale_f(0)
    column("u", 1)
    normalize()
    rotation_table()
    x_gather.start()
    t_gather.start()
    q_start()
    column("d", 0)
    column("g", 3)
    column("g", 0)
    spread("g", 0)
    swap_go()
    spread("d", 3)
    column("u", 0)
    t_gather.relay_y()
    q_chain.take_in(1)
    x_gather.relay_x()
    spread("u", 1)
    x_gather.relay_y()
    q_chain.pass_on(1)
    q_chain.pass_on(2)
    spread("g", 3)
    column("g", 2)
    t_gather.relay_x()
    spread("d", 0)
    t_gather.finish()
    spread("u", 0)
    q_chain.pass_on(3)
    column("u", 2)
    code_go()
    relay("d", 0)
    spread("g", 2)
    relay("d", 3)
    relay("u", 0)
    relay("g", 0)
    q_chain.take_in(2)
    q_chain.take_in(3)
    o_start()
    x_gather.finish()
    relay("u", 1)
    spread("u", 2)
    column("g", 1)
    relay("g", 3)
    project()
    o_chain.pass_on(1)
    o_chain.pass_on(2)
    spread("g", 1)
    column("u", 3)
    attention(0)
    o_chain.pass_on(3)
    relay("g", 2)
    c_start()
    relay("d", 1)
    spread("u", 3)
    relay("g", 1)
    attention(1)
    o_chain.take_in(1)
    o_chain.take_in(2)
    relay("u", 2)
    o_chain.take_in(3)
    out_product()
    total.start()
    c_chain.pass_on(1)
    c_chain.pass_on(2)
    column("d", 2)
    total.cores()
    total.chips()
    spread("d", 2)
    c_chain.pass_on(3)
    relay("u", 3)
    c_chain.take_in(1)
    c_chain.take_in(2)
    relay("d", 2)
    c_chain.take_in(3)
    stores.append(total.finish(sums))
    for copy in last:
        copy.wait_recv()
    c_chain.twin_all()
    for copy in stores:
        copy.wait()
    net.finish()


def add_to(into, more):
    step = 16
    rows = into.shape[-2]
    steps = rows // step

    def body(k, carry):
        if len(into.shape) == 2:
            at = (pl.ds(pl.multiple_of(k * step, step), step),)
        else:
            at = (lax.div(k, steps), pl.ds(pl.multiple_of(lax.rem(k, steps) * step, step), step))
        into[at] = (into[at].astype(F32) + more[at].astype(F32)).astype(BF16)
        return carry

    lax.fori_loop(0, steps * (1 if len(into.shape) == 2 else into.shape[0]), body, 0)


class PlaneGather:
    def __init__(self, me, net, slab):
        self.me, self.net, self.slab = me, net, slab
        self.twin = me.plane(0, 0, 1)[0]
        self.x_next, self.px = me.plane(1, 0, 0)
        self.y_next, self.py = me.plane(0, 1, 0)
        self.pd = me.plane(1, 1, 0)[1]

    def start(self):
        net, own = self.net, self.slab(self.me.p)
        self.by_x = net.put(own, own, self.x_next)
        self.by_y = net.put(own, own, self.y_next)
        self.late = [net.put(own, own, self.twin)]

    def half(self, p, k):
        ref = self.slab(p)
        rows = ref.shape[0] // 2
        return ref.at[pl.ds(k * rows, rows)]

    def across(self, p):
        ref = self.slab(p)
        self.late.append(self.net.put(ref, ref, self.twin))

    def relay_x(self):
        self.by_x.wait_recv()
        ref = self.half(self.px, 0)
        self.first = self.net.put(ref, ref, self.y_next)
        self.across(self.px)

    def relay_y(self):
        self.by_y.wait_recv()
        ref = self.half(self.py, 1)
        self.second = self.net.put(ref, ref, self.x_next)
        self.across(self.py)

    def finish(self):
        self.first.wait_recv()
        self.second.wait_recv()
        self.across(self.pd)
        for copy in self.late:
            copy.wait_recv()


class PlaneSum:
    def __init__(self, me, net, slab, swapped, came):
        self.me, self.net, self.slab, self.swapped, self.came = me, net, slab, swapped, came
        self.x_next, self.y_next = me.plane(1, 0, 0)[0], me.plane(0, 1, 0)[0]
        self.places = [me.plane(dx, dy, 0)[1] for dx, dy in FLIPS + [(0, 0)]]

    def start(self):
        me = self.me
        self.swaps = []
        for k, (dx, dy) in enumerate(FLIPS + [(0, 0)]):
            other = me.plane(dx, dy, 1)[1]
            self.swaps.append(
                self.net.put(self.slab(other), self.swapped.at[k], me.plane(0, 0, 1)[0])
            )

    def half(self, k, h):
        ref = self.slab(self.places[k])
        rows = ref.shape[0] // 2
        return ref.at[pl.ds(h * rows, rows)]

    def cores(self):
        for k in range(4):
            self.swaps[k].wait_recv()
            add_to(self.slab(self.places[k]), self.swapped.at[k])
            if k == 2:
                net, came = self.net, self.came
                self.first = [
                    net.put(self.half(2, 0), came.at[1], self.x_next),
                    net.put(self.half(2, 1), came.at[3], self.y_next),
                    net.put(self.half(0, 0), came.at[0], self.x_next),
                    net.put(self.half(1, 1), came.at[2], self.y_next),
                ]

    def chips(self):
        net, came = self.net, self.came
        for copy in self.first:
            copy.wait_recv()
        add_to(self.half(1, 0), came.at[1])
        second = [net.put(self.half(1, 0), came.at[4], self.y_next)]
        add_to(self.half(0, 1), came.at[3])
        second.append(net.put(self.half(0, 1), came.at[5], self.x_next))
        add_to(self.half(3, 0), came.at[0])
        add_to(self.half(3, 1), came.at[2])
        self.second = second

    def finish(self, out):
        for h in (0, 1):
            self.second[h].wait_recv()
            add_to(self.half(3, h), self.came.at[4 + h])
        return self.net.keep(self.slab(self.places[3]), out)


class ChainSum:
    def __init__(self, me, net, slots, up, down, add=add_to):
        self.me, self.net, self.slots, self.up, self.down, self.add = me, net, slots, up, down, add
        self.base = net.take(8)

    def copy(self, z, upward, target):
        me = self.me
        landing = self.up.at[z - 1] if upward else self.down.at[z]
        k = self.base + z + (0 if upward else 4)
        return self.net.copy(self.slots.at[z], landing, k, k, me.at(target, me.x, me.y, me.c))

    def step(self, at, z, upward):
        copy = self.copy(z, upward, at + 1 if upward else at - 1)
        here = self.me.z == at

        def go():
            if at != (0 if upward else DEPTH - 1):
                copy.wait_recv()
                self.add(self.slots.at[z], self.up.at[z - 1] if upward else self.down.at[z])
            copy.start()

        pl.when(here)(go)
        self.net.sent.append((here, copy))

    def begin(self, hops):
        self.step(0, hops, True)
        self.step(DEPTH - 1, DEPTH - 1 - hops, False)

    def near(self, hops):
        self.step(1, 1 + hops, True)
        self.step(2, 2 - hops, False)

    def far(self):
        self.step(2, 3, True)
        self.step(1, 0, False)

    def finish(self):
        me = self.me

        @pl.when(me.z > 0)
        def _():
            self.copy(me.z, True, me.z).wait_recv()
            self.add(self.slots.at[me.z], self.up.at[me.z - 1])

        @pl.when(me.z < DEPTH - 1)
        def _():
            self.copy(me.z, False, me.z).wait_recv()
            self.add(self.slots.at[me.z], self.down.at[me.z])


def ffn_kernel(
    x, branch, cot, wg, wu, wd, e_out, o_out, gg, gu, gd, gain, X, N, C, Wg, Wu, Wd, H, DG, DU, O, E, R, G, S, n_send, n_recv, x_send, x_recv, e_send, e_recv, local,
):
    me = Place()
    tokens = x.shape[0]
    chip = 2 * tokens
    twin = me.plane(0, 0, 1)[0]
    ids = [me.column(dz, 0)[0] for dz in range(1, DEPTH)] + [twin]
    barrier = greet(ids)
    own_rows = pl.ds(pl.multiple_of(me.q * tokens, tokens), tokens)
    mine = [pltpu.make_async_copy(src, X.at[i], local.at[(4, 11)[i]]) for i, src in enumerate((x, branch))]
    loads = [
        pltpu.make_async_copy(src, dst, local.at[i])
        for i, (src, dst) in enumerate(((wg, Wg), (wu, Wu), (wd, Wd), (cot, C)))
    ]
    for load in mine + loads:
        load.start()

    def rows_of(z, c):
        return pl.ds(pl.multiple_of((z * 2 + c) * tokens, tokens), tokens)

    def remote(src, dst, send, recv, device):
        return pltpu.make_async_remote_copy(
            src_ref=src,
            dst_ref=dst,
            send_sem=send,
            recv_sem=recv,
            device_id=device,
            device_id_type=MESH,
        )

    def column_id(z):
        return me.at(z, me.x, me.y, me.c)

    odd = lax.rem(me.z, 2)
    order = [me.z, 1 + odd, lax.rem(me.z + 2, DEPTH), 3 * (1 - odd)]
    net = Net(n_send, n_recv, local)
    chain = Chain(me, net, lambda z, c: N.at[rows_of(z, c)], twin)

    def twin_has(i):
        chain.twin_has(order[i])

    tile = 512

    def rows_at(i):
        return pl.ds(pl.multiple_of(order[i] * chip, chip), chip)

    def hidden(i):
        twin_has(i)
        rows = rows_at(i)

        def body(t, carry):
            cols = pl.ds(t * tile, tile)
            gate = dot(N[rows, :], Wg[:, cols])
            raised = dot(N[rows, :], Wu[:, cols])
            d_hidden = dot(C[rows, :], Wd[:, cols])
            sig = jax.nn.sigmoid(gate)
            act = gate * sig
            H[rows, cols] = (act * raised).astype(BF16)
            DU[rows, cols] = (d_hidden * act).astype(BF16)
            DG[rows, cols] = (d_hidden * raised * sig * (1.0 + gate * (1.0 - sig))).astype(BF16)
            return carry

        for t in range(H.shape[1] // tile):
            body(t, 0)

    def products(i):
        rows = rows_at(i)

        def body(t, carry):
            cols = pl.ds(t * tile, tile)
            e = dot(DG[rows, :], Wg[cols, :], NT) + dot(DU[rows, :], Wu[cols, :], NT)
            E[rows, cols] = e.astype(BF16)
            piece = jnp.sum((e * N[rows, cols].astype(F32)).reshape(chip // 8, 8, tile), axis=0)
            if i == 0:
                S[:, cols] = piece
            else:
                S[:, cols] += piece
            O[rows, cols] = dot(H[rows, :], Wd[cols, :], NT).astype(BF16)
            return carry

        for t in range(E.shape[1] // tile):
            body(t, 0)
        swap(i)

    swaps, sums = {}, {}

    def swap(i):
        o = order[i]
        copy = remote(E.at[rows_of(o, 1 - me.c)], R.at[i], x_send.at[i], x_recv.at[i], twin)
        copy.start()
        swaps[i] = copy

    def total(i):
        o = order[i]
        swaps[i].wait_recv()
        first = (o * 2 + me.c) * tokens

        def body(k, carry):
            at = pl.ds(pl.multiple_of(k * 16, 16), 16)
            to = pl.ds(pl.multiple_of(first + k * 16, 16), 16)
            E[to, :] = (E[to, :].astype(F32) + R[i, at, :].astype(F32)).astype(BF16)
            return carry

        lax.fori_loop(0, tokens // 16, body, 0)
        rows = rows_of(o, me.c)
        if i == 0:
            copy = pltpu.make_async_copy(E.at[rows], e_out.at[me.z], local.at[5])
        else:
            copy = remote(E.at[rows], e_out.at[me.z], e_send.at[i], e_recv.at[me.z], column_id(o))
        copy.start()
        sums[i] = copy

    for load in mine:
        load.wait()

    def normalize(i, carry):
        at = pl.ds(pl.multiple_of(i * 16, 16), 16)
        v = X[0, at, :].astype(F32) + X[1, at, :].astype(F32)
        v = v * lax.rsqrt(jnp.mean(v * v, axis=-1, keepdims=True) + EPS)
        N[pl.ds(pl.multiple_of(me.q * tokens + i * 16, 16), 16), :] = v.astype(BF16)
        return carry

    lax.fori_loop(0, tokens // 16, normalize, 0)
    pl.semaphore_wait(barrier, 4)
    span = 256
    stores = []

    def grad_tile(t):
        rows = pl.ds(t * span, span)
        n, c = N[:, rows], C[:, rows]
        for k, (left, right, out) in enumerate(((c, H, gd), (n, DG, gg), (n, DU, gu))):
            G[k, rows, :] = dot(left, right[...], TN).astype(BF16)
            store = pltpu.make_async_copy(G.at[k, rows], out.at[rows], local.at[12 + len(stores)])
            store.start()
            stores.append(store)

    chain.start()
    for load in loads:
        load.wait()
    hidden(0)
    products(0)
    chain.pass_on(1)
    chain.pass_on(2)
    chain.take_in(1)
    hidden(1)
    products(1)
    chain.take_in(2)
    chain.pass_on(3)
    total(1)
    chain.take_in(3)
    hidden(2)
    products(2)
    total(2)
    hidden(3)
    products(3)
    total(3)
    total(0)
    grad_tile(0)
    grad_tile(1)
    grad_tile(2)
    grad_tile(3)
    grad_tile(4)
    grad_tile(5)
    grad_tile(6)
    grad_tile(7)
    for src, dst, k in ((O, o_out, 6), (S, gain, 7)):
        store = pltpu.make_async_copy(src, dst, local.at[k])
        store.start()
        stores.append(store)
    for i in range(1, DEPTH):
        o = order[i]
        remote(E.at[own_rows], e_out.at[o], e_send.at[i], e_recv.at[o], twin).wait_recv()
    sums[0].wait()
    for i in range(DEPTH):
        swaps[i].wait_send()
        if i:
            sums[i].wait_send()
    net.finish()
    for store in stores:
        store.wait()


def back_kernel(
    x, branch, cot, e_parts, part_o, gg, gu, gd, gain_f, u, r, pw, att, t, wq, wo,
    d_mid, out_o, out_e, og, ou, od, oq, oo, ov,
    DM, D, U, R, P, A, T, Wq, Wo, dA, dR, E, GQ, GO, gains, out, out_swap, out_up, out_down, e_swap, e_came,
    own, side, came, q_up, q_down, o_up, o_down, v_up, v_down, send, recv, local,
):
    me = Place()
    net = Net(send, recv, local)
    tokens = x.shape[0]
    raw = [net.keep(src, E.at[pl.ds(k * tokens, tokens)]) for k, src in enumerate((x, branch, cot))]
    raw += [net.keep(e_parts.at[k], E.at[pl.ds((3 + k) * tokens, tokens)]) for k in range(DEPTH)]
    there, away = swap_owner(me)
    barrier = greet(plane_ids(me) + column_ids(me))

    @pl.when(away)
    def _():
        pl.semaphore_signal(barrier, inc=1, device_id=there, device_id_type=MESH)

    pl.semaphore_wait(barrier, jnp.where(away, 14, 13))
    twin = me.plane(0, 0, 1)[0]
    x_next, px = me.plane(1, 0, 0)
    y_next, py = me.plane(0, 1, 0)
    pd = me.plane(1, 1, 0)[1]

    def slab(p):
        return pl.ds(pl.multiple_of(p * tokens, tokens), tokens)

    def quarter(grad, p, z):
        return grad.at[pl.ds(z * 8 + p - me.c, 2)]

    grads = {"d": (0, gd, od), "g": (1, gg, og), "u": (2, gu, ou)}
    begun, passed, late, kept = {}, {}, [], []
    hand_send = hand_recv = net.take(24)

    def first(n, z):
        g, grad, _ = grads[n]
        half = z // 2
        device, near, far = (y_next, py, px) if half else (x_next, px, py)
        at = pl.ds(z % 2 * 2, 2)
        begun[n, z] = [
            net.put(quarter(grad, near, z), came.at[g * 6 + half * 3, at], device).wait_recv,
            net.put(quarter(grad, pd, z), came.at[g * 6 + half * 3 + 1, at], device).wait_recv,
            net.keep(quarter(grad, me.p, z), own.at[g * 2 + half, at]).wait,
            net.keep(quarter(grad, far, z), side.at[g * 2 + half, at]).wait,
        ]

    def second(n, z):
        g, half, at = grads[n][0], z // 2, pl.ds(z % 2 * 2, 2)
        for wait in begun[n, z]:
            wait()
        mine = side.at[g * 2 + half, at]
        add_to(mine, came.at[g * 6 + half * 3 + 1, at])
        passed[n, z] = net.put(mine, came.at[g * 6 + half * 3 + 2, at], x_next if half else y_next)
        add_to(own.at[g * 2 + half, at], came.at[g * 6 + half * 3, at])

    def third(n, z):
        g, _, result = grads[n]
        half, at = z // 2, pl.ds(z % 2 * 2, 2)
        cols = pl.ds(pl.multiple_of(me.q * 1024, 1024), 1024)
        passed[n, z].wait_recv()
        add_to(own.at[g * 2 + half, at], came.at[g * 6 + half * 3 + 2, at])
        for c in (0, 1):
            src, dst = own.at[g * 2 + half, z % 2 * 2 + c], result.at[:, cols]
            mine = jnp.logical_and(me.z == z, me.c == c)
            k = hand_send + g * 8 + z * 2 + c
            copy = net.copy(src, dst, k, hand_recv + g * 8 + me.q, me.at(z, me.x, me.y, c))
            net.put_if(jnp.logical_not(mine), copy)
            here = pltpu.make_async_copy(src, dst, local.at[local.shape[0] - 2 - g])
            pl.when(mine)(here.start)
            late.append((mine, here))

    def norm():
        for copy in raw:
            copy.wait()

        def body(i, carry):
            def part(k):
                return E[pl.ds(pl.multiple_of(k * tokens + i * 16, 16), 16), :].astype(F32)

            v = part(0) + part(1)
            inverse = lax.rsqrt(jnp.mean(v * v, axis=-1, keepdims=True) + EPS)
            unit = v * inverse
            e = part(3) + part(4) + part(5) + part(6)
            d = part(2) + inverse * (e - unit * jnp.mean(e * unit, axis=-1, keepdims=True))
            DM[pl.ds(pl.multiple_of(i * 16, 16), 16), :] = d
            D[pl.ds(pl.multiple_of(me.p * tokens + i * 16, 16), 16), :] = d.astype(BF16)
            return carry

        lax.fori_loop(0, tokens // 16, body, 0)
        kept.append(net.keep(DM, d_mid))

    d_gather = PlaneGather(me, net, lambda p: D.at[slab(p)])
    loads = {}
    for name, src, dst in (
        ("att", att, A), ("wo", wo, Wo), ("r", r, R), ("pw", pw, P), ("t", t, T), ("u", u, U), ("wq", wq, Wq),
    ):
        loads[name] = [net.keep(src, dst)]
    loads["gain"] = [
        net.keep(gain_f.at[:, pl.ds(z * 512, 512)], gains.at[z, 1]) for z in range(DEPTH)
    ]

    def need(*names):
        for name in names:
            for copy in loads.pop(name, ()):
                copy.wait()

    out_in = []

    def out_swaps():
        for z in range(DEPTH):
            other, mine = slab(z * 2 + 1 - me.c), slab(z * 2 + me.c)
            out_in.append((net.put(part_o.at[other], out_swap.at[z], twin), net.keep(part_o.at[mine], out.at[z])))

    def out_add():
        for z in range(DEPTH):
            got, mine = out_in[z]
            got.wait_recv()
            mine.wait()
            add_to(out.at[z], out_swap.at[z])

    out_sum = ChainSum(me, net, out, out_up, out_down)

    def out_finish():
        out_sum.finish()
        kept.append(net.keep(out.at[me.z], out_o))

    block = 2 * tokens
    length = 4 * tokens
    lead = GROUP * HEAD_DIM
    scale = HEAD_DIM ** (-0.5)

    def d_attended():
        need("wo")

        def body(i, carry):
            rows = pl.ds(pl.multiple_of(i * block, block), block)
            dA[rows, :] = dot(D[rows, :], Wo[...].reshape(Wo.shape[0] * Wo.shape[1], Wo.shape[2]), NT).astype(BF16)
            return carry

        lax.fori_loop(0, 8 * tokens // block, body, 0)

    def turn_back(v, rows):
        cosine, sine = rotations(T[rows, :])
        return (v * cosine - turn(v) * sine).astype(BF16)

    def attend_back(seq):
        need("r", "pw", "t")
        keys_at = pl.ds(seq * length, length)
        keys = R[keys_at, lead : lead + HEAD_DIM]
        values = R[keys_at, lead + HEAD_DIM :]
        d_keys = jnp.zeros((length, HEAD_DIM), F32)
        d_values = jnp.zeros((length, HEAD_DIM), F32)
        for h in range(GROUP):
            cols = slice(h * HEAD_DIM, (h + 1) * HEAD_DIM)
            for part in range(2):
                rows = pl.ds(seq * length + part * (length // 2), length // 2)
                low = P[h, rows, :]
                weights = low.astype(F32)
                d_out = dA[rows, cols]
                d_weights = dot(d_out, values, NT)
                d_scores = (
                    weights * (d_weights - jnp.sum(weights * d_weights, axis=-1, keepdims=True))
                ).astype(BF16)
                dR[rows, cols] = turn_back(dot(d_scores, keys) * scale, rows)
                d_keys += dot(d_scores, R[rows, cols], TN)
                d_values += dot(low, d_out, TN)
        dR[keys_at, lead : lead + HEAD_DIM] = turn_back(d_keys * scale, keys_at)
        dR[keys_at, lead + HEAD_DIM :] = d_values.astype(BF16)

    tile = 512

    def e_product():
        need("u", "wq", "gain")

        def body(k, carry):
            i, j = lax.div(k, E.shape[1] // tile), lax.rem(k, E.shape[1] // tile)
            rows = pl.ds(pl.multiple_of(i * block, block), block)
            cols = pl.ds(pl.multiple_of(j * tile, tile), tile)
            slots = pl.ds(j * (tile // Wq.shape[1]), tile // Wq.shape[1])
            e = dot(dR[rows, :], Wq[slots].reshape(tile, Wq.shape[2]), NT)
            E[rows, cols] = e.astype(BF16)
            piece = jnp.sum((e * U[rows, cols].astype(F32)).reshape(block // 8, 8, tile), axis=0)
            gains[j, 0] = jnp.where(i == 0, 0.0, gains[j, 0]) + piece
            return carry

        lax.fori_loop(0, 8 * tokens // block * (E.shape[1] // tile), body, 0)

    e_sum = PlaneSum(me, net, lambda p: E.at[slab(p)], e_swap, e_came)
    span = 256

    def q_product():
        need("u")

        def body(k, carry):
            cols = pl.ds(pl.multiple_of(k * span, span), span)
            per = span // GQ.shape[2]
            g = dot(U[:, cols], dR[...], TN).astype(BF16)
            at = pl.ds(lax.rem(k, PLANE // per) * per, per)
            GQ[lax.div(k, PLANE // per), at] = g.reshape(per, GQ.shape[2], GQ.shape[3])
            return carry

        lax.fori_loop(0, U.shape[1] // span, body, 0)

    def o_product():
        need("att")

        def body(k, carry):
            cols = pl.ds(pl.multiple_of(k * tile, tile), tile)
            g = dot(A[...], D[:, cols], TN).astype(BF16)
            GO[:, 0, :, cols] = g.reshape(GO.shape[0], GO.shape[2], tile)
            return carry

        lax.fori_loop(0, D.shape[1] // tile, body, 0)

    def add_all(into, more):
        into[...] = into[...] + more[...]

    q_sum = ChainSum(me, net, GQ, q_up, q_down)
    o_sum = ChainSum(me, net, GO, o_up, o_down)
    v_sum = ChainSum(me, net, gains, v_up, v_down, add_all)

    def q_begin(hops):
        q_sum.begin(hops)
        v_sum.begin(hops)

    def q_near(hops):
        q_sum.near(hops)
        v_sum.near(hops)

    def q_far():
        q_sum.far()
        v_sum.far()

    def q_finish():
        q_sum.finish()
        v_sum.finish()

    k = net.take(1)
    swap = net.copy(GO.at[me.z, 0], oo, k, k, there)
    stay = pltpu.make_async_copy(GO.at[me.z, 0], oo, local.at[local.shape[0] - 1])
    stays = jnp.logical_not(away)
    owned = []

    def o_owners():
        pl.when(away)(swap.start)
        pl.when(stays)(stay.start)

    def q_owners():
        for dx in (0, 1):
            for dy in (0, 1):
                for dc in (0, 1):
                    device, p = me.plane(dx, dy, dc)
                    lanes = pl.ds(pl.multiple_of(lax.div(p, 2) * 128, 128), 128)
                    for src, dst in ((GQ.at[me.z, p], oq.at[me.p]), (gains.at[me.z, :, :, lanes], ov.at[me.p])):
                        if dx + dy + dc:
                            owned.append(net.put(src, dst, device))
                        else:
                            kept.append(net.keep(src, dst))

    def e_finish():
        kept.append(e_sum.finish(out_e))

    out_swaps()
    norm()
    d_gather.start()
    out_add()
    out_sum.begin(3)
    d_gather.relay_y()
    d_gather.relay_x()
    first("d", 0)
    out_sum.near(2)
    first("d", 3)
    out_sum.begin(2)
    d_gather.finish()
    o_product()
    out_sum.near(1)
    d_attended()
    o_sum.begin(3)
    o_sum.begin(2)
    attend_back(0)
    second("d", 0)
    first("u", 2)
    second("d", 3)
    o_sum.near(2)
    attend_back(1)
    o_sum.begin(1)
    first("g", 1)
    third("d", 0)
    q_product()
    third("d", 3)
    e_product()
    first("g", 0)
    first("d", 1)
    o_sum.near(1)
    first("g", 3)
    out_sum.far()
    o_sum.far()
    q_begin(3)
    q_near(2)
    second("u", 2)
    q_begin(2)
    first("g", 2)
    first("u", 3)
    out_sum.begin(1)
    q_near(1)
    q_far()
    second("g", 1)
    second("g", 3)
    second("g", 0)
    first("u", 0)
    third("u", 2)
    third("g", 3)
    second("d", 1)
    second("g", 2)
    third("g", 1)
    first("d", 2)
    second("u", 3)
    o_sum.finish()
    out_finish()
    o_owners()
    third("g", 2)
    e_sum.start()
    first("u", 1)
    third("g", 0)
    second("u", 0)
    third("d", 1)
    third("u", 3)
    e_sum.cores()
    q_begin(1)
    second("d", 2)
    third("u", 0)
    second("u", 1)
    third("d", 2)
    e_sum.chips()
    third("u", 1)
    q_finish()
    q_owners()
    e_finish()
    for n in "dgu":
        g, _, result = grads[n]
        for dz in range(DEPTH):
            for dc in (0, 1):
                if dz + dc:
                    _, z, c = me.column(dz, dc)
                    cols = pl.ds(pl.multiple_of((z * 2 + c) * 1024, 1024), 1024)
                    k = hand_recv + g * 8 + z * 2 + c
                    net.copy(own.at[g * 2, 0], result.at[:, cols], k, k, twin).wait_recv()
    for copy in owned:
        copy.wait_recv()
    for copy in kept:
        copy.wait()
    for mine, here in late:
        pl.when(mine)(here.wait)
    net.finish()
    pl.when(away)(swap.wait)
    pl.when(stays)(stay.wait)


def final_kernel(
    og, ou, od, oq, oo, o_sum, e_sum, d_mid, x, branch, gain,
    layer, input_grad, g_gate, g_up, g_down, g_qkv, g_out,
    v_og, v_ou, v_od, v_oq, v_oo, v_o, v_e, v_d, v_x, v_b, v_gain, f_gate, f_up, f_down, f_qkv, f_out, f_layer, f_input, sem,
):
    pairs = (
        (gain, v_gain), (og, v_og), (ou, v_ou), (od, v_od), (oq, v_oq), (oo, v_oo),
        (x, v_x), (branch, v_b), (o_sum, v_o), (e_sum, v_e), (d_mid, v_d),
    )
    loads = [pltpu.make_async_copy(src, dst, sem.at[i]) for i, (src, dst) in enumerate(pairs)]
    for load in loads:
        load.start()
    loads[0].wait()
    stores = []

    def store(src, dst):
        copy = pltpu.make_async_copy(src, dst, sem.at[len(pairs) + len(stores)])
        copy.start()
        stores.append(copy)

    def columns(src, dst, by):
        def body(i, carry):
            cols = pl.ds(pl.multiple_of(i * 1024, 1024), 1024)
            v = src[:, cols].astype(F32)
            dst[:, cols] = v if by is None else v * by
            return carry

        lax.fori_loop(0, src.shape[1] // 1024, body, 0)

    for i, (src, dst, out, by) in enumerate(
        ((v_og, f_gate, g_gate, gain), (v_ou, f_up, g_up, gain), (v_od, f_down, g_down, None))
    ):
        loads[1 + i].wait()
        columns(src, dst, None if by is None else column_of(v_gain[1:2, :])[: f_gate.shape[0]])
        store(dst, out)
    loads[4].wait()
    by = column_of(v_gain[0:1, :])[: f_qkv.shape[0]]
    for p in range(KV_HEADS):
        at = 0
        for first, size in head_columns(head_of(p)):
            f_qkv[:, first : first + size] = v_oq[p, :, at : at + size].astype(F32) * by
            at += size
    store(f_qkv, g_qkv)
    loads[5].wait()
    columns(v_oo, f_out, None)
    store(f_out, g_out)
    for load in loads[6:]:
        load.wait()

    def tokens_back(i, carry):
        at = pl.ds(pl.multiple_of(i * 16, 16), 16)
        v = v_x[at, :].astype(F32)
        f_layer[at, :] = (v + v_b[at, :].astype(F32) + v_o[at, :].astype(F32)).astype(BF16)
        inverse = lax.rsqrt(jnp.mean(v * v, axis=-1, keepdims=True) + EPS)
        unit = v * inverse
        e = v_e[at, :].astype(F32)
        f_input[at, :] = v_d[at, :] + inverse * (e - unit * jnp.mean(e * unit, axis=-1, keepdims=True))
        return carry

    lax.fori_loop(0, f_layer.shape[0] // 16, tokens_back, 0)
    store(f_layer, layer)
    store(f_input, input_grad)
    for copy in stores:
        copy.wait()


def shape(*dims, dtype=BF16):
    return jax.ShapeDtypeStruct(dims, dtype)


def shards(copies, block_input, positions, cotangent, norm_attn, w_qkv, w_out, norm_ffn, w_gate, w_up, w_down):
    tokens, width = block_input.shape
    ff = w_gate.shape[1]
    q_cols, kv_cols = HEADS * HEAD_DIM, KV_HEADS * HEAD_DIM
    spread = ("rep", "fsdp")
    place = lax.rem(lax.axis_index("rep"), PLANE) * 4 + lax.axis_index("fsdp")

    def take(w):
        if copies == 1:
            return w
        rows = w.shape[0] * copies
        whole = lax.all_gather(w, spread, axis=0, tiled=True)
        return lax.dynamic_slice_in_dim(whole, place * rows, rows, axis=0)

    def give(grad):
        if copies == 1:
            return grad
        rows = grad.shape[0]
        whole = jnp.zeros((rows * 32,) + grad.shape[1:], grad.dtype)
        whole = lax.dynamic_update_slice_in_dim(whole, grad, place * rows, axis=0)
        return lax.psum_scatter(whole, spread, scatter_dimension=0, tiled=True)

    gain_a = take(norm_attn).astype(F32)
    gain_f = take(norm_ffn).astype(F32)
    rows = gain_a.shape[0]
    gains = jnp.pad(jnp.stack([gain_a, gain_f]), ((0, 0), (0, 128 - rows)))
    own_qkv, own_gate, own_up = take(w_qkv), take(w_gate), take(w_up)
    own_down = take(w_down)
    own_out = take(w_out)
    head_cols = (GROUP + 2) * HEAD_DIM
    ff_cols = ff // 8
    full = 8 * tokens
    places = positions[None, :]
    sums, U, R, Pw, A, T, Wq, Wo, cg, Wg, Wu, Wd = call(
        front_kernel,
        0,
        [
            shape(tokens, width),
            shape(full, width),
            shape(full, head_cols),
            shape(GROUP, full, full // 2),
            shape(full, GROUP * HEAD_DIM),
            shape(full, HEAD_DIM, dtype=F32),
            shape(32, rows, head_cols),
            shape(4, rows, width),
            shape(8, tokens, width),
            shape(32, rows, ff_cols),
            shape(32, rows, ff_cols),
            shape(32, rows, ff_cols),
        ],
        (
            block_input,
            places,
            gains,
            cotangent,
            own_qkv,
            own_out,
            own_gate,
            own_up,
            own_down,
        ),
        150,
        36,
        [
            pltpu.VMEM((tokens, width), BF16),
            pltpu.VMEM((1, tokens), jnp.int32),
            pltpu.VMEM((2, 128), F32),
            pltpu.VMEM((8, tokens), F32),
            pltpu.VMEM((rows, q_cols + 2 * kv_cols), BF16),
            pltpu.VMEM((8, rows, head_cols), BF16),
            pltpu.VMEM((rows, ff), BF16),
            pltpu.VMEM((rows, ff), BF16),
            pltpu.VMEM((full, width), BF16),
            pltpu.VMEM((full, HEAD_DIM), F32),
            pltpu.VMEM((2, 8, full // 2), F32),
            pltpu.VMEM((32, rows, head_cols), BF16),
            pltpu.VMEM((4, rows, width), BF16),
            pltpu.VMEM((full, head_cols), BF16),
            pltpu.VMEM((GROUP, full, full // 2), BF16),
            pltpu.VMEM((full, GROUP * HEAD_DIM), BF16),
            pltpu.VMEM((full, width), BF16),
            pltpu.VMEM((4, tokens, width), BF16),
            pltpu.VMEM((6, tokens // 2, width), BF16),
        ],
    )
    cg = cg.reshape(full, width)
    Wg, Wu, Wd = [w.reshape(width, ff_cols) for w in (Wg, Wu, Wd)]

    e_sums, out_part, g_gate, g_up, g_down, gain_f_part = pl.pallas_call(
        ffn_kernel,
        out_shape=[
            shape(4, tokens, width),
            shape(full, width),
            shape(width, ff_cols),
            shape(width, ff_cols),
            shape(width, ff_cols),
            shape(8, width, dtype=F32),
        ],
        in_specs=[ANY] * 6,
        out_specs=[ANY] * 6,
        scratch_shapes=[pltpu.VMEM((2, tokens, width), BF16)]
        + [pltpu.VMEM((full, width), BF16)] * 2
        + [pltpu.VMEM((width, ff_cols), BF16)] * 3
        + [pltpu.VMEM((full, ff_cols), BF16)] * 3
        + [pltpu.VMEM((full, width), BF16)] * 2
        + [
            pltpu.VMEM((4, tokens, width), BF16),
            pltpu.VMEM((3, width, ff_cols), BF16),
            pltpu.VMEM((8, width), F32),
        ]
        + [pltpu.SemaphoreType.DMA((12,))] * 6
        + [pltpu.SemaphoreType.DMA((12 + 3 * width // 256,))],
        compiler_params=pltpu.CompilerParams(
            collective_id=2, has_side_effects=True, vmem_limit_bytes=60 * 1024 * 1024
        ),
    )(block_input, sums, cg, Wg, Wu, Wd)
    g_gate, g_up, g_down = [g.reshape(32, rows, ff_cols) for g in (g_gate, g_up, g_down)]
    d_mid, out_sums, ea_sums, og, ou, od, oq, oo, ov = call(
        back_kernel,
        3,
        [shape(tokens, width, dtype=F32)]
        + [shape(tokens, width)] * 2
        + [shape(rows, ff)] * 3
        + [
            shape(8, rows, head_cols),
            shape(rows, width),
            shape(8, 2, 8, 128, dtype=F32),
        ],
        (block_input, sums, cotangent, e_sums, out_part, g_gate, g_up, g_down, gain_f_part, U, R, Pw, A, T, Wq, Wo),
        140,
        90,
        [
            pltpu.VMEM((tokens, width), F32),
            pltpu.VMEM((full, width), BF16),
            pltpu.VMEM((full, width), BF16),
            pltpu.VMEM((full, head_cols), BF16),
            pltpu.VMEM((GROUP, full, full // 2), BF16),
            pltpu.VMEM((full, GROUP * HEAD_DIM), BF16),
            pltpu.VMEM((full, HEAD_DIM), F32),
            pltpu.VMEM((32, rows, head_cols), BF16),
            pltpu.VMEM((4, rows, width), BF16),
            pltpu.VMEM((full, GROUP * HEAD_DIM), BF16),
            pltpu.VMEM((full, head_cols), BF16),
            pltpu.VMEM((full, width), BF16),
            pltpu.VMEM((4, PLANE, rows, head_cols), BF16),
            pltpu.VMEM((4, 1, rows, width), BF16),
            pltpu.VMEM((4, 2, 8, width // 4), F32),
            pltpu.VMEM((4, tokens, width), BF16),
            pltpu.VMEM((4, tokens, width), BF16),
            pltpu.VMEM((3, tokens, width), BF16),
            pltpu.VMEM((3, tokens, width), BF16),
            pltpu.VMEM((4, tokens, width), BF16),
            pltpu.VMEM((6, tokens // 2, width), BF16),
            pltpu.VMEM((6, 4, rows, ff_cols), BF16),
            pltpu.VMEM((6, 4, rows, ff_cols), BF16),
            pltpu.VMEM((18, 4, rows, ff_cols), BF16),
        ]
        + [pltpu.VMEM((3, PLANE, rows, head_cols), BF16)] * 2
        + [pltpu.VMEM((3, 1, rows, width), BF16)] * 2
        + [pltpu.VMEM((3, 2, 8, width // 4), F32)] * 2,
    )
    layer_output, input_gradient, g_gate, g_up, g_down, g_qkv, g_out = pl.pallas_call(
        final_kernel,
        out_shape=[
            shape(tokens, width),
            shape(tokens, width, dtype=F32),
            shape(rows, ff, dtype=F32),
            shape(rows, ff, dtype=F32),
            shape(rows, ff, dtype=F32),
            shape(rows, q_cols + 2 * kv_cols, dtype=F32),
            shape(rows, width, dtype=F32),
        ],
        in_specs=[ANY] * 11,
        out_specs=[ANY] * 7,
        scratch_shapes=[pltpu.VMEM((rows, ff), BF16)] * 3
        + [pltpu.VMEM((8, rows, head_cols), BF16), pltpu.VMEM((rows, width), BF16)]
        + [pltpu.VMEM((tokens, width), BF16)] * 2
        + [pltpu.VMEM((tokens, width), F32)]
        + [pltpu.VMEM((tokens, width), BF16)] * 2
        + [pltpu.VMEM((2, 128), F32)]
        + [pltpu.VMEM((rows, ff), F32)] * 3
        + [
            pltpu.VMEM((rows, q_cols + 2 * kv_cols), F32),
            pltpu.VMEM((rows, width), F32),
            pltpu.VMEM((tokens, width), BF16),
            pltpu.VMEM((tokens, width), F32),
            pltpu.SemaphoreType.DMA((18,)),
        ],
        compiler_params=pltpu.CompilerParams(vmem_limit_bytes=60 * 1024 * 1024),
    )(og, ou, od, oq, oo, out_sums, ea_sums, d_mid, block_input, sums, gains)
    gain_sums = jnp.sum(ov, axis=(0, 2))
    gain_sums = lax.dynamic_slice_in_dim(gain_sums, place % 2 * rows, rows, axis=1)
    return (
        layer_output,
        input_gradient,
        give(gain_sums[0] / gain_a),
        give(g_qkv),
        give(g_out),
        give(gain_sums[1] / gain_f),
        give(g_gate),
        give(g_up),
        give(g_down),
    )


def solution(mesh):
    copies = mesh.shape["rep"] * mesh.shape["fsdp"] // 32
    rows, flat = P(("rep", "fsdp"), None), P(("rep", "fsdp"))
    return jax.shard_map(
        functools.partial(shards, copies),
        mesh=mesh,
        in_specs=(rows, flat, rows, flat, rows, rows, flat, rows, rows, rows),
        out_specs=(rows, rows, flat, rows, rows, flat, rows, rows, rows),
        check_vma=False,
    )
```

```python
import functools
import math

import jax
import jax.numpy as jnp
from jax import lax
from jax.experimental import pallas as pl
from jax.experimental.pallas import tpu as pltpu
from jax.sharding import PartitionSpec as P

HEADS = 16
KV_HEADS = 8
HEAD_DIM = 128
BLOCK = 256
MOST_BLOCKS = 2
GROUP = HEADS // KV_HEADS
EPS = 1e-05
THETA = 1000000.0
MESH = pl.DeviceIdType.MESH
F32 = jnp.float32
BF16 = jnp.bfloat16

PLANE = 8
DEPTH = 4
FLIPS = [(1, 0), (0, 1), (1, 1)]


def dot(a, b, dims=((1,), (0,))):
    return lax.dot_general(a, b, (dims, ((), ())), preferred_element_type=F32)


NT = ((1,), (1,))
TN = ((0,), (0,))


def flip(bit, by):
    return lax.rem(bit + by, 2)


class Place:
    def __init__(self):
        rep, self.f = lax.axis_index("rep"), lax.axis_index("fsdp")
        self.r = lax.rem(rep, PLANE)
        self.base = rep - self.r
        self.z, self.x = lax.div(self.r, 2), lax.rem(self.r, 2)
        self.y, self.c = lax.div(self.f, 2), lax.rem(self.f, 2)
        self.p = self.x * 4 + self.f
        self.q = self.z * 2 + self.c
        self.d = self.r * 4 + self.f

    def at(self, z, x, y, c):
        return (self.base + z * 2 + x, y * 2 + c)

    def plane(self, dx, dy, dc):
        x, y, c = flip(self.x, dx), flip(self.y, dy), flip(self.c, dc)
        return self.at(self.z, x, y, c), x * 4 + y * 2 + c

    def column(self, dz, dc):
        z, c = lax.rem(self.z + dz, DEPTH), flip(self.c, dc)
        return self.at(z, self.x, self.y, c), z, c

    def behind(self, dz):
        return lax.rem(self.z + (DEPTH - dz), DEPTH)


class Net:
    def __init__(self, send, recv, local):
        self.send, self.recv, self.local_sem = send, recv, local
        self.used = 0
        self.sent, self.kept = [], []

    def take(self, count):
        self.used += count
        return self.used - count

    def copy(self, src, dst, send, recv, device):
        return pltpu.make_async_remote_copy(
            src_ref=src,
            dst_ref=dst,
            send_sem=self.send.at[send],
            recv_sem=self.recv.at[recv],
            device_id=device,
            device_id_type=MESH,
        )

    def put(self, src, dst, device):
        k = self.take(1)
        copy = self.copy(src, dst, k, k, device)
        copy.start()
        self.sent.append((None, copy))
        return copy

    def put_if(self, when, copy):
        pl.when(when)(copy.start)
        self.sent.append((when, copy))
        return copy

    def keep(self, src, dst):
        copy = pltpu.make_async_copy(src, dst, self.local_sem.at[len(self.kept)])
        copy.start()
        self.kept.append(copy)
        return copy

    def finish(self):
        for when, copy in self.sent:
            if when is None:
                copy.wait_send()
            else:
                pl.when(when)(copy.wait_send)


class Chain:
    def __init__(self, me, net, slot, twins=None):
        self.me, self.net, self.slot, self.twins = me, net, slot, twins
        self.base = net.take(12)
        last = DEPTH - 1
        self.first, self.last = me.z == 0, me.z == last
        self.inner = jnp.logical_and(me.z > 0, me.z < last)
        self.order = [
            me.z,
            1 + lax.rem(me.z, 2),
            jnp.where(self.inner, last * (me.z - 1), 2 - lax.div(me.z, last)),
            last * (1 - lax.div(me.z, 2)),
        ]
        self.steps = [None] + [self.arrival(i) for i in range(1, DEPTH)]

    def pass_on(self, i):
        self.steps[i][0]()

    def take_in(self, i):
        self.steps[i][1]()

    def link(self, z, k, target):
        me = self.me
        ref = self.slot(z, me.c)
        return self.net.copy(ref, ref, self.base + k, self.base + z, me.at(target, me.x, me.y, me.c))

    def start(self):
        me, net = self.me, self.net
        net.put_if(jnp.logical_not(self.last), self.link(me.z, 0, me.z + 1))
        net.put_if(jnp.logical_not(self.first), self.link(me.z, 1, me.z - 1))
        if self.twins is not None:
            self.twin(me.z, 0)

    def twin(self, z, k):
        ref, net = self.slot(z, self.me.c), self.net
        copy = net.copy(ref, ref, self.base + 8 + k, self.base + 4 + z, self.twins)
        copy.start()
        net.sent.append((None, copy))

    def arrival(self, i):
        me, net = self.me, self.net
        z = self.order[i]
        onward = self.link(z, 1 + i, me.z + jnp.where(z < me.z, 1, -1))
        across = None
        net.sent.append((self.inner, onward))
        if self.twins is not None:
            ref = self.slot(z, me.c)
            across = net.copy(ref, ref, self.base + 8 + i, self.base + 4 + z, self.twins)
            net.sent.append((None, across))

        def take(passes):
            onward.wait_recv()
            if passes:
                onward.start()
            if across is not None:
                across.start()

        return (
            lambda: pl.when(self.inner)(lambda: take(True)),
            lambda: pl.when(jnp.logical_not(self.inner))(lambda: take(False)),
        )

    def twin_has(self, z):
        ref = self.slot(z, 1 - self.me.c)
        self.net.copy(ref, ref, self.base + 4, self.base + 4 + z, self.twins).wait_recv()

    def twin_all(self):
        for z in range(DEPTH):
            self.twin_has(z)


def greet(devices):
    barrier = pltpu.get_barrier_semaphore()
    for device in devices:
        pl.semaphore_signal(barrier, inc=1, device_id=device, device_id_type=MESH)
    return barrier


def plane_ids(me):
    return [
        me.plane(dx, dy, dc)[0] for dx in (0, 1) for dy in (0, 1) for dc in (0, 1) if dx + dy + dc
    ]


def column_ids(me):
    return [me.column(dz, dc)[0] for dz in range(1, DEPTH) for dc in (0, 1)]


def sems(sends, locals_):
    return [
        pltpu.SemaphoreType.DMA((sends,)),
        pltpu.SemaphoreType.DMA((sends,)),
        pltpu.SemaphoreType.DMA((locals_,)),
    ]


ANY = pl.BlockSpec(memory_space=pl.ANY)


def call(kernel, ident, outs, args, sends, locals_, scratch=()):
    return pl.pallas_call(
        kernel,
        out_shape=outs,
        in_specs=[ANY] * len(args),
        out_specs=[ANY] * len(outs),
        scratch_shapes=list(scratch) + sems(sends, locals_),
        compiler_params=pltpu.CompilerParams(
            collective_id=ident, has_side_effects=True, vmem_limit_bytes=60 * 1024 * 1024
        ),
    )(*args)


def head_of(p):
    return 2 * (p % 4) + p // 4


def head_columns(head):
    lead = GROUP * HEAD_DIM
    return (
        (head * lead, lead),
        (HEADS * HEAD_DIM + head * HEAD_DIM, HEAD_DIM),
        ((HEADS + KV_HEADS + head) * HEAD_DIM, HEAD_DIM),
    )


def column_of(row):
    return jnp.transpose(jnp.broadcast_to(row.astype(F32), (8, row.shape[1])))[:, 0:1]


def swap_owner(me):
    return me.at(me.f, me.x, lax.div(me.z, 2), lax.rem(me.z, 2)), me.f != me.z


def turn(v):
    return pltpu.roll(v, HEAD_DIM // 2, 1)


def rotations(table):
    swapped = turn(table)
    low = lax.broadcasted_iota(jnp.int32, table.shape, 1) < HEAD_DIM // 2
    return jnp.where(low, table, swapped), jnp.where(low, -swapped, table)


def attend(R, codes, P, A, seq, length):
    half = length // 2
    keys_at = pl.ds(seq * length, length)
    keys = R[keys_at, GROUP * HEAD_DIM : (GROUP + 1) * HEAD_DIM]
    values = R[keys_at, (GROUP + 1) * HEAD_DIM :]
    code = codes[seq, 0:1, :]
    for part in range(2):
        rows = pl.ds(seq * length + part * half, half)
        most = jnp.transpose(codes[seq, :, part * half : (part + 1) * half])[:, 0:1]
        least = jnp.floor(most * (1.0 / MOST_BLOCKS)) * MOST_BLOCKS
        allowed = (code <= most) & (code >= least)
        for h in range(GROUP):
            cols = slice(h * HEAD_DIM, (h + 1) * HEAD_DIM)
            scores = dot(R[rows, cols], keys, NT) * HEAD_DIM ** (-0.5)
            scores = jnp.where(allowed, scores, -1e30)
            exponent = jnp.exp(scores - jnp.max(scores, axis=-1, keepdims=True))
            weights = (exponent / jnp.sum(exponent, axis=-1, keepdims=True)).astype(BF16)
            P[h, rows, :] = weights
            A[rows, cols] = dot(weights, values).astype(BF16)


def front_kernel(
    x, pos, gain, cot, wq, wo, wg, wu, wd,
    sums, Uo, Ro, Po, Ao, To, Wqo, Woo, cg, Wg, Wu, Wd,
    X, places, gains, code, q_raw, q_own, g_own, u_own, d_own, c_own, U, T, codes, Wq, Wo, R, P, A, E, swapped, came, send, recv, local,
):
    me = Place()
    net = Net(send, recv, local)
    tokens = x.shape[0]
    there, away = swap_owner(me)
    barrier = greet(plane_ids(me) + column_ids(me))

    raw = [net.keep(src, dst) for src, dst in ((pos, places), (gain, gains), (wd, d_own), (x, X), (wq, q_raw), (wg, g_own), (wu, u_own), (cot, c_own))]

    @pl.when(away)
    def _():
        pl.semaphore_signal(barrier, inc=1, device_id=there, device_id_type=MESH)

    pl.semaphore_wait(barrier, jnp.where(away, 14, 13))
    twin = me.plane(0, 0, 1)[0]
    x_next, y_next = me.plane(1, 0, 0)[0], me.plane(0, 1, 0)[0]

    def slab(p):
        return pl.ds(pl.multiple_of(p * tokens, tokens), tokens)

    own_rows = slab(me.p)
    raw[1].wait()
    raw[2].wait()

    def normalize():
        raw[3].wait()

        def body(i, carry):
            at = pl.ds(pl.multiple_of(i * 16, 16), 16)
            v = X[at, :].astype(F32)
            v = v * lax.rsqrt(jnp.mean(v * v, axis=-1, keepdims=True) + EPS)
            U[pl.ds(pl.multiple_of(me.p * tokens + i * 16, 16), 16), :] = v.astype(BF16)
            return carry

        lax.fori_loop(0, tokens // 16, body, 0)

    def rotation_table():
        raw[0].wait()
        half = HEAD_DIM // 2
        place = jnp.broadcast_to(places[...], code.shape)
        column = jnp.transpose(place.astype(F32))[:, 0:1]
        index = lax.broadcasted_iota(jnp.int32, (1, half), 1).astype(F32)
        angles = column * jnp.exp(index * (-math.log(THETA) / half))
        T[own_rows, :] = jnp.concatenate([jnp.cos(angles), jnp.sin(angles)], axis=1)
        lane = lax.broadcasted_iota(jnp.int32, place.shape, 1)
        start = me.f * tokens + lane - place
        code[...] = (start * MOST_BLOCKS + lax.div(place, jnp.full_like(place, BLOCK))).astype(F32)

    def scale_q():
        raw[4].wait()
        by = column_of(gains[0:1, :])[: q_raw.shape[0]]
        for p in range(KV_HEADS):
            to = 0
            for first, size in head_columns(head_of(p)):
                q_own[p, :, to : to + size] = (q_raw[:, first : first + size].astype(F32) * by).astype(BF16)
                to += size

    def scale_f(k):
        raw[5 + k].wait()
        w = (g_own, u_own)[k]
        by = column_of(gains[1:2, :])[: w.shape[0]]

        def body(i, carry):
            cols = pl.ds(pl.multiple_of(i * 1024, 1024), 1024)
            w[:, cols] = (w[:, cols].astype(F32) * by).astype(BF16)
            return carry

        lax.fori_loop(0, w.shape[1] // 1024, body, 0)

    weights = {"g": (g_own, Wg), "u": (u_own, Wu), "d": (d_own, Wd)}
    taken, sent, last = {}, {}, []

    def column(n, dz):
        w, W = weights[n]
        taken[n, dz] = []
        for dc in (0, 1):
            device, z, c = me.column(dz, dc)
            cols = pl.ds(pl.multiple_of((z * 2 + c) * 1024, 1024), 1024)
            if dz + dc:
                taken[n, dz].append(net.put(w.at[:, cols], W.at[me.d], device).wait_recv)
            else:
                taken[n, dz].append(net.keep(w.at[:, cols], W.at[me.d]).wait)

    def spread(n, dz):
        W = weights[n][1]
        for wait in taken[n, dz]:
            wait()
        rows = pl.ds(me.behind(dz) * 8 + me.p - me.c, 2)
        sent[n, dz] = [net.put(W.at[rows], W.at[rows], device) for device in (x_next, y_next)]

    def relay(n, dz):
        W = weights[n][1]
        by_x, by_y = sent[n, dz]
        first = me.behind(dz) * 8 - me.c
        if dz % 2:
            by_x.wait_recv()
            rows = pl.ds(first + me.plane(1, 0, 0)[1], 2)
            last.extend((net.put(W.at[rows], W.at[rows], y_next), by_y))
        else:
            by_y.wait_recv()
            rows = pl.ds(first + me.plane(0, 1, 0)[1], 2)
            last.extend((net.put(W.at[rows], W.at[rows], x_next), by_x))

    q_in = []

    def q_go():
        scale_q()
        for dx in (0, 1):
            for dy in (0, 1):
                for dc in (0, 1):
                    device, p = me.plane(dx, dy, dc)
                    if dx + dy + dc:
                        q_in.append(net.put(q_own.at[p], Wq.at[me.d], device))
                    else:
                        own = net.keep(q_own.at[p], Wq.at[me.d])
        q_in.append(own)

    q_chain = Chain(me, net, lambda z, c: Wq.at[pl.ds(z * PLANE, PLANE)])
    o_chain = Chain(me, net, lambda z, c: Wo.at[z])
    c_chain = Chain(me, net, lambda z, c: cg.at[z * 2 + c], twin)

    def q_start():
        for copy in q_in[:-1]:
            copy.wait_recv()
        q_in[-1].wait()
        q_chain.start()

    k = net.take(1)
    swap = net.copy(wo, Wo.at[me.f], k, k, there)
    stay = pltpu.make_async_copy(wo, Wo.at[me.f], local.at[local.shape[0] - 1])
    stays = jnp.logical_not(away)

    def swap_go():
        pl.when(away)(swap.start)
        pl.when(stays)(stay.start)

    def o_start():
        pl.when(away)(swap.wait)
        pl.when(stays)(stay.wait)
        o_chain.start()

    def c_start():
        raw[7].wait()
        net.keep(c_own, cg.at[me.q]).wait()
        c_chain.start()

    t_gather = PlaneGather(me, net, lambda p: T.at[slab(p)])
    x_gather = PlaneGather(me, net, lambda p: U.at[slab(p)])
    code_in = []

    def code_go():
        lanes = pl.ds(pl.multiple_of(lax.rem(me.p, 4) * tokens, tokens), tokens)
        at = codes.at[lax.div(me.p, 4), :, lanes]
        code_in.extend(net.put(code, at, device) for device in plane_ids(me))
        code_in.append(net.keep(code, at))

    block = 2 * tokens
    lead = GROUP * HEAD_DIM

    def project():
        def body(i, carry):
            rows = pl.ds(pl.multiple_of(i * block, block), block)
            q = dot(U[rows, :], Wq[...].reshape(Wq.shape[0] * Wq.shape[1], Wq.shape[2]))
            cosine, sine = rotations(T[rows, :])
            for h in range(GROUP + 1):
                v = q[:, h * HEAD_DIM : (h + 1) * HEAD_DIM]
                R[rows, h * HEAD_DIM : (h + 1) * HEAD_DIM] = (v * cosine + turn(v) * sine).astype(BF16)
            R[rows, lead + HEAD_DIM :] = q[:, lead + HEAD_DIM :].astype(BF16)
            return carry

        lax.fori_loop(0, 8 * tokens // block, body, 0)

    def attention(seq):
        if seq == 0:
            for copy in code_in[:-1]:
                copy.wait_recv()
            code_in[-1].wait()
        attend(R, codes, P, A, seq, 4 * tokens)

    total = PlaneSum(me, net, lambda p: E.at[slab(p)], swapped, came)
    stores = []

    def out_product():
        def body(i, carry):
            rows = pl.ds(pl.multiple_of(i * block, block), block)
            E[rows, :] = dot(A[rows, :], Wo[...].reshape(Wo.shape[0] * Wo.shape[1], Wo.shape[2])).astype(BF16)
            return carry

        lax.fori_loop(0, 8 * tokens // block, body, 0)
        for src, dst in ((U, Uo), (R, Ro), (P, Po), (A, Ao), (T, To), (Wq, Wqo), (Wo, Woo)):
            stores.append(net.keep(src, dst))

    column("d", 1)
    q_go()
    scale_f(1)
    column("u", 1)
    spread("d", 1)
    column("u", 0)
    q_start()
    spread("u", 0)
    rotation_table()
    t_gather.start()
    column("u", 3)
    code_go()
    normalize()
    scale_f(0)
    column("g", 0)
    x_gather.start()
    swap_go()
    column("g", 3)
    t_gather.relay_y()
    relay("u", 0)
    column("u", 2)
    spread("u", 1)
    x_gather.relay_x()
    q_chain.take_in(1)
    x_gather.relay_y()
    o_start()
    column("d", 0)
    spread("u", 3)
    t_gather.relay_x()
    q_chain.pass_on(1)
    spread("g", 0)
    q_chain.pass_on(2)
    t_gather.finish()
    spread("u", 2)
    spread("g", 3)
    o_chain.pass_on(1)
    relay("u", 3)
    q_chain.take_in(2)
    column("g", 2)
    spread("d", 0)
    relay("g", 0)
    relay("d", 1)
    o_chain.pass_on(2)
    relay("g", 3)
    q_chain.pass_on(3)
    x_gather.finish()
    relay("u", 1)
    column("g", 1)
    relay("d", 0)
    spread("g", 2)
    q_chain.take_in(3)
    o_chain.take_in(1)
    column("d", 3)
    o_chain.pass_on(3)
    o_chain.take_in(2)
    project()
    spread("g", 1)
    c_start()
    relay("u", 2)
    attention(0)
    spread("d", 3)
    attention(1)
    relay("g", 1)
    relay("g", 2)
    o_chain.take_in(3)
    out_product()
    total.start()
    c_chain.pass_on(1)
    c_chain.pass_on(2)
    column("d", 2)
    total.cores()
    total.chips()
    spread("d", 2)
    c_chain.take_in(1)
    c_chain.pass_on(3)
    relay("d", 3)
    c_chain.take_in(2)
    relay("d", 2)
    c_chain.take_in(3)
    stores.append(total.finish(sums))
    for copy in last:
        copy.wait_recv()
    c_chain.twin_all()
    for copy in stores:
        copy.wait()
    net.finish()


def add_to(into, more):
    step = 16
    rows = into.shape[-2]
    steps = rows // step

    def body(k, carry):
        if len(into.shape) == 2:
            at = (pl.ds(pl.multiple_of(k * step, step), step),)
        else:
            at = (lax.div(k, steps), pl.ds(pl.multiple_of(lax.rem(k, steps) * step, step), step))
        into[at] = (into[at].astype(F32) + more[at].astype(F32)).astype(BF16)
        return carry

    lax.fori_loop(0, steps * (1 if len(into.shape) == 2 else into.shape[0]), body, 0)


class PlaneGather:
    def __init__(self, me, net, slab):
        self.me, self.net, self.slab = me, net, slab
        self.twin = me.plane(0, 0, 1)[0]
        self.x_next, self.px = me.plane(1, 0, 0)
        self.y_next, self.py = me.plane(0, 1, 0)
        self.pd = me.plane(1, 1, 0)[1]

    def start(self):
        net, own = self.net, self.slab(self.me.p)
        self.by_x = net.put(own, own, self.x_next)
        self.by_y = net.put(own, own, self.y_next)
        self.late = [net.put(own, own, self.twin)]

    def half(self, p, k):
        ref = self.slab(p)
        rows = ref.shape[0] // 2
        return ref.at[pl.ds(k * rows, rows)]

    def across(self, p):
        ref = self.slab(p)
        self.late.append(self.net.put(ref, ref, self.twin))

    def relay_x(self):
        self.by_x.wait_recv()
        ref = self.half(self.px, 0)
        self.first = self.net.put(ref, ref, self.y_next)
        self.across(self.px)

    def relay_y(self):
        self.by_y.wait_recv()
        ref = self.half(self.py, 1)
        self.second = self.net.put(ref, ref, self.x_next)
        self.across(self.py)

    def finish(self):
        self.first.wait_recv()
        self.second.wait_recv()
        self.across(self.pd)
        for copy in self.late:
            copy.wait_recv()


class PlaneSum:
    def __init__(self, me, net, slab, swapped, came):
        self.me, self.net, self.slab, self.swapped, self.came = me, net, slab, swapped, came
        self.x_next, self.y_next = me.plane(1, 0, 0)[0], me.plane(0, 1, 0)[0]
        self.places = [me.plane(dx, dy, 0)[1] for dx, dy in FLIPS + [(0, 0)]]

    def start(self):
        me = self.me
        self.swaps = []
        for k, (dx, dy) in enumerate(FLIPS + [(0, 0)]):
            other = me.plane(dx, dy, 1)[1]
            self.swaps.append(
                self.net.put(self.slab(other), self.swapped.at[k], me.plane(0, 0, 1)[0])
            )

    def half(self, k, h):
        ref = self.slab(self.places[k])
        rows = ref.shape[0] // 2
        return ref.at[pl.ds(h * rows, rows)]

    def cores(self):
        for k in range(4):
            self.swaps[k].wait_recv()
            add_to(self.slab(self.places[k]), self.swapped.at[k])
            if k == 2:
                net, came = self.net, self.came
                self.first = [
                    net.put(self.half(2, 0), came.at[1], self.x_next),
                    net.put(self.half(2, 1), came.at[3], self.y_next),
                    net.put(self.half(0, 0), came.at[0], self.x_next),
                    net.put(self.half(1, 1), came.at[2], self.y_next),
                ]

    def chips(self):
        net, came = self.net, self.came
        for copy in self.first:
            copy.wait_recv()
        add_to(self.half(1, 0), came.at[1])
        second = [net.put(self.half(1, 0), came.at[4], self.y_next)]
        add_to(self.half(0, 1), came.at[3])
        second.append(net.put(self.half(0, 1), came.at[5], self.x_next))
        add_to(self.half(3, 0), came.at[0])
        add_to(self.half(3, 1), came.at[2])
        self.second = second

    def finish(self, out):
        for h in (0, 1):
            self.second[h].wait_recv()
            add_to(self.half(3, h), self.came.at[4 + h])
        return self.net.keep(self.slab(self.places[3]), out)


class ChainSum:
    def __init__(self, me, net, slots, up, down, add=add_to):
        self.me, self.net, self.slots, self.up, self.down, self.add = me, net, slots, up, down, add
        self.base = net.take(8)

    def copy(self, z, upward, target):
        me = self.me
        landing = self.up.at[z - 1] if upward else self.down.at[z]
        k = self.base + z + (0 if upward else 4)
        return self.net.copy(self.slots.at[z], landing, k, k, me.at(target, me.x, me.y, me.c))

    def step(self, at, z, upward):
        copy = self.copy(z, upward, at + 1 if upward else at - 1)
        here = self.me.z == at

        def go():
            if at != (0 if upward else DEPTH - 1):
                copy.wait_recv()
                self.add(self.slots.at[z], self.up.at[z - 1] if upward else self.down.at[z])
            copy.start()

        pl.when(here)(go)
        self.net.sent.append((here, copy))

    def begin(self, hops):
        self.step(0, hops, True)
        self.step(DEPTH - 1, DEPTH - 1 - hops, False)

    def near(self, hops):
        self.step(1, 1 + hops, True)
        self.step(2, 2 - hops, False)

    def far(self):
        self.step(2, 3, True)
        self.step(1, 0, False)

    def finish(self):
        me = self.me

        @pl.when(me.z > 0)
        def _():
            self.copy(me.z, True, me.z).wait_recv()
            self.add(self.slots.at[me.z], self.up.at[me.z - 1])

        @pl.when(me.z < DEPTH - 1)
        def _():
            self.copy(me.z, False, me.z).wait_recv()
            self.add(self.slots.at[me.z], self.down.at[me.z])


def ffn_kernel(
    x, branch, cot, wg, wu, wd, e_out, o_out, gg, gu, gd, gain, X, N, C, Wg, Wu, Wd, H, DG, DU, O, E, R, G, S, n_send, n_recv, x_send, x_recv, e_send, e_recv, local,
):
    me = Place()
    tokens = x.shape[0]
    chip = 2 * tokens
    twin = me.plane(0, 0, 1)[0]
    ids = [me.column(dz, 0)[0] for dz in range(1, DEPTH)] + [twin]
    barrier = greet(ids)
    own_rows = pl.ds(pl.multiple_of(me.q * tokens, tokens), tokens)
    mine = [pltpu.make_async_copy(src, X.at[i], local.at[(4, 11)[i]]) for i, src in enumerate((x, branch))]
    loads = [
        pltpu.make_async_copy(src, dst, local.at[i])
        for i, (src, dst) in enumerate(((wg, Wg), (wu, Wu), (wd, Wd), (cot, C)))
    ]
    for load in mine + loads:
        load.start()

    def rows_of(z, c):
        return pl.ds(pl.multiple_of((z * 2 + c) * tokens, tokens), tokens)

    def remote(src, dst, send, recv, device):
        return pltpu.make_async_remote_copy(
            src_ref=src,
            dst_ref=dst,
            send_sem=send,
            recv_sem=recv,
            device_id=device,
            device_id_type=MESH,
        )

    def column_id(z):
        return me.at(z, me.x, me.y, me.c)

    odd = lax.rem(me.z, 2)
    order = [me.z, 1 + odd, lax.rem(me.z + 2, DEPTH), 3 * (1 - odd)]
    net = Net(n_send, n_recv, local)
    chain = Chain(me, net, lambda z, c: N.at[rows_of(z, c)], twin)

    def twin_has(i):
        chain.twin_has(order[i])

    tile = 512

    def rows_at(i):
        return pl.ds(pl.multiple_of(order[i] * chip, chip), chip)

    def hidden(i):
        twin_has(i)
        rows = rows_at(i)

        def body(t, carry):
            cols = pl.ds(t * tile, tile)
            gate = dot(N[rows, :], Wg[:, cols])
            raised = dot(N[rows, :], Wu[:, cols])
            d_hidden = dot(C[rows, :], Wd[:, cols])
            sig = jax.nn.sigmoid(gate)
            act = gate * sig
            H[rows, cols] = (act * raised).astype(BF16)
            DU[rows, cols] = (d_hidden * act).astype(BF16)
            DG[rows, cols] = (d_hidden * raised * sig * (1.0 + gate * (1.0 - sig))).astype(BF16)
            return carry

        for t in range(H.shape[1] // tile):
            body(t, 0)

    def products(i):
        rows = rows_at(i)

        def body(t, carry):
            cols = pl.ds(t * tile, tile)
            e = dot(DG[rows, :], Wg[cols, :], NT) + dot(DU[rows, :], Wu[cols, :], NT)
            E[rows, cols] = e.astype(BF16)
            piece = jnp.sum((e * N[rows, cols].astype(F32)).reshape(chip // 8, 8, tile), axis=0)
            if i == 0:
                S[:, cols] = piece
            else:
                S[:, cols] += piece
            O[rows, cols] = dot(H[rows, :], Wd[cols, :], NT).astype(BF16)
            return carry

        for t in range(E.shape[1] // tile):
            body(t, 0)
        swap(i)

    swaps, sums = {}, {}

    def swap(i):
        o = order[i]
        copy = remote(E.at[rows_of(o, 1 - me.c)], R.at[i], x_send.at[i], x_recv.at[i], twin)
        copy.start()
        swaps[i] = copy

    def total(i):
        o = order[i]
        swaps[i].wait_recv()
        first = (o * 2 + me.c) * tokens

        def body(k, carry):
            at = pl.ds(pl.multiple_of(k * 16, 16), 16)
            to = pl.ds(pl.multiple_of(first + k * 16, 16), 16)
            E[to, :] = (E[to, :].astype(F32) + R[i, at, :].astype(F32)).astype(BF16)
            return carry

        lax.fori_loop(0, tokens // 16, body, 0)
        rows = rows_of(o, me.c)
        if i == 0:
            copy = pltpu.make_async_copy(E.at[rows], e_out.at[me.z], local.at[5])
        else:
            copy = remote(E.at[rows], e_out.at[me.z], e_send.at[i], e_recv.at[me.z], column_id(o))
        copy.start()
        sums[i] = copy

    for load in mine:
        load.wait()

    def normalize(i, carry):
        at = pl.ds(pl.multiple_of(i * 16, 16), 16)
        v = X[0, at, :].astype(F32) + X[1, at, :].astype(F32)
        v = v * lax.rsqrt(jnp.mean(v * v, axis=-1, keepdims=True) + EPS)
        N[pl.ds(pl.multiple_of(me.q * tokens + i * 16, 16), 16), :] = v.astype(BF16)
        return carry

    lax.fori_loop(0, tokens // 16, normalize, 0)
    pl.semaphore_wait(barrier, 4)
    span = 256
    stores = []

    def grad_tile(t):
        rows = pl.ds(t * span, span)
        n, c = N[:, rows], C[:, rows]
        for k, (left, right, out) in enumerate(((c, H, gd), (n, DG, gg), (n, DU, gu))):
            G[k, rows, :] = dot(left, right[...], TN).astype(BF16)
            store = pltpu.make_async_copy(G.at[k, rows], out.at[rows], local.at[12 + len(stores)])
            store.start()
            stores.append(store)

    chain.start()
    for load in loads:
        load.wait()
    hidden(0)
    products(0)
    chain.pass_on(1)
    chain.pass_on(2)
    chain.take_in(1)
    hidden(1)
    products(1)
    chain.take_in(2)
    chain.pass_on(3)
    total(1)
    chain.take_in(3)
    hidden(2)
    products(2)
    total(2)
    hidden(3)
    products(3)
    total(3)
    total(0)
    grad_tile(0)
    grad_tile(1)
    grad_tile(2)
    grad_tile(3)
    grad_tile(4)
    grad_tile(5)
    grad_tile(6)
    grad_tile(7)
    for src, dst, k in ((O, o_out, 6), (S, gain, 7)):
        store = pltpu.make_async_copy(src, dst, local.at[k])
        store.start()
        stores.append(store)
    for i in range(1, DEPTH):
        o = order[i]
        remote(E.at[own_rows], e_out.at[o], e_send.at[i], e_recv.at[o], twin).wait_recv()
    sums[0].wait()
    for i in range(DEPTH):
        swaps[i].wait_send()
        if i:
            sums[i].wait_send()
    net.finish()
    for store in stores:
        store.wait()


def back_kernel(
    x, branch, cot, e_parts, part_o, gg, gu, gd, gain_f, u, r, pw, att, t, wq, wo,
    d_mid, out_o, out_e, og, ou, od, oq, oo, ov,
    DM, D, U, R, P, A, T, Wq, Wo, dA, dR, E, GQ, GO, gains, out, out_swap, out_up, out_down, e_swap, e_came,
    own, side, came, q_up, q_down, o_up, o_down, v_up, v_down, send, recv, local,
):
    me = Place()
    net = Net(send, recv, local)
    tokens = x.shape[0]
    raw = [net.keep(src, E.at[pl.ds(k * tokens, tokens)]) for k, src in enumerate((x, branch, cot))]
    raw += [net.keep(e_parts.at[k], E.at[pl.ds((3 + k) * tokens, tokens)]) for k in range(DEPTH)]
    there, away = swap_owner(me)
    barrier = greet(plane_ids(me) + column_ids(me))

    @pl.when(away)
    def _():
        pl.semaphore_signal(barrier, inc=1, device_id=there, device_id_type=MESH)

    pl.semaphore_wait(barrier, jnp.where(away, 14, 13))
    twin = me.plane(0, 0, 1)[0]
    x_next, px = me.plane(1, 0, 0)
    y_next, py = me.plane(0, 1, 0)
    pd = me.plane(1, 1, 0)[1]

    def slab(p):
        return pl.ds(pl.multiple_of(p * tokens, tokens), tokens)

    def quarter(grad, p, z):
        return grad.at[pl.ds(z * 8 + p - me.c, 2)]

    grads = {"d": (0, gd, od), "g": (1, gg, og), "u": (2, gu, ou)}
    begun, passed, late, kept = {}, {}, [], []
    hand_send = hand_recv = net.take(24)

    def first(n, z):
        g, grad, _ = grads[n]
        half = z // 2
        device, near, far = (y_next, py, px) if half else (x_next, px, py)
        at = pl.ds(z % 2 * 2, 2)
        begun[n, z] = [
            net.put(quarter(grad, near, z), came.at[g * 6 + half * 3, at], device).wait_recv,
            net.put(quarter(grad, pd, z), came.at[g * 6 + half * 3 + 1, at], device).wait_recv,
            net.keep(quarter(grad, me.p, z), own.at[g * 2 + half, at]).wait,
            net.keep(quarter(grad, far, z), side.at[g * 2 + half, at]).wait,
        ]

    def second(n, z):
        g, half, at = grads[n][0], z // 2, pl.ds(z % 2 * 2, 2)
        for wait in begun[n, z]:
            wait()
        mine = side.at[g * 2 + half, at]
        add_to(mine, came.at[g * 6 + half * 3 + 1, at])
        passed[n, z] = net.put(mine, came.at[g * 6 + half * 3 + 2, at], x_next if half else y_next)
        add_to(own.at[g * 2 + half, at], came.at[g * 6 + half * 3, at])

    def third(n, z):
        g, _, result = grads[n]
        half, at = z // 2, pl.ds(z % 2 * 2, 2)
        cols = pl.ds(pl.multiple_of(me.q * 1024, 1024), 1024)
        passed[n, z].wait_recv()
        add_to(own.at[g * 2 + half, at], came.at[g * 6 + half * 3 + 2, at])
        for c in (0, 1):
            src, dst = own.at[g * 2 + half, z % 2 * 2 + c], result.at[:, cols]
            mine = jnp.logical_and(me.z == z, me.c == c)
            k = hand_send + g * 8 + z * 2 + c
            copy = net.copy(src, dst, k, hand_recv + g * 8 + me.q, me.at(z, me.x, me.y, c))
            net.put_if(jnp.logical_not(mine), copy)
            here = pltpu.make_async_copy(src, dst, local.at[local.shape[0] - 2 - g])
            pl.when(mine)(here.start)
            late.append((mine, here))

    def norm():
        for copy in raw:
            copy.wait()

        def body(i, carry):
            def part(k):
                return E[pl.ds(pl.multiple_of(k * tokens + i * 16, 16), 16), :].astype(F32)

            v = part(0) + part(1)
            inverse = lax.rsqrt(jnp.mean(v * v, axis=-1, keepdims=True) + EPS)
            unit = v * inverse
            e = part(3) + part(4) + part(5) + part(6)
            d = part(2) + inverse * (e - unit * jnp.mean(e * unit, axis=-1, keepdims=True))
            DM[pl.ds(pl.multiple_of(i * 16, 16), 16), :] = d
            D[pl.ds(pl.multiple_of(me.p * tokens + i * 16, 16), 16), :] = d.astype(BF16)
            return carry

        lax.fori_loop(0, tokens // 16, body, 0)
        kept.append(net.keep(DM, d_mid))

    d_gather = PlaneGather(me, net, lambda p: D.at[slab(p)])
    loads = {}
    for name, src, dst in (
        ("att", att, A), ("wo", wo, Wo), ("r", r, R), ("pw", pw, P), ("t", t, T), ("u", u, U), ("wq", wq, Wq),
    ):
        loads[name] = [net.keep(src, dst)]
    loads["gain"] = [
        net.keep(gain_f.at[:, pl.ds(z * 512, 512)], gains.at[z, 1]) for z in range(DEPTH)
    ]

    def need(*names):
        for name in names:
            for copy in loads.pop(name, ()):
                copy.wait()

    out_in = []

    def out_swaps():
        for z in range(DEPTH):
            other, mine = slab(z * 2 + 1 - me.c), slab(z * 2 + me.c)
            out_in.append((net.put(part_o.at[other], out_swap.at[z], twin), net.keep(part_o.at[mine], out.at[z])))

    def out_add():
        for z in range(DEPTH):
            got, mine = out_in[z]
            got.wait_recv()
            mine.wait()
            add_to(out.at[z], out_swap.at[z])

    out_sum = ChainSum(me, net, out, out_up, out_down)

    def out_finish():
        out_sum.finish()
        kept.append(net.keep(out.at[me.z], out_o))

    block = 2 * tokens
    length = 4 * tokens
    lead = GROUP * HEAD_DIM
    scale = HEAD_DIM ** (-0.5)

    def d_attended():
        need("wo")

        def body(i, carry):
            rows = pl.ds(pl.multiple_of(i * block, block), block)
            dA[rows, :] = dot(D[rows, :], Wo[...].reshape(Wo.shape[0] * Wo.shape[1], Wo.shape[2]), NT).astype(BF16)
            return carry

        lax.fori_loop(0, 8 * tokens // block, body, 0)

    def turn_back(v, rows):
        cosine, sine = rotations(T[rows, :])
        return (v * cosine - turn(v) * sine).astype(BF16)

    def attend_back(seq):
        need("r", "pw", "t")
        keys_at = pl.ds(seq * length, length)
        keys = R[keys_at, lead : lead + HEAD_DIM]
        values = R[keys_at, lead + HEAD_DIM :]
        d_keys = jnp.zeros((length, HEAD_DIM), F32)
        d_values = jnp.zeros((length, HEAD_DIM), F32)
        for h in range(GROUP):
            cols = slice(h * HEAD_DIM, (h + 1) * HEAD_DIM)
            for part in range(2):
                rows = pl.ds(seq * length + part * (length // 2), length // 2)
                low = P[h, rows, :]
                weights = low.astype(F32)
                d_out = dA[rows, cols]
                d_weights = dot(d_out, values, NT)
                d_scores = (
                    weights * (d_weights - jnp.sum(weights * d_weights, axis=-1, keepdims=True))
                ).astype(BF16)
                dR[rows, cols] = turn_back(dot(d_scores, keys) * scale, rows)
                d_keys += dot(d_scores, R[rows, cols], TN)
                d_values += dot(low, d_out, TN)
        dR[keys_at, lead : lead + HEAD_DIM] = turn_back(d_keys * scale, keys_at)
        dR[keys_at, lead + HEAD_DIM :] = d_values.astype(BF16)

    tile = 512

    def e_product():
        need("u", "wq", "gain")

        def body(k, carry):
            i, j = lax.div(k, E.shape[1] // tile), lax.rem(k, E.shape[1] // tile)
            rows = pl.ds(pl.multiple_of(i * block, block), block)
            cols = pl.ds(pl.multiple_of(j * tile, tile), tile)
            slots = pl.ds(j * (tile // Wq.shape[1]), tile // Wq.shape[1])
            e = dot(dR[rows, :], Wq[slots].reshape(tile, Wq.shape[2]), NT)
            E[rows, cols] = e.astype(BF16)
            piece = jnp.sum((e * U[rows, cols].astype(F32)).reshape(block // 8, 8, tile), axis=0)
            gains[j, 0] = jnp.where(i == 0, 0.0, gains[j, 0]) + piece
            return carry

        lax.fori_loop(0, 8 * tokens // block * (E.shape[1] // tile), body, 0)

    e_sum = PlaneSum(me, net, lambda p: E.at[slab(p)], e_swap, e_came)
    span = 256

    def q_product():
        need("u")

        def body(k, carry):
            cols = pl.ds(pl.multiple_of(k * span, span), span)
            per = span // GQ.shape[2]
            g = dot(U[:, cols], dR[...], TN).astype(BF16)
            at = pl.ds(lax.rem(k, PLANE // per) * per, per)
            GQ[lax.div(k, PLANE // per), at] = g.reshape(per, GQ.shape[2], GQ.shape[3])
            return carry

        lax.fori_loop(0, U.shape[1] // span, body, 0)

    def o_product():
        need("att")

        def body(k, carry):
            cols = pl.ds(pl.multiple_of(k * tile, tile), tile)
            g = dot(A[...], D[:, cols], TN).astype(BF16)
            GO[:, 0, :, cols] = g.reshape(GO.shape[0], GO.shape[2], tile)
            return carry

        lax.fori_loop(0, D.shape[1] // tile, body, 0)

    def add_all(into, more):
        into[...] = into[...] + more[...]

    q_sum = ChainSum(me, net, GQ, q_up, q_down)
    o_sum = ChainSum(me, net, GO, o_up, o_down)
    v_sum = ChainSum(me, net, gains, v_up, v_down, add_all)

    def q_begin(hops):
        q_sum.begin(hops)
        v_sum.begin(hops)

    def q_near(hops):
        q_sum.near(hops)
        v_sum.near(hops)

    def q_far():
        q_sum.far()
        v_sum.far()

    def q_finish():
        q_sum.finish()
        v_sum.finish()

    k = net.take(1)
    swap = net.copy(GO.at[me.z, 0], oo, k, k, there)
    stay = pltpu.make_async_copy(GO.at[me.z, 0], oo, local.at[local.shape[0] - 1])
    stays = jnp.logical_not(away)
    owned = []

    def o_owners():
        pl.when(away)(swap.start)
        pl.when(stays)(stay.start)

    def q_owners():
        for dx in (0, 1):
            for dy in (0, 1):
                for dc in (0, 1):
                    device, p = me.plane(dx, dy, dc)
                    lanes = pl.ds(pl.multiple_of(lax.div(p, 2) * 128, 128), 128)
                    for src, dst in ((GQ.at[me.z, p], oq.at[me.p]), (gains.at[me.z, :, :, lanes], ov.at[me.p])):
                        if dx + dy + dc:
                            owned.append(net.put(src, dst, device))
                        else:
                            kept.append(net.keep(src, dst))

    def e_finish():
        kept.append(e_sum.finish(out_e))

    out_swaps()
    norm()
    d_gather.start()
    out_add()
    out_sum.begin(3)
    d_gather.relay_x()
    d_gather.relay_y()
    out_sum.near(2)
    first("g", 2)
    out_sum.begin(2)
    d_gather.finish()
    first("d", 0)
    first("u", 0)
    first("d", 1)
    d_attended()
    o_product()
    o_sum.begin(3)
    o_sum.begin(2)
    out_sum.near(1)
    first("d", 3)
    attend_back(0)
    out_sum.far()
    o_sum.near(2)
    attend_back(1)
    o_sum.near(1)
    first("g", 1)
    o_sum.begin(1)
    first("u", 3)
    e_product()
    o_sum.far()
    q_product()
    q_begin(3)
    o_sum.finish()
    o_owners()
    second("d", 0)
    q_begin(2)
    second("d", 3)
    second("u", 0)
    second("d", 1)
    q_near(2)
    first("d", 2)
    second("u", 3)
    third("u", 0)
    second("g", 1)
    first("u", 2)
    third("d", 3)
    second("g", 2)
    third("d", 1)
    third("g", 2)
    first("g", 3)
    out_sum.begin(1)
    third("u", 3)
    second("d", 2)
    q_near(1)
    q_far()
    q_begin(1)
    first("g", 0)
    second("u", 2)
    e_sum.start()
    third("d", 0)
    first("u", 1)
    third("g", 1)
    second("g", 0)
    second("g", 3)
    third("d", 2)
    e_sum.cores()
    q_finish()
    third("g", 3)
    third("g", 0)
    second("u", 1)
    third("u", 2)
    out_finish()
    third("u", 1)
    e_sum.chips()
    e_finish()
    q_owners()
    for n in "dgu":
        g, _, result = grads[n]
        for dz in range(DEPTH):
            for dc in (0, 1):
                if dz + dc:
                    _, z, c = me.column(dz, dc)
                    cols = pl.ds(pl.multiple_of((z * 2 + c) * 1024, 1024), 1024)
                    k = hand_recv + g * 8 + z * 2 + c
                    net.copy(own.at[g * 2, 0], result.at[:, cols], k, k, twin).wait_recv()
    for copy in owned:
        copy.wait_recv()
    for copy in kept:
        copy.wait()
    for mine, here in late:
        pl.when(mine)(here.wait)
    net.finish()
    pl.when(away)(swap.wait)
    pl.when(stays)(stay.wait)


def final_kernel(
    og, ou, od, oq, oo, o_sum, e_sum, d_mid, x, branch, gain,
    layer, input_grad, g_gate, g_up, g_down, g_qkv, g_out,
    v_og, v_ou, v_od, v_oq, v_oo, v_o, v_e, v_d, v_x, v_b, v_gain, f_gate, f_up, f_down, f_qkv, f_out, f_layer, f_input, sem,
):
    pairs = (
        (gain, v_gain), (og, v_og), (ou, v_ou), (od, v_od), (oq, v_oq), (oo, v_oo),
        (x, v_x), (branch, v_b), (o_sum, v_o), (e_sum, v_e), (d_mid, v_d),
    )
    loads = [pltpu.make_async_copy(src, dst, sem.at[i]) for i, (src, dst) in enumerate(pairs)]
    for load in loads:
        load.start()
    loads[0].wait()
    stores = []

    def store(src, dst):
        copy = pltpu.make_async_copy(src, dst, sem.at[len(pairs) + len(stores)])
        copy.start()
        stores.append(copy)

    def columns(src, dst, by):
        def body(i, carry):
            cols = pl.ds(pl.multiple_of(i * 1024, 1024), 1024)
            v = src[:, cols].astype(F32)
            dst[:, cols] = v if by is None else v * by
            return carry

        lax.fori_loop(0, src.shape[1] // 1024, body, 0)

    for i, (src, dst, out, by) in enumerate(
        ((v_og, f_gate, g_gate, gain), (v_ou, f_up, g_up, gain), (v_od, f_down, g_down, None))
    ):
        loads[1 + i].wait()
        columns(src, dst, None if by is None else column_of(v_gain[1:2, :])[: f_gate.shape[0]])
        store(dst, out)
    loads[4].wait()
    by = column_of(v_gain[0:1, :])[: f_qkv.shape[0]]
    for p in range(KV_HEADS):
        at = 0
        for first, size in head_columns(head_of(p)):
            f_qkv[:, first : first + size] = v_oq[p, :, at : at + size].astype(F32) * by
            at += size
    store(f_qkv, g_qkv)
    loads[5].wait()
    columns(v_oo, f_out, None)
    store(f_out, g_out)
    for load in loads[6:]:
        load.wait()

    def tokens_back(i, carry):
        at = pl.ds(pl.multiple_of(i * 16, 16), 16)
        v = v_x[at, :].astype(F32)
        f_layer[at, :] = (v + v_b[at, :].astype(F32) + v_o[at, :].astype(F32)).astype(BF16)
        inverse = lax.rsqrt(jnp.mean(v * v, axis=-1, keepdims=True) + EPS)
        unit = v * inverse
        e = v_e[at, :].astype(F32)
        f_input[at, :] = v_d[at, :] + inverse * (e - unit * jnp.mean(e * unit, axis=-1, keepdims=True))
        return carry

    lax.fori_loop(0, f_layer.shape[0] // 16, tokens_back, 0)
    store(f_layer, layer)
    store(f_input, input_grad)
    for copy in stores:
        copy.wait()


def shape(*dims, dtype=BF16):
    return jax.ShapeDtypeStruct(dims, dtype)


def shards(copies, block_input, positions, cotangent, norm_attn, w_qkv, w_out, norm_ffn, w_gate, w_up, w_down):
    tokens, width = block_input.shape
    ff = w_gate.shape[1]
    q_cols, kv_cols = HEADS * HEAD_DIM, KV_HEADS * HEAD_DIM
    spread = ("rep", "fsdp")
    place = lax.rem(lax.axis_index("rep"), PLANE) * 4 + lax.axis_index("fsdp")

    def take(w):
        if copies == 1:
            return w
        rows = w.shape[0] * copies
        whole = lax.all_gather(w, spread, axis=0, tiled=True)
        return lax.dynamic_slice_in_dim(whole, place * rows, rows, axis=0)

    def give(grad):
        if copies == 1:
            return grad
        rows = grad.shape[0]
        whole = jnp.zeros((rows * 32,) + grad.shape[1:], grad.dtype)
        whole = lax.dynamic_update_slice_in_dim(whole, grad, place * rows, axis=0)
        return lax.psum_scatter(whole, spread, scatter_dimension=0, tiled=True)

    gain_a = take(norm_attn).astype(F32)
    gain_f = take(norm_ffn).astype(F32)
    rows = gain_a.shape[0]
    gains = jnp.pad(jnp.stack([gain_a, gain_f]), ((0, 0), (0, 128 - rows)))
    own_qkv, own_gate, own_up = take(w_qkv), take(w_gate), take(w_up)
    own_down = take(w_down)
    own_out = take(w_out)
    head_cols = (GROUP + 2) * HEAD_DIM
    ff_cols = ff // 8
    full = 8 * tokens
    places = positions[None, :]
    sums, U, R, Pw, A, T, Wq, Wo, cg, Wg, Wu, Wd = call(
        front_kernel,
        0,
        [
            shape(tokens, width),
            shape(full, width),
            shape(full, head_cols),
            shape(GROUP, full, full // 2),
            shape(full, GROUP * HEAD_DIM),
            shape(full, HEAD_DIM, dtype=F32),
            shape(32, rows, head_cols),
            shape(4, rows, width),
            shape(8, tokens, width),
            shape(32, rows, ff_cols),
            shape(32, rows, ff_cols),
            shape(32, rows, ff_cols),
        ],
        (
            block_input,
            places,
            gains,
            cotangent,
            own_qkv,
            own_out,
            own_gate,
            own_up,
            own_down,
        ),
        150,
        36,
        [
            pltpu.VMEM((tokens, width), BF16),
            pltpu.VMEM((1, tokens), jnp.int32),
            pltpu.VMEM((2, 128), F32),
            pltpu.VMEM((8, tokens), F32),
            pltpu.VMEM((rows, q_cols + 2 * kv_cols), BF16),
            pltpu.VMEM((8, rows, head_cols), BF16),
            pltpu.VMEM((rows, ff), BF16),
            pltpu.VMEM((rows, ff), BF16),
            pltpu.VMEM((rows, ff), BF16),
            pltpu.VMEM((tokens, width), BF16),
            pltpu.VMEM((full, width), BF16),
            pltpu.VMEM((full, HEAD_DIM), F32),
            pltpu.VMEM((2, 8, full // 2), F32),
            pltpu.VMEM((32, rows, head_cols), BF16),
            pltpu.VMEM((4, rows, width), BF16),
            pltpu.VMEM((full, head_cols), BF16),
            pltpu.VMEM((GROUP, full, full // 2), BF16),
            pltpu.VMEM((full, GROUP * HEAD_DIM), BF16),
            pltpu.VMEM((full, width), BF16),
            pltpu.VMEM((4, tokens, width), BF16),
            pltpu.VMEM((6, tokens // 2, width), BF16),
        ],
    )
    cg = cg.reshape(full, width)
    Wg, Wu, Wd = [w.reshape(width, ff_cols) for w in (Wg, Wu, Wd)]

    e_sums, out_part, g_gate, g_up, g_down, gain_f_part = pl.pallas_call(
        ffn_kernel,
        out_shape=[
            shape(4, tokens, width),
            shape(full, width),
            shape(width, ff_cols),
            shape(width, ff_cols),
            shape(width, ff_cols),
            shape(8, width, dtype=F32),
        ],
        in_specs=[ANY] * 6,
        out_specs=[ANY] * 6,
        scratch_shapes=[pltpu.VMEM((2, tokens, width), BF16)]
        + [pltpu.VMEM((full, width), BF16)] * 2
        + [pltpu.VMEM((width, ff_cols), BF16)] * 3
        + [pltpu.VMEM((full, ff_cols), BF16)] * 3
        + [pltpu.VMEM((full, width), BF16)] * 2
        + [
            pltpu.VMEM((4, tokens, width), BF16),
            pltpu.VMEM((3, width, ff_cols), BF16),
            pltpu.VMEM((8, width), F32),
        ]
        + [pltpu.SemaphoreType.DMA((12,))] * 6
        + [pltpu.SemaphoreType.DMA((12 + 3 * width // 256,))],
        compiler_params=pltpu.CompilerParams(
            collective_id=2, has_side_effects=True, vmem_limit_bytes=60 * 1024 * 1024
        ),
    )(block_input, sums, cg, Wg, Wu, Wd)
    g_gate, g_up, g_down = [g.reshape(32, rows, ff_cols) for g in (g_gate, g_up, g_down)]
    d_mid, out_sums, ea_sums, og, ou, od, oq, oo, ov = call(
        back_kernel,
        3,
        [shape(tokens, width, dtype=F32)]
        + [shape(tokens, width)] * 2
        + [shape(rows, ff)] * 3
        + [
            shape(8, rows, head_cols),
            shape(rows, width),
            shape(8, 2, 8, 128, dtype=F32),
        ],
        (block_input, sums, cotangent, e_sums, out_part, g_gate, g_up, g_down, gain_f_part, U, R, Pw, A, T, Wq, Wo),
        140,
        90,
        [
            pltpu.VMEM((tokens, width), F32),
            pltpu.VMEM((full, width), BF16),
            pltpu.VMEM((full, width), BF16),
            pltpu.VMEM((full, head_cols), BF16),
            pltpu.VMEM((GROUP, full, full // 2), BF16),
            pltpu.VMEM((full, GROUP * HEAD_DIM), BF16),
            pltpu.VMEM((full, HEAD_DIM), F32),
            pltpu.VMEM((32, rows, head_cols), BF16),
            pltpu.VMEM((4, rows, width), BF16),
            pltpu.VMEM((full, GROUP * HEAD_DIM), BF16),
            pltpu.VMEM((full, head_cols), BF16),
            pltpu.VMEM((full, width), BF16),
            pltpu.VMEM((4, PLANE, rows, head_cols), BF16),
            pltpu.VMEM((4, 1, rows, width), BF16),
            pltpu.VMEM((4, 2, 8, width // 4), F32),
            pltpu.VMEM((4, tokens, width), BF16),
            pltpu.VMEM((4, tokens, width), BF16),
            pltpu.VMEM((3, tokens, width), BF16),
            pltpu.VMEM((3, tokens, width), BF16),
            pltpu.VMEM((4, tokens, width), BF16),
            pltpu.VMEM((6, tokens // 2, width), BF16),
            pltpu.VMEM((6, 4, rows, ff_cols), BF16),
            pltpu.VMEM((6, 4, rows, ff_cols), BF16),
            pltpu.VMEM((18, 4, rows, ff_cols), BF16),
        ]
        + [pltpu.VMEM((3, PLANE, rows, head_cols), BF16)] * 2
        + [pltpu.VMEM((3, 1, rows, width), BF16)] * 2
        + [pltpu.VMEM((3, 2, 8, width // 4), F32)] * 2,
    )
    layer_output, input_gradient, g_gate, g_up, g_down, g_qkv, g_out = pl.pallas_call(
        final_kernel,
        out_shape=[
            shape(tokens, width),
            shape(tokens, width, dtype=F32),
            shape(rows, ff, dtype=F32),
            shape(rows, ff, dtype=F32),
            shape(rows, ff, dtype=F32),
            shape(rows, q_cols + 2 * kv_cols, dtype=F32),
            shape(rows, width, dtype=F32),
        ],
        in_specs=[ANY] * 11,
        out_specs=[ANY] * 7,
        scratch_shapes=[pltpu.VMEM((rows, ff), BF16)] * 3
        + [pltpu.VMEM((8, rows, head_cols), BF16), pltpu.VMEM((rows, width), BF16)]
        + [pltpu.VMEM((tokens, width), BF16)] * 2
        + [pltpu.VMEM((tokens, width), F32)]
        + [pltpu.VMEM((tokens, width), BF16)] * 2
        + [pltpu.VMEM((2, 128), F32)]
        + [pltpu.VMEM((rows, ff), F32)] * 3
        + [
            pltpu.VMEM((rows, q_cols + 2 * kv_cols), F32),
            pltpu.VMEM((rows, width), F32),
            pltpu.VMEM((tokens, width), BF16),
            pltpu.VMEM((tokens, width), F32),
            pltpu.SemaphoreType.DMA((18,)),
        ],
        compiler_params=pltpu.CompilerParams(vmem_limit_bytes=60 * 1024 * 1024),
    )(og, ou, od, oq, oo, out_sums, ea_sums, d_mid, block_input, sums, gains)
    gain_sums = jnp.sum(ov, axis=(0, 2))
    gain_sums = lax.dynamic_slice_in_dim(gain_sums, place % 2 * rows, rows, axis=1)
    return (
        layer_output,
        input_gradient,
        give(gain_sums[0] / gain_a),
        give(g_qkv),
        give(g_out),
        give(gain_sums[1] / gain_f),
        give(g_gate),
        give(g_up),
        give(g_down),
    )


def solution(mesh):
    copies = mesh.shape["rep"] * mesh.shape["fsdp"] // 32
    rows, flat = P(("rep", "fsdp"), None), P(("rep", "fsdp"))
    return jax.shard_map(
        functools.partial(shards, copies),
        mesh=mesh,
        in_specs=(rows, flat, rows, flat, rows, rows, flat, rows, rows, rows),
        out_specs=(rows, rows, flat, rows, rows, flat, rows, rows, rows),
        check_vma=False,
    )
```

```python
import functools
import math

import jax
import jax.numpy as jnp
from jax import lax
from jax.experimental import pallas as pl
from jax.experimental.pallas import tpu as pltpu
from jax.sharding import PartitionSpec as P

HEADS = 16
KV_HEADS = 8
HEAD_DIM = 128
BLOCK = 256
MOST_BLOCKS = 2
GROUP = HEADS // KV_HEADS
EPS = 1e-05
THETA = 1000000.0
MESH = pl.DeviceIdType.MESH
F32 = jnp.float32
BF16 = jnp.bfloat16

PLANE = 8
DEPTH = 4
FLIPS = [(1, 0), (0, 1), (1, 1)]


def dot(a, b, dims=((1,), (0,))):
    return lax.dot_general(a, b, (dims, ((), ())), preferred_element_type=F32)


NT = ((1,), (1,))
TN = ((0,), (0,))


def flip(bit, by):
    return lax.rem(bit + by, 2)


class Place:
    def __init__(self):
        rep, self.f = lax.axis_index("rep"), lax.axis_index("fsdp")
        self.r = lax.rem(rep, PLANE)
        self.base = rep - self.r
        self.z, self.x = lax.div(self.r, 2), lax.rem(self.r, 2)
        self.y, self.c = lax.div(self.f, 2), lax.rem(self.f, 2)
        self.p = self.x * 4 + self.f
        self.q = self.z * 2 + self.c
        self.d = self.r * 4 + self.f

    def at(self, z, x, y, c):
        return (self.base + z * 2 + x, y * 2 + c)

    def plane(self, dx, dy, dc):
        x, y, c = flip(self.x, dx), flip(self.y, dy), flip(self.c, dc)
        return self.at(self.z, x, y, c), x * 4 + y * 2 + c

    def column(self, dz, dc):
        z, c = lax.rem(self.z + dz, DEPTH), flip(self.c, dc)
        return self.at(z, self.x, self.y, c), z, c

    def behind(self, dz):
        return lax.rem(self.z + (DEPTH - dz), DEPTH)


class Net:
    def __init__(self, send, recv, local):
        self.send, self.recv, self.local_sem = send, recv, local
        self.used = 0
        self.sent, self.kept = [], []

    def take(self, count):
        self.used += count
        return self.used - count

    def copy(self, src, dst, send, recv, device):
        return pltpu.make_async_remote_copy(
            src_ref=src,
            dst_ref=dst,
            send_sem=self.send.at[send],
            recv_sem=self.recv.at[recv],
            device_id=device,
            device_id_type=MESH,
        )

    def put(self, src, dst, device):
        k = self.take(1)
        copy = self.copy(src, dst, k, k, device)
        copy.start()
        self.sent.append((None, copy))
        return copy

    def put_if(self, when, copy):
        pl.when(when)(copy.start)
        self.sent.append((when, copy))
        return copy

    def keep(self, src, dst):
        copy = pltpu.make_async_copy(src, dst, self.local_sem.at[len(self.kept)])
        copy.start()
        self.kept.append(copy)
        return copy

    def finish(self):
        for when, copy in self.sent:
            if when is None:
                copy.wait_send()
            else:
                pl.when(when)(copy.wait_send)


class Chain:
    def __init__(self, me, net, slot, twins=None):
        self.me, self.net, self.slot, self.twins = me, net, slot, twins
        self.base = net.take(12)
        last = DEPTH - 1
        self.first, self.last = me.z == 0, me.z == last
        self.inner = jnp.logical_and(me.z > 0, me.z < last)
        self.order = [
            me.z,
            1 + lax.rem(me.z, 2),
            jnp.where(self.inner, last * (me.z - 1), 2 - lax.div(me.z, last)),
            last * (1 - lax.div(me.z, 2)),
        ]
        self.steps = [None] + [self.arrival(i) for i in range(1, DEPTH)]

    def pass_on(self, i):
        self.steps[i][0]()

    def take_in(self, i):
        self.steps[i][1]()

    def link(self, z, k, target):
        me = self.me
        ref = self.slot(z, me.c)
        return self.net.copy(ref, ref, self.base + k, self.base + z, me.at(target, me.x, me.y, me.c))

    def start(self):
        me, net = self.me, self.net
        net.put_if(jnp.logical_not(self.last), self.link(me.z, 0, me.z + 1))
        net.put_if(jnp.logical_not(self.first), self.link(me.z, 1, me.z - 1))
        if self.twins is not None:
            self.twin(me.z, 0)

    def twin(self, z, k):
        ref, net = self.slot(z, self.me.c), self.net
        copy = net.copy(ref, ref, self.base + 8 + k, self.base + 4 + z, self.twins)
        copy.start()
        net.sent.append((None, copy))

    def arrival(self, i):
        me, net = self.me, self.net
        z = self.order[i]
        onward = self.link(z, 1 + i, me.z + jnp.where(z < me.z, 1, -1))
        across = None
        net.sent.append((self.inner, onward))
        if self.twins is not None:
            ref = self.slot(z, me.c)
            across = net.copy(ref, ref, self.base + 8 + i, self.base + 4 + z, self.twins)
            net.sent.append((None, across))

        def take(passes):
            onward.wait_recv()
            if passes:
                onward.start()
            if across is not None:
                across.start()

        return (
            lambda: pl.when(self.inner)(lambda: take(True)),
            lambda: pl.when(jnp.logical_not(self.inner))(lambda: take(False)),
        )

    def twin_has(self, z):
        ref = self.slot(z, 1 - self.me.c)
        self.net.copy(ref, ref, self.base + 4, self.base + 4 + z, self.twins).wait_recv()

    def twin_all(self):
        for z in range(DEPTH):
            self.twin_has(z)


def greet(devices):
    barrier = pltpu.get_barrier_semaphore()
    for device in devices:
        pl.semaphore_signal(barrier, inc=1, device_id=device, device_id_type=MESH)
    return barrier


def plane_ids(me):
    return [
        me.plane(dx, dy, dc)[0] for dx in (0, 1) for dy in (0, 1) for dc in (0, 1) if dx + dy + dc
    ]


def column_ids(me):
    return [me.column(dz, dc)[0] for dz in range(1, DEPTH) for dc in (0, 1)]


def sems(sends, locals_):
    return [
        pltpu.SemaphoreType.DMA((sends,)),
        pltpu.SemaphoreType.DMA((sends,)),
        pltpu.SemaphoreType.DMA((locals_,)),
    ]


ANY = pl.BlockSpec(memory_space=pl.ANY)


def call(kernel, ident, outs, args, sends, locals_, scratch=()):
    return pl.pallas_call(
        kernel,
        out_shape=outs,
        in_specs=[ANY] * len(args),
        out_specs=[ANY] * len(outs),
        scratch_shapes=list(scratch) + sems(sends, locals_),
        compiler_params=pltpu.CompilerParams(
            collective_id=ident, has_side_effects=True, vmem_limit_bytes=60 * 1024 * 1024
        ),
    )(*args)


def head_of(p):
    return 2 * (p % 4) + p // 4


def head_columns(head):
    lead = GROUP * HEAD_DIM
    return (
        (head * lead, lead),
        (HEADS * HEAD_DIM + head * HEAD_DIM, HEAD_DIM),
        ((HEADS + KV_HEADS + head) * HEAD_DIM, HEAD_DIM),
    )


def column_of(row):
    return jnp.transpose(jnp.broadcast_to(row.astype(F32), (8, row.shape[1])))[:, 0:1]


def swap_owner(me):
    return me.at(me.f, me.x, lax.div(me.z, 2), lax.rem(me.z, 2)), me.f != me.z


def turn(v):
    return pltpu.roll(v, HEAD_DIM // 2, 1)


def rotations(table):
    swapped = turn(table)
    low = lax.broadcasted_iota(jnp.int32, table.shape, 1) < HEAD_DIM // 2
    return jnp.where(low, table, swapped), jnp.where(low, -swapped, table)


def attend(R, codes, P, A, seq, length):
    half = length // 2
    keys_at = pl.ds(seq * length, length)
    keys = R[keys_at, GROUP * HEAD_DIM : (GROUP + 1) * HEAD_DIM]
    values = R[keys_at, (GROUP + 1) * HEAD_DIM :]
    code = codes[seq, 0:1, :]
    for part in range(2):
        rows = pl.ds(seq * length + part * half, half)
        most = jnp.transpose(codes[seq, :, part * half : (part + 1) * half])[:, 0:1]
        least = jnp.floor(most * (1.0 / MOST_BLOCKS)) * MOST_BLOCKS
        allowed = (code <= most) & (code >= least)
        for h in range(GROUP):
            cols = slice(h * HEAD_DIM, (h + 1) * HEAD_DIM)
            scores = dot(R[rows, cols], keys, NT) * HEAD_DIM ** (-0.5)
            scores = jnp.where(allowed, scores, -1e30)
            exponent = jnp.exp(scores - jnp.max(scores, axis=-1, keepdims=True))
            weights = (exponent / jnp.sum(exponent, axis=-1, keepdims=True)).astype(BF16)
            P[h, rows, :] = weights
            A[rows, cols] = dot(weights, values).astype(BF16)


def front_kernel(
    x, pos, gain, cot, wq, wo, wg, wu, wd,
    sums, Uo, Ro, Po, Ao, To, Wqo, Woo, cg, Wg, Wu, Wd,
    X, places, gains, code, q_raw, q_own, g_own, u_own, d_own, c_own, U, T, codes, Wq, Wo, R, P, A, E, swapped, came, send, recv, local,
):
    me = Place()
    net = Net(send, recv, local)
    tokens = x.shape[0]
    there, away = swap_owner(me)
    barrier = greet(plane_ids(me) + column_ids(me))

    raw = [net.keep(src, dst) for src, dst in ((pos, places), (gain, gains), (wd, d_own), (x, X), (wq, q_raw), (wg, g_own), (wu, u_own), (cot, c_own))]

    @pl.when(away)
    def _():
        pl.semaphore_signal(barrier, inc=1, device_id=there, device_id_type=MESH)


    def enter():
        pl.semaphore_wait(barrier, jnp.where(away, 14, 13))

    twin = me.plane(0, 0, 1)[0]
    x_next, y_next = me.plane(1, 0, 0)[0], me.plane(0, 1, 0)[0]

    def slab(p):
        return pl.ds(pl.multiple_of(p * tokens, tokens), tokens)

    own_rows = slab(me.p)
    raw[1].wait()
    raw[2].wait()

    def normalize():
        raw[3].wait()

        def body(i, carry):
            at = pl.ds(pl.multiple_of(i * 16, 16), 16)
            v = X[at, :].astype(F32)
            v = v * lax.rsqrt(jnp.mean(v * v, axis=-1, keepdims=True) + EPS)
            U[pl.ds(pl.multiple_of(me.p * tokens + i * 16, 16), 16), :] = v.astype(BF16)
            return carry

        lax.fori_loop(0, tokens // 16, body, 0)

    def rotation_table():
        raw[0].wait()
        half = HEAD_DIM // 2
        place = jnp.broadcast_to(places[...], code.shape)
        column = jnp.transpose(place.astype(F32))[:, 0:1]
        index = lax.broadcasted_iota(jnp.int32, (1, half), 1).astype(F32)
        angles = column * jnp.exp(index * (-math.log(THETA) / half))
        T[own_rows, :] = jnp.concatenate([jnp.cos(angles), jnp.sin(angles)], axis=1)
        lane = lax.broadcasted_iota(jnp.int32, place.shape, 1)
        start = me.f * tokens + lane - place
        code[...] = (start * MOST_BLOCKS + lax.div(place, jnp.full_like(place, BLOCK))).astype(F32)

    def scale_q():
        raw[4].wait()
        by = column_of(gains[0:1, :])[: q_raw.shape[0]]
        for p in range(KV_HEADS):
            to = 0
            for first, size in head_columns(head_of(p)):
                q_own[p, :, to : to + size] = (q_raw[:, first : first + size].astype(F32) * by).astype(BF16)
                to += size

    def scale_f(k):
        raw[5 + k].wait()
        w = (g_own, u_own)[k]
        by = column_of(gains[1:2, :])[: w.shape[0]]

        def body(i, carry):
            cols = pl.ds(pl.multiple_of(i * 1024, 1024), 1024)
            w[:, cols] = (w[:, cols].astype(F32) * by).astype(BF16)
            return carry

        lax.fori_loop(0, w.shape[1] // 1024, body, 0)

    weights = {"g": (g_own, Wg), "u": (u_own, Wu), "d": (d_own, Wd)}
    taken, sent, last = {}, {}, []

    def column(n, dz):
        w, W = weights[n]
        taken[n, dz] = []
        for dc in (0, 1):
            device, z, c = me.column(dz, dc)
            cols = pl.ds(pl.multiple_of((z * 2 + c) * 1024, 1024), 1024)
            if dz + dc:
                taken[n, dz].append(net.put(w.at[:, cols], W.at[me.d], device).wait_recv)
            else:
                taken[n, dz].append(net.keep(w.at[:, cols], W.at[me.d]).wait)

    def spread(n, dz):
        W = weights[n][1]
        for wait in taken[n, dz]:
            wait()
        rows = pl.ds(me.behind(dz) * 8 + me.p - me.c, 2)
        sent[n, dz] = [net.put(W.at[rows], W.at[rows], device) for device in (x_next, y_next)]

    def relay(n, dz):
        W = weights[n][1]
        by_x, by_y = sent[n, dz]
        first = me.behind(dz) * 8 - me.c
        if dz % 2:
            by_x.wait_recv()
            rows = pl.ds(first + me.plane(1, 0, 0)[1], 2)
            last.extend((net.put(W.at[rows], W.at[rows], y_next), by_y))
        else:
            by_y.wait_recv()
            rows = pl.ds(first + me.plane(0, 1, 0)[1], 2)
            last.extend((net.put(W.at[rows], W.at[rows], x_next), by_x))

    q_in = []

    def q_go():
        for dx in (0, 1):
            for dy in (0, 1):
                for dc in (0, 1):
                    device, p = me.plane(dx, dy, dc)
                    if dx + dy + dc:
                        q_in.append(net.put(q_own.at[p], Wq.at[me.d], device))
                    else:
                        own = net.keep(q_own.at[p], Wq.at[me.d])
        q_in.append(own)

    q_chain = Chain(me, net, lambda z, c: Wq.at[pl.ds(z * PLANE, PLANE)])
    o_chain = Chain(me, net, lambda z, c: Wo.at[z])
    c_chain = Chain(me, net, lambda z, c: cg.at[z * 2 + c], twin)

    def q_start():
        for copy in q_in[:-1]:
            copy.wait_recv()
        q_in[-1].wait()
        q_chain.start()

    k = net.take(1)
    swap = net.copy(wo, Wo.at[me.f], k, k, there)
    stay = pltpu.make_async_copy(wo, Wo.at[me.f], local.at[local.shape[0] - 1])
    stays = jnp.logical_not(away)

    def swap_go():
        pl.when(away)(swap.start)
        pl.when(stays)(stay.start)

    def o_start():
        pl.when(away)(swap.wait)
        pl.when(stays)(stay.wait)
        o_chain.start()

    def c_start():
        raw[7].wait()
        net.keep(c_own, cg.at[me.q]).wait()
        c_chain.start()

    t_gather = PlaneGather(me, net, lambda p: T.at[slab(p)])
    x_gather = PlaneGather(me, net, lambda p: U.at[slab(p)])
    code_in = []

    def code_go():
        lanes = pl.ds(pl.multiple_of(lax.rem(me.p, 4) * tokens, tokens), tokens)
        at = codes.at[lax.div(me.p, 4), :, lanes]
        code_in.extend(net.put(code, at, device) for device in plane_ids(me))
        code_in.append(net.keep(code, at))

    block = 2 * tokens
    lead = GROUP * HEAD_DIM

    def project():
        def body(i, carry):
            rows = pl.ds(pl.multiple_of(i * block, block), block)
            q = dot(U[rows, :], Wq[...].reshape(Wq.shape[0] * Wq.shape[1], Wq.shape[2]))
            cosine, sine = rotations(T[rows, :])
            for h in range(GROUP + 1):
                v = q[:, h * HEAD_DIM : (h + 1) * HEAD_DIM]
                R[rows, h * HEAD_DIM : (h + 1) * HEAD_DIM] = (v * cosine + turn(v) * sine).astype(BF16)
            R[rows, lead + HEAD_DIM :] = q[:, lead + HEAD_DIM :].astype(BF16)
            return carry

        lax.fori_loop(0, 8 * tokens // block, body, 0)

    def attention(seq):
        if seq == 0:
            for copy in code_in[:-1]:
                copy.wait_recv()
            code_in[-1].wait()
        attend(R, codes, P, A, seq, 4 * tokens)

    total = PlaneSum(me, net, lambda p: E.at[slab(p)], swapped, came)
    stores = []

    def out_product():
        def body(i, carry):
            rows = pl.ds(pl.multiple_of(i * block, block), block)
            E[rows, :] = dot(A[rows, :], Wo[...].reshape(Wo.shape[0] * Wo.shape[1], Wo.shape[2])).astype(BF16)
            return carry

        lax.fori_loop(0, 8 * tokens // block, body, 0)
        for src, dst in ((U, Uo), (R, Ro), (P, Po), (A, Ao), (T, To), (Wq, Wqo), (Wo, Woo)):
            stores.append(net.keep(src, dst))

    scale_q()
    enter()
    column("d", 1)
    q_go()
    scale_f(1)
    column("u", 1)
    spread("d", 1)
    column("u", 0)
    q_start()
    spread("u", 0)
    rotation_table()
    t_gather.start()
    column("u", 3)
    code_go()
    normalize()
    scale_f(0)
    column("g", 0)
    x_gather.start()
    swap_go()
    column("g", 3)
    t_gather.relay_y()
    relay("u", 0)
    column("u", 2)
    spread("u", 1)
    x_gather.relay_x()
    q_chain.take_in(1)
    x_gather.relay_y()
    o_start()
    column("d", 0)
    spread("u", 3)
    t_gather.relay_x()
    q_chain.pass_on(1)
    spread("g", 0)
    q_chain.pass_on(2)
    t_gather.finish()
    spread("u", 2)
    spread("g", 3)
    o_chain.pass_on(1)
    relay("u", 3)
    q_chain.take_in(2)
    column("g", 2)
    spread("d", 0)
    relay("g", 0)
    relay("d", 1)
    o_chain.pass_on(2)
    relay("g", 3)
    q_chain.pass_on(3)
    x_gather.finish()
    relay("u", 1)
    column("g", 1)
    relay("d", 0)
    spread("g", 2)
    q_chain.take_in(3)
    o_chain.take_in(1)
    column("d", 3)
    o_chain.pass_on(3)
    o_chain.take_in(2)
    project()
    spread("g", 1)
    c_start()
    relay("u", 2)
    attention(0)
    spread("d", 3)
    attention(1)
    relay("g", 1)
    relay("g", 2)
    o_chain.take_in(3)
    out_product()
    total.start()
    c_chain.pass_on(1)
    c_chain.pass_on(2)
    column("d", 2)
    total.cores()
    total.chips()
    spread("d", 2)
    c_chain.take_in(1)
    c_chain.pass_on(3)
    relay("d", 3)
    c_chain.take_in(2)
    relay("d", 2)
    c_chain.take_in(3)
    stores.append(total.finish(sums))
    for copy in last:
        copy.wait_recv()
    c_chain.twin_all()
    for copy in stores:
        copy.wait()
    net.finish()


def add_to(into, more):
    step = 16
    rows = into.shape[-2]
    steps = rows // step

    def body(k, carry):
        if len(into.shape) == 2:
            at = (pl.ds(pl.multiple_of(k * step, step), step),)
        else:
            at = (lax.div(k, steps), pl.ds(pl.multiple_of(lax.rem(k, steps) * step, step), step))
        into[at] = (into[at].astype(F32) + more[at].astype(F32)).astype(BF16)
        return carry

    lax.fori_loop(0, steps * (1 if len(into.shape) == 2 else into.shape[0]), body, 0)


class PlaneGather:
    def __init__(self, me, net, slab):
        self.me, self.net, self.slab = me, net, slab
        self.twin = me.plane(0, 0, 1)[0]
        self.x_next, self.px = me.plane(1, 0, 0)
        self.y_next, self.py = me.plane(0, 1, 0)
        self.pd = me.plane(1, 1, 0)[1]

    def start(self):
        net, own = self.net, self.slab(self.me.p)
        self.by_x = net.put(own, own, self.x_next)
        self.by_y = net.put(own, own, self.y_next)
        self.late = [net.put(own, own, self.twin)]

    def half(self, p, k):
        ref = self.slab(p)
        rows = ref.shape[0] // 2
        return ref.at[pl.ds(k * rows, rows)]

    def across(self, p):
        ref = self.slab(p)
        self.late.append(self.net.put(ref, ref, self.twin))

    def relay_x(self):
        self.by_x.wait_recv()
        ref = self.half(self.px, 0)
        self.first = self.net.put(ref, ref, self.y_next)
        self.across(self.px)

    def relay_y(self):
        self.by_y.wait_recv()
        ref = self.half(self.py, 1)
        self.second = self.net.put(ref, ref, self.x_next)
        self.across(self.py)

    def finish(self):
        self.first.wait_recv()
        self.second.wait_recv()
        self.across(self.pd)
        for copy in self.late:
            copy.wait_recv()


class PlaneSum:
    def __init__(self, me, net, slab, swapped, came):
        self.me, self.net, self.slab, self.swapped, self.came = me, net, slab, swapped, came
        self.x_next, self.y_next = me.plane(1, 0, 0)[0], me.plane(0, 1, 0)[0]
        self.places = [me.plane(dx, dy, 0)[1] for dx, dy in FLIPS + [(0, 0)]]

    def start(self):
        me = self.me
        self.swaps = []
        for k, (dx, dy) in enumerate(FLIPS + [(0, 0)]):
            other = me.plane(dx, dy, 1)[1]
            self.swaps.append(
                self.net.put(self.slab(other), self.swapped.at[k], me.plane(0, 0, 1)[0])
            )

    def half(self, k, h):
        ref = self.slab(self.places[k])
        rows = ref.shape[0] // 2
        return ref.at[pl.ds(h * rows, rows)]

    def cores(self):
        for k in range(4):
            self.swaps[k].wait_recv()
            add_to(self.slab(self.places[k]), self.swapped.at[k])
            if k == 2:
                net, came = self.net, self.came
                self.first = [
                    net.put(self.half(2, 0), came.at[1], self.x_next),
                    net.put(self.half(2, 1), came.at[3], self.y_next),
                    net.put(self.half(0, 0), came.at[0], self.x_next),
                    net.put(self.half(1, 1), came.at[2], self.y_next),
                ]

    def chips(self):
        net, came = self.net, self.came
        for copy in self.first:
            copy.wait_recv()
        add_to(self.half(1, 0), came.at[1])
        second = [net.put(self.half(1, 0), came.at[4], self.y_next)]
        add_to(self.half(0, 1), came.at[3])
        second.append(net.put(self.half(0, 1), came.at[5], self.x_next))
        add_to(self.half(3, 0), came.at[0])
        add_to(self.half(3, 1), came.at[2])
        self.second = second

    def finish(self, out):
        for h in (0, 1):
            self.second[h].wait_recv()
            add_to(self.half(3, h), self.came.at[4 + h])
        return self.net.keep(self.slab(self.places[3]), out)


class ChainSum:
    def __init__(self, me, net, slots, up, down, add=add_to):
        self.me, self.net, self.slots, self.up, self.down, self.add = me, net, slots, up, down, add
        self.base = net.take(8)

    def copy(self, z, upward, target):
        me = self.me
        landing = self.up.at[z - 1] if upward else self.down.at[z]
        k = self.base + z + (0 if upward else 4)
        return self.net.copy(self.slots.at[z], landing, k, k, me.at(target, me.x, me.y, me.c))

    def step(self, at, z, upward):
        copy = self.copy(z, upward, at + 1 if upward else at - 1)
        here = self.me.z == at

        def go():
            if at != (0 if upward else DEPTH - 1):
                copy.wait_recv()
                self.add(self.slots.at[z], self.up.at[z - 1] if upward else self.down.at[z])
            copy.start()

        pl.when(here)(go)
        self.net.sent.append((here, copy))

    def begin(self, hops):
        self.step(0, hops, True)
        self.step(DEPTH - 1, DEPTH - 1 - hops, False)

    def near(self, hops):
        self.step(1, 1 + hops, True)
        self.step(2, 2 - hops, False)

    def far(self):
        self.step(2, 3, True)
        self.step(1, 0, False)

    def finish(self):
        me = self.me

        @pl.when(me.z > 0)
        def _():
            self.copy(me.z, True, me.z).wait_recv()
            self.add(self.slots.at[me.z], self.up.at[me.z - 1])

        @pl.when(me.z < DEPTH - 1)
        def _():
            self.copy(me.z, False, me.z).wait_recv()
            self.add(self.slots.at[me.z], self.down.at[me.z])


def ffn_kernel(
    x, branch, cot, wg, wu, wd, e_out, o_out, gg, gu, gd, gain, X, N, C, Wg, Wu, Wd, H, DG, DU, O, E, R, G, S, n_send, n_recv, x_send, x_recv, e_send, e_recv, local,
):
    me = Place()
    tokens = x.shape[0]
    chip = 2 * tokens
    twin = me.plane(0, 0, 1)[0]
    ids = [me.column(dz, 0)[0] for dz in range(1, DEPTH)] + [twin]
    barrier = greet(ids)
    own_rows = pl.ds(pl.multiple_of(me.q * tokens, tokens), tokens)
    mine = [pltpu.make_async_copy(src, X.at[i], local.at[(4, 11)[i]]) for i, src in enumerate((x, branch))]
    loads = [
        pltpu.make_async_copy(src, dst, local.at[i])
        for i, (src, dst) in enumerate(((wg, Wg), (wu, Wu), (wd, Wd), (cot, C)))
    ]
    for load in mine + loads:
        load.start()

    def rows_of(z, c):
        return pl.ds(pl.multiple_of((z * 2 + c) * tokens, tokens), tokens)

    def remote(src, dst, send, recv, device):
        return pltpu.make_async_remote_copy(
            src_ref=src,
            dst_ref=dst,
            send_sem=send,
            recv_sem=recv,
            device_id=device,
            device_id_type=MESH,
        )

    def column_id(z):
        return me.at(z, me.x, me.y, me.c)

    odd = lax.rem(me.z, 2)
    order = [me.z, 1 + odd, lax.rem(me.z + 2, DEPTH), 3 * (1 - odd)]
    net = Net(n_send, n_recv, local)
    chain = Chain(me, net, lambda z, c: N.at[rows_of(z, c)], twin)

    def twin_has(i):
        chain.twin_has(order[i])

    tile = 512

    def rows_at(i):
        return pl.ds(pl.multiple_of(order[i] * chip, chip), chip)

    def hidden(i):
        twin_has(i)
        rows = rows_at(i)

        def body(t, carry):
            cols = pl.ds(t * tile, tile)
            gate = dot(N[rows, :], Wg[:, cols])
            raised = dot(N[rows, :], Wu[:, cols])
            d_hidden = dot(C[rows, :], Wd[:, cols])
            sig = jax.nn.sigmoid(gate)
            act = gate * sig
            H[rows, cols] = (act * raised).astype(BF16)
            DU[rows, cols] = (d_hidden * act).astype(BF16)
            DG[rows, cols] = (d_hidden * raised * sig * (1.0 + gate * (1.0 - sig))).astype(BF16)
            return carry

        for t in range(H.shape[1] // tile):
            body(t, 0)

    def products(i):
        rows = rows_at(i)

        def body(t, carry):
            cols = pl.ds(t * tile, tile)
            e = dot(DG[rows, :], Wg[cols, :], NT) + dot(DU[rows, :], Wu[cols, :], NT)
            E[rows, cols] = e.astype(BF16)
            piece = jnp.sum((e * N[rows, cols].astype(F32)).reshape(chip // 8, 8, tile), axis=0)
            if i == 0:
                S[:, cols] = piece
            else:
                S[:, cols] += piece
            O[rows, cols] = dot(H[rows, :], Wd[cols, :], NT).astype(BF16)
            return carry

        for t in range(E.shape[1] // tile):
            body(t, 0)
        swap(i)

    swaps, sums = {}, {}

    def swap(i):
        o = order[i]
        copy = remote(E.at[rows_of(o, 1 - me.c)], R.at[i], x_send.at[i], x_recv.at[i], twin)
        copy.start()
        swaps[i] = copy

    def total(i):
        o = order[i]
        swaps[i].wait_recv()
        first = (o * 2 + me.c) * tokens

        def body(k, carry):
            at = pl.ds(pl.multiple_of(k * 16, 16), 16)
            to = pl.ds(pl.multiple_of(first + k * 16, 16), 16)
            E[to, :] = (E[to, :].astype(F32) + R[i, at, :].astype(F32)).astype(BF16)
            return carry

        lax.fori_loop(0, tokens // 16, body, 0)
        rows = rows_of(o, me.c)
        if i == 0:
            copy = pltpu.make_async_copy(E.at[rows], e_out.at[me.z], local.at[5])
        else:
            copy = remote(E.at[rows], e_out.at[me.z], e_send.at[i], e_recv.at[me.z], column_id(o))
        copy.start()
        sums[i] = copy

    for load in mine:
        load.wait()

    def normalize(i, carry):
        at = pl.ds(pl.multiple_of(i * 16, 16), 16)
        v = X[0, at, :].astype(F32) + X[1, at, :].astype(F32)
        v = v * lax.rsqrt(jnp.mean(v * v, axis=-1, keepdims=True) + EPS)
        N[pl.ds(pl.multiple_of(me.q * tokens + i * 16, 16), 16), :] = v.astype(BF16)
        return carry

    lax.fori_loop(0, tokens // 16, normalize, 0)
    pl.semaphore_wait(barrier, 4)
    span = 256
    stores = []

    def grad_tile(t):
        rows = pl.ds(t * span, span)
        n, c = N[:, rows], C[:, rows]
        for k, (left, right, out) in enumerate(((c, H, gd), (n, DG, gg), (n, DU, gu))):
            G[k, rows, :] = dot(left, right[...], TN).astype(BF16)
            store = pltpu.make_async_copy(G.at[k, rows], out.at[rows], local.at[12 + len(stores)])
            store.start()
            stores.append(store)

    chain.start()
    for load in loads:
        load.wait()
    hidden(0)
    products(0)
    chain.pass_on(1)
    chain.pass_on(2)
    chain.take_in(1)
    hidden(1)
    products(1)
    chain.take_in(2)
    chain.pass_on(3)
    total(1)
    chain.take_in(3)
    hidden(2)
    products(2)
    total(2)
    hidden(3)
    products(3)
    total(3)
    total(0)
    grad_tile(0)
    grad_tile(1)
    grad_tile(2)
    grad_tile(3)
    grad_tile(4)
    grad_tile(5)
    grad_tile(6)
    grad_tile(7)
    for src, dst, k in ((O, o_out, 6), (S, gain, 7)):
        store = pltpu.make_async_copy(src, dst, local.at[k])
        store.start()
        stores.append(store)
    for i in range(1, DEPTH):
        o = order[i]
        remote(E.at[own_rows], e_out.at[o], e_send.at[i], e_recv.at[o], twin).wait_recv()
    sums[0].wait()
    for i in range(DEPTH):
        swaps[i].wait_send()
        if i:
            sums[i].wait_send()
    net.finish()
    for store in stores:
        store.wait()


def back_kernel(
    x, branch, cot, e_parts, part_o, gg, gu, gd, gain_f, u, r, pw, att, t, wq, wo,
    d_mid, out_o, out_e, og, ou, od, oq, oo, ov,
    DM, D, U, R, P, A, T, Wq, Wo, dA, dR, E, GQ, GO, gains, out, out_swap, out_up, out_down, e_swap, e_came,
    own, side, came, q_up, q_down, o_up, o_down, v_up, v_down, send, recv, local,
):
    me = Place()
    net = Net(send, recv, local)
    tokens = x.shape[0]
    raw = [net.keep(src, E.at[pl.ds(k * tokens, tokens)]) for k, src in enumerate((x, branch, cot))]
    raw += [net.keep(e_parts.at[k], E.at[pl.ds((3 + k) * tokens, tokens)]) for k in range(DEPTH)]
    there, away = swap_owner(me)
    barrier = greet(plane_ids(me) + column_ids(me))

    @pl.when(away)
    def _():
        pl.semaphore_signal(barrier, inc=1, device_id=there, device_id_type=MESH)


    def enter():
        pl.semaphore_wait(barrier, jnp.where(away, 14, 13))

    twin = me.plane(0, 0, 1)[0]
    x_next, px = me.plane(1, 0, 0)
    y_next, py = me.plane(0, 1, 0)
    pd = me.plane(1, 1, 0)[1]

    def slab(p):
        return pl.ds(pl.multiple_of(p * tokens, tokens), tokens)

    def quarter(grad, p, z):
        return grad.at[pl.ds(z * 8 + p - me.c, 2)]

    grads = {"d": (0, gd, od), "g": (1, gg, og), "u": (2, gu, ou)}
    begun, passed, late, kept = {}, {}, [], []
    hand_send = hand_recv = net.take(24)

    def first(n, z):
        g, grad, _ = grads[n]
        half = z // 2
        device, near, far = (y_next, py, px) if half else (x_next, px, py)
        at = pl.ds(z % 2 * 2, 2)
        begun[n, z] = [
            net.put(quarter(grad, near, z), came.at[g * 6 + half * 3, at], device).wait_recv,
            net.put(quarter(grad, pd, z), came.at[g * 6 + half * 3 + 1, at], device).wait_recv,
            net.keep(quarter(grad, me.p, z), own.at[g * 2 + half, at]).wait,
            net.keep(quarter(grad, far, z), side.at[g * 2 + half, at]).wait,
        ]

    def second(n, z):
        g, half, at = grads[n][0], z // 2, pl.ds(z % 2 * 2, 2)
        for wait in begun[n, z]:
            wait()
        mine = side.at[g * 2 + half, at]
        add_to(mine, came.at[g * 6 + half * 3 + 1, at])
        passed[n, z] = net.put(mine, came.at[g * 6 + half * 3 + 2, at], x_next if half else y_next)
        add_to(own.at[g * 2 + half, at], came.at[g * 6 + half * 3, at])

    def third(n, z):
        g, _, result = grads[n]
        half, at = z // 2, pl.ds(z % 2 * 2, 2)
        cols = pl.ds(pl.multiple_of(me.q * 1024, 1024), 1024)
        passed[n, z].wait_recv()
        add_to(own.at[g * 2 + half, at], came.at[g * 6 + half * 3 + 2, at])
        for c in (0, 1):
            src, dst = own.at[g * 2 + half, z % 2 * 2 + c], result.at[:, cols]
            mine = jnp.logical_and(me.z == z, me.c == c)
            k = hand_send + g * 8 + z * 2 + c
            copy = net.copy(src, dst, k, hand_recv + g * 8 + me.q, me.at(z, me.x, me.y, c))
            net.put_if(jnp.logical_not(mine), copy)
            here = pltpu.make_async_copy(src, dst, local.at[local.shape[0] - 2 - g])
            pl.when(mine)(here.start)
            late.append((mine, here))

    def norm():
        for copy in raw:
            copy.wait()

        def body(i, carry):
            def part(k):
                return E[pl.ds(pl.multiple_of(k * tokens + i * 16, 16), 16), :].astype(F32)

            v = part(0) + part(1)
            inverse = lax.rsqrt(jnp.mean(v * v, axis=-1, keepdims=True) + EPS)
            unit = v * inverse
            e = part(3) + part(4) + part(5) + part(6)
            d = part(2) + inverse * (e - unit * jnp.mean(e * unit, axis=-1, keepdims=True))
            DM[pl.ds(pl.multiple_of(i * 16, 16), 16), :] = d
            D[pl.ds(pl.multiple_of(me.p * tokens + i * 16, 16), 16), :] = d.astype(BF16)
            return carry

        lax.fori_loop(0, tokens // 16, body, 0)
        kept.append(net.keep(DM, d_mid))

    d_gather = PlaneGather(me, net, lambda p: D.at[slab(p)])
    loads = {}
    for name, src, dst in (
        ("att", att, A), ("wo", wo, Wo), ("r", r, R), ("pw", pw, P), ("t", t, T), ("u", u, U), ("wq", wq, Wq),
    ):
        loads[name] = [net.keep(src, dst)]
    loads["gain"] = [
        net.keep(gain_f.at[:, pl.ds(z * 512, 512)], gains.at[z, 1]) for z in range(DEPTH)
    ]

    def need(*names):
        for name in names:
            for copy in loads.pop(name, ()):
                copy.wait()

    out_in = []

    def out_swaps():
        for z in range(DEPTH):
            other, mine = slab(z * 2 + 1 - me.c), slab(z * 2 + me.c)
            out_in.append((net.put(part_o.at[other], out_swap.at[z], twin), net.keep(part_o.at[mine], out.at[z])))

    def out_add():
        for z in range(DEPTH):
            got, mine = out_in[z]
            got.wait_recv()
            mine.wait()
            add_to(out.at[z], out_swap.at[z])

    out_sum = ChainSum(me, net, out, out_up, out_down)

    def out_finish():
        out_sum.finish()
        kept.append(net.keep(out.at[me.z], out_o))

    block = 2 * tokens
    length = 4 * tokens
    lead = GROUP * HEAD_DIM
    scale = HEAD_DIM ** (-0.5)

    def d_attended():
        need("wo")

        def body(i, carry):
            rows = pl.ds(pl.multiple_of(i * block, block), block)
            dA[rows, :] = dot(D[rows, :], Wo[...].reshape(Wo.shape[0] * Wo.shape[1], Wo.shape[2]), NT).astype(BF16)
            return carry

        lax.fori_loop(0, 8 * tokens // block, body, 0)

    def turn_back(v, rows):
        cosine, sine = rotations(T[rows, :])
        return (v * cosine - turn(v) * sine).astype(BF16)

    def attend_back(seq):
        need("r", "pw", "t")
        keys_at = pl.ds(seq * length, length)
        keys = R[keys_at, lead : lead + HEAD_DIM]
        values = R[keys_at, lead + HEAD_DIM :]
        d_keys = jnp.zeros((length, HEAD_DIM), F32)
        d_values = jnp.zeros((length, HEAD_DIM), F32)
        for h in range(GROUP):
            cols = slice(h * HEAD_DIM, (h + 1) * HEAD_DIM)
            for part in range(2):
                rows = pl.ds(seq * length + part * (length // 2), length // 2)
                low = P[h, rows, :]
                weights = low.astype(F32)
                d_out = dA[rows, cols]
                d_weights = dot(d_out, values, NT)
                d_scores = (
                    weights * (d_weights - jnp.sum(weights * d_weights, axis=-1, keepdims=True))
                ).astype(BF16)
                dR[rows, cols] = turn_back(dot(d_scores, keys) * scale, rows)
                d_keys += dot(d_scores, R[rows, cols], TN)
                d_values += dot(low, d_out, TN)
        dR[keys_at, lead : lead + HEAD_DIM] = turn_back(d_keys * scale, keys_at)
        dR[keys_at, lead + HEAD_DIM :] = d_values.astype(BF16)

    tile = 512

    def e_product():
        need("u", "wq", "gain")

        def body(k, carry):
            i, j = lax.div(k, E.shape[1] // tile), lax.rem(k, E.shape[1] // tile)
            rows = pl.ds(pl.multiple_of(i * block, block), block)
            cols = pl.ds(pl.multiple_of(j * tile, tile), tile)
            slots = pl.ds(j * (tile // Wq.shape[1]), tile // Wq.shape[1])
            e = dot(dR[rows, :], Wq[slots].reshape(tile, Wq.shape[2]), NT)
            E[rows, cols] = e.astype(BF16)
            piece = jnp.sum((e * U[rows, cols].astype(F32)).reshape(block // 8, 8, tile), axis=0)
            gains[j, 0] = jnp.where(i == 0, 0.0, gains[j, 0]) + piece
            return carry

        lax.fori_loop(0, 8 * tokens // block * (E.shape[1] // tile), body, 0)

    e_sum = PlaneSum(me, net, lambda p: E.at[slab(p)], e_swap, e_came)
    span = 256

    def q_product():
        need("u")

        def body(k, carry):
            cols = pl.ds(pl.multiple_of(k * span, span), span)
            per = span // GQ.shape[2]
            g = dot(U[:, cols], dR[...], TN).astype(BF16)
            at = pl.ds(lax.rem(k, PLANE // per) * per, per)
            GQ[lax.div(k, PLANE // per), at] = g.reshape(per, GQ.shape[2], GQ.shape[3])
            return carry

        lax.fori_loop(0, U.shape[1] // span, body, 0)

    def o_product():
        need("att")

        def body(k, carry):
            cols = pl.ds(pl.multiple_of(k * tile, tile), tile)
            g = dot(A[...], D[:, cols], TN).astype(BF16)
            GO[:, 0, :, cols] = g.reshape(GO.shape[0], GO.shape[2], tile)
            return carry

        lax.fori_loop(0, D.shape[1] // tile, body, 0)

    def add_all(into, more):
        into[...] = into[...] + more[...]

    q_sum = ChainSum(me, net, GQ, q_up, q_down)
    o_sum = ChainSum(me, net, GO, o_up, o_down)
    v_sum = ChainSum(me, net, gains, v_up, v_down, add_all)

    def q_begin(hops):
        q_sum.begin(hops)
        v_sum.begin(hops)

    def q_near(hops):
        q_sum.near(hops)
        v_sum.near(hops)

    def q_far():
        q_sum.far()
        v_sum.far()

    def q_finish():
        q_sum.finish()
        v_sum.finish()

    k = net.take(1)
    swap = net.copy(GO.at[me.z, 0], oo, k, k, there)
    stay = pltpu.make_async_copy(GO.at[me.z, 0], oo, local.at[local.shape[0] - 1])
    stays = jnp.logical_not(away)
    owned = []

    def o_owners():
        pl.when(away)(swap.start)
        pl.when(stays)(stay.start)

    def q_owners():
        for dx in (0, 1):
            for dy in (0, 1):
                for dc in (0, 1):
                    device, p = me.plane(dx, dy, dc)
                    lanes = pl.ds(pl.multiple_of(lax.div(p, 2) * 128, 128), 128)
                    for src, dst in ((GQ.at[me.z, p], oq.at[me.p]), (gains.at[me.z, :, :, lanes], ov.at[me.p])):
                        if dx + dy + dc:
                            owned.append(net.put(src, dst, device))
                        else:
                            kept.append(net.keep(src, dst))

    def e_finish():
        kept.append(e_sum.finish(out_e))

    norm()
    enter()
    d_gather.start()
    out_swaps()
    out_add()
    out_sum.begin(3)
    d_gather.relay_x()
    d_gather.relay_y()
    out_sum.near(2)
    first("g", 2)
    out_sum.begin(2)
    d_gather.finish()
    first("d", 0)
    first("u", 0)
    first("d", 1)
    d_attended()
    o_product()
    o_sum.begin(3)
    o_sum.begin(2)
    out_sum.near(1)
    first("d", 3)
    attend_back(0)
    out_sum.far()
    o_sum.near(2)
    attend_back(1)
    o_sum.near(1)
    first("g", 1)
    o_sum.begin(1)
    first("u", 3)
    e_product()
    o_sum.far()
    q_product()
    q_begin(3)
    o_sum.finish()
    o_owners()
    second("d", 0)
    q_begin(2)
    second("d", 3)
    second("u", 0)
    second("d", 1)
    q_near(2)
    first("d", 2)
    second("u", 3)
    third("u", 0)
    second("g", 1)
    first("u", 2)
    third("d", 3)
    second("g", 2)
    third("d", 1)
    third("g", 2)
    first("g", 3)
    out_sum.begin(1)
    third("u", 3)
    second("d", 2)
    q_near(1)
    q_far()
    q_begin(1)
    first("g", 0)
    second("u", 2)
    e_sum.start()
    third("d", 0)
    first("u", 1)
    third("g", 1)
    second("g", 0)
    second("g", 3)
    third("d", 2)
    e_sum.cores()
    q_finish()
    third("g", 3)
    third("g", 0)
    second("u", 1)
    third("u", 2)
    out_finish()
    third("u", 1)
    e_sum.chips()
    e_finish()
    q_owners()
    for n in "dgu":
        g, _, result = grads[n]
        for dz in range(DEPTH):
            for dc in (0, 1):
                if dz + dc:
                    _, z, c = me.column(dz, dc)
                    cols = pl.ds(pl.multiple_of((z * 2 + c) * 1024, 1024), 1024)
                    k = hand_recv + g * 8 + z * 2 + c
                    net.copy(own.at[g * 2, 0], result.at[:, cols], k, k, twin).wait_recv()
    for copy in owned:
        copy.wait_recv()
    for copy in kept:
        copy.wait()
    for mine, here in late:
        pl.when(mine)(here.wait)
    net.finish()
    pl.when(away)(swap.wait)
    pl.when(stays)(stay.wait)


def final_kernel(
    og, ou, od, oq, oo, o_sum, e_sum, d_mid, x, branch, gain,
    layer, input_grad, g_gate, g_up, g_down, g_qkv, g_out,
    v_og, v_ou, v_od, v_oq, v_oo, v_o, v_e, v_d, v_x, v_b, v_gain, f_gate, f_up, f_down, f_qkv, f_out, f_layer, f_input, sem,
):
    pairs = (
        (gain, v_gain), (og, v_og), (ou, v_ou), (od, v_od), (oq, v_oq), (oo, v_oo),
        (x, v_x), (branch, v_b), (o_sum, v_o), (e_sum, v_e), (d_mid, v_d),
    )
    loads = [pltpu.make_async_copy(src, dst, sem.at[i]) for i, (src, dst) in enumerate(pairs)]
    for load in loads:
        load.start()
    loads[0].wait()
    stores = []

    def store(src, dst):
        copy = pltpu.make_async_copy(src, dst, sem.at[len(pairs) + len(stores)])
        copy.start()
        stores.append(copy)

    def columns(src, dst, by):
        def body(i, carry):
            cols = pl.ds(pl.multiple_of(i * 1024, 1024), 1024)
            v = src[:, cols].astype(F32)
            dst[:, cols] = v if by is None else v * by
            return carry

        lax.fori_loop(0, src.shape[1] // 1024, body, 0)

    for i, (src, dst, out, by) in enumerate(
        ((v_og, f_gate, g_gate, gain), (v_ou, f_up, g_up, gain), (v_od, f_down, g_down, None))
    ):
        loads[1 + i].wait()
        columns(src, dst, None if by is None else column_of(v_gain[1:2, :])[: f_gate.shape[0]])
        store(dst, out)
    loads[4].wait()
    by = column_of(v_gain[0:1, :])[: f_qkv.shape[0]]
    for p in range(KV_HEADS):
        at = 0
        for first, size in head_columns(head_of(p)):
            f_qkv[:, first : first + size] = v_oq[p, :, at : at + size].astype(F32) * by
            at += size
    store(f_qkv, g_qkv)
    loads[5].wait()
    columns(v_oo, f_out, None)
    store(f_out, g_out)
    for load in loads[6:]:
        load.wait()

    def tokens_back(i, carry):
        at = pl.ds(pl.multiple_of(i * 16, 16), 16)
        v = v_x[at, :].astype(F32)
        f_layer[at, :] = (v + v_b[at, :].astype(F32) + v_o[at, :].astype(F32)).astype(BF16)
        inverse = lax.rsqrt(jnp.mean(v * v, axis=-1, keepdims=True) + EPS)
        unit = v * inverse
        e = v_e[at, :].astype(F32)
        f_input[at, :] = v_d[at, :] + inverse * (e - unit * jnp.mean(e * unit, axis=-1, keepdims=True))
        return carry

    lax.fori_loop(0, f_layer.shape[0] // 16, tokens_back, 0)
    store(f_layer, layer)
    store(f_input, input_grad)
    for copy in stores:
        copy.wait()


def shape(*dims, dtype=BF16):
    return jax.ShapeDtypeStruct(dims, dtype)


def shards(copies, block_input, positions, cotangent, norm_attn, w_qkv, w_out, norm_ffn, w_gate, w_up, w_down):
    tokens, width = block_input.shape
    ff = w_gate.shape[1]
    q_cols, kv_cols = HEADS * HEAD_DIM, KV_HEADS * HEAD_DIM
    spread = ("rep", "fsdp")
    place = lax.rem(lax.axis_index("rep"), PLANE) * 4 + lax.axis_index("fsdp")

    def take(w):
        if copies == 1:
            return w
        rows = w.shape[0] * copies
        whole = lax.all_gather(w, spread, axis=0, tiled=True)
        return lax.dynamic_slice_in_dim(whole, place * rows, rows, axis=0)

    def give(grad):
        if copies == 1:
            return grad
        rows = grad.shape[0]
        whole = jnp.zeros((rows * 32,) + grad.shape[1:], grad.dtype)
        whole = lax.dynamic_update_slice_in_dim(whole, grad, place * rows, axis=0)
        return lax.psum_scatter(whole, spread, scatter_dimension=0, tiled=True)

    gain_a = take(norm_attn).astype(F32)
    gain_f = take(norm_ffn).astype(F32)
    rows = gain_a.shape[0]
    gains = jnp.pad(jnp.stack([gain_a, gain_f]), ((0, 0), (0, 128 - rows)))
    own_qkv, own_gate, own_up = take(w_qkv), take(w_gate), take(w_up)
    own_down = take(w_down)
    own_out = take(w_out)
    head_cols = (GROUP + 2) * HEAD_DIM
    ff_cols = ff // 8
    full = 8 * tokens
    places = positions[None, :]
    sums, U, R, Pw, A, T, Wq, Wo, cg, Wg, Wu, Wd = call(
        front_kernel,
        0,
        [
            shape(tokens, width),
            shape(full, width),
            shape(full, head_cols),
            shape(GROUP, full, full // 2),
            shape(full, GROUP * HEAD_DIM),
            shape(full, HEAD_DIM, dtype=F32),
            shape(32, rows, head_cols),
            shape(4, rows, width),
            shape(8, tokens, width),
            shape(32, rows, ff_cols),
            shape(32, rows, ff_cols),
            shape(32, rows, ff_cols),
        ],
        (
            block_input,
            places,
            gains,
            cotangent,
            own_qkv,
            own_out,
            own_gate,
            own_up,
            own_down,
        ),
        150,
        36,
        [
            pltpu.VMEM((tokens, width), BF16),
            pltpu.VMEM((1, tokens), jnp.int32),
            pltpu.VMEM((2, 128), F32),
            pltpu.VMEM((8, tokens), F32),
            pltpu.VMEM((rows, q_cols + 2 * kv_cols), BF16),
            pltpu.VMEM((8, rows, head_cols), BF16),
            pltpu.VMEM((rows, ff), BF16),
            pltpu.VMEM((rows, ff), BF16),
            pltpu.VMEM((rows, ff), BF16),
            pltpu.VMEM((tokens, width), BF16),
            pltpu.VMEM((full, width), BF16),
            pltpu.VMEM((full, HEAD_DIM), F32),
            pltpu.VMEM((2, 8, full // 2), F32),
            pltpu.VMEM((32, rows, head_cols), BF16),
            pltpu.VMEM((4, rows, width), BF16),
            pltpu.VMEM((full, head_cols), BF16),
            pltpu.VMEM((GROUP, full, full // 2), BF16),
            pltpu.VMEM((full, GROUP * HEAD_DIM), BF16),
            pltpu.VMEM((full, width), BF16),
            pltpu.VMEM((4, tokens, width), BF16),
            pltpu.VMEM((6, tokens // 2, width), BF16),
        ],
    )
    cg = cg.reshape(full, width)
    Wg, Wu, Wd = [w.reshape(width, ff_cols) for w in (Wg, Wu, Wd)]

    e_sums, out_part, g_gate, g_up, g_down, gain_f_part = pl.pallas_call(
        ffn_kernel,
        out_shape=[
            shape(4, tokens, width),
            shape(full, width),
            shape(width, ff_cols),
            shape(width, ff_cols),
            shape(width, ff_cols),
            shape(8, width, dtype=F32),
        ],
        in_specs=[ANY] * 6,
        out_specs=[ANY] * 6,
        scratch_shapes=[pltpu.VMEM((2, tokens, width), BF16)]
        + [pltpu.VMEM((full, width), BF16)] * 2
        + [pltpu.VMEM((width, ff_cols), BF16)] * 3
        + [pltpu.VMEM((full, ff_cols), BF16)] * 3
        + [pltpu.VMEM((full, width), BF16)] * 2
        + [
            pltpu.VMEM((4, tokens, width), BF16),
            pltpu.VMEM((3, width, ff_cols), BF16),
            pltpu.VMEM((8, width), F32),
        ]
        + [pltpu.SemaphoreType.DMA((12,))] * 6
        + [pltpu.SemaphoreType.DMA((12 + 3 * width // 256,))],
        compiler_params=pltpu.CompilerParams(
            collective_id=2, has_side_effects=True, vmem_limit_bytes=60 * 1024 * 1024
        ),
    )(block_input, sums, cg, Wg, Wu, Wd)
    g_gate, g_up, g_down = [g.reshape(32, rows, ff_cols) for g in (g_gate, g_up, g_down)]
    d_mid, out_sums, ea_sums, og, ou, od, oq, oo, ov = call(
        back_kernel,
        3,
        [shape(tokens, width, dtype=F32)]
        + [shape(tokens, width)] * 2
        + [shape(rows, ff)] * 3
        + [
            shape(8, rows, head_cols),
            shape(rows, width),
            shape(8, 2, 8, 128, dtype=F32),
        ],
        (block_input, sums, cotangent, e_sums, out_part, g_gate, g_up, g_down, gain_f_part, U, R, Pw, A, T, Wq, Wo),
        140,
        90,
        [
            pltpu.VMEM((tokens, width), F32),
            pltpu.VMEM((full, width), BF16),
            pltpu.VMEM((full, width), BF16),
            pltpu.VMEM((full, head_cols), BF16),
            pltpu.VMEM((GROUP, full, full // 2), BF16),
            pltpu.VMEM((full, GROUP * HEAD_DIM), BF16),
            pltpu.VMEM((full, HEAD_DIM), F32),
            pltpu.VMEM((32, rows, head_cols), BF16),
            pltpu.VMEM((4, rows, width), BF16),
            pltpu.VMEM((full, GROUP * HEAD_DIM), BF16),
            pltpu.VMEM((full, head_cols), BF16),
            pltpu.VMEM((full, width), BF16),
            pltpu.VMEM((4, PLANE, rows, head_cols), BF16),
            pltpu.VMEM((4, 1, rows, width), BF16),
            pltpu.VMEM((4, 2, 8, width // 4), F32),
            pltpu.VMEM((4, tokens, width), BF16),
            pltpu.VMEM((4, tokens, width), BF16),
            pltpu.VMEM((3, tokens, width), BF16),
            pltpu.VMEM((3, tokens, width), BF16),
            pltpu.VMEM((4, tokens, width), BF16),
            pltpu.VMEM((6, tokens // 2, width), BF16),
            pltpu.VMEM((6, 4, rows, ff_cols), BF16),
            pltpu.VMEM((6, 4, rows, ff_cols), BF16),
            pltpu.VMEM((18, 4, rows, ff_cols), BF16),
        ]
        + [pltpu.VMEM((3, PLANE, rows, head_cols), BF16)] * 2
        + [pltpu.VMEM((3, 1, rows, width), BF16)] * 2
        + [pltpu.VMEM((3, 2, 8, width // 4), F32)] * 2,
    )
    layer_output, input_gradient, g_gate, g_up, g_down, g_qkv, g_out = pl.pallas_call(
        final_kernel,
        out_shape=[
            shape(tokens, width),
            shape(tokens, width, dtype=F32),
            shape(rows, ff, dtype=F32),
            shape(rows, ff, dtype=F32),
            shape(rows, ff, dtype=F32),
            shape(rows, q_cols + 2 * kv_cols, dtype=F32),
            shape(rows, width, dtype=F32),
        ],
        in_specs=[ANY] * 11,
        out_specs=[ANY] * 7,
        scratch_shapes=[pltpu.VMEM((rows, ff), BF16)] * 3
        + [pltpu.VMEM((8, rows, head_cols), BF16), pltpu.VMEM((rows, width), BF16)]
        + [pltpu.VMEM((tokens, width), BF16)] * 2
        + [pltpu.VMEM((tokens, width), F32)]
        + [pltpu.VMEM((tokens, width), BF16)] * 2
        + [pltpu.VMEM((2, 128), F32)]
        + [pltpu.VMEM((rows, ff), F32)] * 3
        + [
            pltpu.VMEM((rows, q_cols + 2 * kv_cols), F32),
            pltpu.VMEM((rows, width), F32),
            pltpu.VMEM((tokens, width), BF16),
            pltpu.VMEM((tokens, width), F32),
            pltpu.SemaphoreType.DMA((18,)),
        ],
        compiler_params=pltpu.CompilerParams(vmem_limit_bytes=60 * 1024 * 1024),
    )(og, ou, od, oq, oo, out_sums, ea_sums, d_mid, block_input, sums, gains)
    gain_sums = jnp.sum(ov, axis=(0, 2))
    gain_sums = lax.dynamic_slice_in_dim(gain_sums, place % 2 * rows, rows, axis=1)
    return (
        layer_output,
        input_gradient,
        give(gain_sums[0] / gain_a),
        give(g_qkv),
        give(g_out),
        give(gain_sums[1] / gain_f),
        give(g_gate),
        give(g_up),
        give(g_down),
    )


def solution(mesh):
    copies = mesh.shape["rep"] * mesh.shape["fsdp"] // 32
    rows, flat = P(("rep", "fsdp"), None), P(("rep", "fsdp"))
    return jax.shard_map(
        functools.partial(shards, copies),
        mesh=mesh,
        in_specs=(rows, flat, rows, flat, rows, rows, flat, rows, rows, rows),
        out_specs=(rows, rows, flat, rows, rows, flat, rows, rows, rows),
        check_vma=False,
    )
```
